32 devices in a mesh: freq: 2 (over y), tm: 16 (over z, x, core).
Axes of the slice: x: 2, y: 2, z: 4, core: 2. Of those that a mesh axis runs over, the one named last changes fastest.
Arguments:
- audio: bfloat16 [16, 2097152], P('tm', 'freq'), may hold values from -8 to 8
- w_start: float32 [32, 4096], P(None, 'freq'), may hold values from 0.05 to 0.5
- h_start: float32 [32, 4096], P(None, 'tm'), may hold values from 0.05 to 0.5
Outputs:
- components: float32 [32, 4096], P(None, 'freq')
- activations: float32 [32, 4096], P(None, 'tm')
The draws below stay inside these ranges and needn't reach their ends.
All inputs are finite; a program needn't handle non-finite values.
Results may differ from the reference program's by a relative error of at most 0.00053.
Values may be sent and summed in bfloat16 or wider, within the bound.
No kernel may reach another device: no remote copies, remote signals or barrier semaphores. Data moves between devices by JAX's collectives and lax.ppermute only.
A program may use at most 64 MiB of HBM per device.

```python
import math
import jax
import jax.numpy as jnp
from jax import lax

BINS = 4096
COMP = 32
FR_SUB = 128
ITERS = 2
FRAMES = 4096
N_FREQ = 2
N_TM = 16


def upsample(values, factor):
    spread = jnp.broadcast_to(values[..., None], values.shape + (factor,))
    return spread.reshape(values.shape[:-1] + (values.shape[-1] * factor,))


def log_uniform(key, shape_given, low_value, high_value):
    return jnp.exp(jax.random.uniform(key, shape_given, minval=math.log(low_value), maxval=math.log(high_value)))


def draw_audio(key, part):
    key = jax.random.fold_in(key, 7)
    row_count = N_TM
    frame_count = N_FREQ * FR_SUB
    frame_len = 2 * BINS
    tone_count = 16
    band_count = 8
    subkeys = jax.random.split(key, 15)
    full_shape = (row_count, frame_count, frame_len)
    position = jnp.arange(frame_len, dtype=jnp.int32)
    tone_bins = jax.random.randint(subkeys[0], (tone_count,), 4, BINS - 4)
    band_bins = jax.random.randint(subkeys[1], (band_count,), 16, BINS - 16)
    tone_base = log_uniform(subkeys[2], (tone_count,), 0.3, 3.0)
    band_base = log_uniform(subkeys[3], (band_count,), 0.05, 0.4)
    tone_phase = jax.random.uniform(subkeys[4], (row_count, frame_count, tone_count), minval=-math.pi, maxval=math.pi)
    tone_swing = jnp.exp(0.6 * jax.random.normal(subkeys[5], (row_count, frame_count, tone_count)))
    tone_onset = 0.15 + jax.random.bernoulli(subkeys[6], 0.6, (row_count, frame_count, tone_count)).astype(jnp.float32)
    band_swing = jnp.exp(0.6 * jax.random.normal(subkeys[7], (row_count, frame_count, band_count)))
    band_onset = 0.15 + jax.random.bernoulli(subkeys[8], 0.6, (row_count, frame_count, band_count)).astype(jnp.float32)
    frame_gain = log_uniform(subkeys[9], (row_count, frame_count, 1), 0.5, 2.0)
    coarse_noise = upsample(jax.random.normal(subkeys[10], (row_count, frame_count, frame_len // 16)), 16)
    slow_noise = upsample(jax.random.normal(subkeys[11], (row_count, frame_count, frame_len // 128)), 128)
    white_noise = jax.random.normal(subkeys[12], full_shape)
    signal = frame_gain * (0.25 * white_noise + 0.5 * coarse_noise + 0.25 * slow_noise)
    tone_scale = 8.0 / math.sqrt(frame_len)
    for source in range(tone_count):
        turns = (tone_bins[source] * position % frame_len).astype(jnp.float32)
        phase_angle = 2.0 * math.pi * turns / frame_len + tone_phase[:, :, source:source + 1]
        level = tone_scale * tone_base[source] * tone_swing[:, :, source:source + 1] * tone_onset[:, :, source:source + 1]
        signal = signal + level * jnp.cos(phase_angle)
    band_noise = jax.random.normal(subkeys[14], (band_count, row_count, frame_count, frame_len // 256))
    for source in range(band_count):
        envelope = upsample(band_noise[source], 256)
        turns = (band_bins[source] * position % frame_len).astype(jnp.float32)
        phase_angle = 2.0 * math.pi * turns / frame_len
        level = band_base[source] * band_swing[:, :, source:source + 1] * band_onset[:, :, source:source + 1]
        signal = signal + level * envelope * jnp.cos(phase_angle)
    signal = jnp.clip(signal, -8.0, 8.0)
    return signal.reshape(row_count, frame_count * frame_len).astype(jnp.bfloat16)


def block_levels(stream_key, extent, cuts, least, largest):
    loudness, own = 1.0, jax.random.fold_in(stream_key, 6)
    for dim, shards_of in cuts:
        steps = jnp.exp(jax.random.uniform(jax.random.fold_in(own, dim), (shards_of,), jnp.float32, least / len(cuts), largest / len(cuts)))
        loudness = loudness * jnp.repeat(steps, extent[dim] // shards_of).reshape([-1 if axis == dim else 1 for axis in range(len(extent))])
    return loudness


def setup_inputs(seed: int = 0) -> dict:
    keys = jax.random.split(jax.random.key(seed), 4)
    return {
        "audio": draw_audio(jax.random.fold_in(keys[3], 71), 0),
        "w_start": jnp.clip(jnp.exp(math.log(0.5) - 2.3025851 * jax.random.uniform(keys[1], (COMP, BINS), jnp.float32) ** block_levels(keys[1], (COMP, BINS), ((1, 2),), -0.2, 0.2)), 0.05, 0.5),
        "h_start": jnp.clip(jnp.exp(math.log(0.5) - 2.3025851 * jax.random.uniform(keys[2], (COMP, FRAMES), jnp.float32) ** block_levels(keys[2], (COMP, FRAMES), ((1, 16),), -0.2, 0.2)), 0.05, 0.5),
    }


def reference(audio, w_start, h_start):
    frame_len = 2 * BINS
    signal = audio.reshape(-1, FR_SUB, frame_len)
    position = jnp.arange(frame_len).astype(jnp.float32)
    window = 0.5 - 0.5 * jnp.cos(2.0 * math.pi * position / frame_len)
    factor = 1.0 / math.sqrt(0.375 * frame_len)

    def one_block(block):
        windowed = block.astype(jnp.float32) * window
        transform = jnp.fft.rfft(windowed, axis=-1)[:, :BINS]
        real_part = jnp.real(transform)
        imag_part = jnp.imag(transform)
        return (jnp.sqrt(real_part * real_part + imag_part * imag_part) * factor).astype(jnp.bfloat16)
    magnitude = lax.map(one_block, signal).reshape(-1, BINS)
    highest = lax.Precision.HIGHEST
    components = w_start
    activations = h_start
    for step in range(ITERS):
        numer_h = jnp.dot(components.astype(jnp.bfloat16), magnitude.T, preferred_element_type=jnp.float32)
        gram_w = jnp.dot(components, components.T, precision=highest)
        activations = activations * numer_h / jnp.dot(gram_w, activations, precision=highest)
        numer_w = jnp.dot(activations.astype(jnp.bfloat16), magnitude, preferred_element_type=jnp.float32)
        gram_h = jnp.dot(activations, activations.T, precision=highest)
        components = components * numer_w / jnp.dot(gram_h, components, precision=highest)
    return (components, activations)
```

```python
import functools
import math

import jax
import jax.numpy as jnp
import numpy as np
from jax import lax
from jax.experimental import pallas as pl
from jax.experimental.pallas import tpu as pltpu
from jax.sharding import PartitionSpec as P

ITERS = 2
HIGHEST = lax.Precision.HIGHEST
ALL = ("freq", "tm")
LANES = 128
OUTER = 64
HALF = OUTER // 2
FRAME = OUTER * LANES
CHUNK = 16
PAIR = 2
GROUP = 4
NT = (((1,), (1,)), ((), ()))
LEAST = 2.0**-126


def tables():
    a = np.arange(OUTER)
    i = np.arange(LANES)
    r = np.arange(HALF)
    position = a[:, None] * LANES + i[None, :]
    window = 0.5 - 0.5 * np.cos(2 * np.pi * position / FRAME)
    window = window / math.sqrt(0.375 * FRAME)
    angle = 2 * np.pi * (r[:, None] * a[None, :] % OUTER) / OUTER
    first = np.stack([np.cos(angle), -np.sin(angle)], axis=1).reshape(2 * HALF, OUTER)
    first[1] = np.cos(np.pi * a)
    turn = 2 * np.pi * r[:, None] * i[None, :] / FRAME
    turn_cos = np.cos(turn)
    turn_sin = np.sin(turn)
    m = np.arange(OUTER)
    column = np.concatenate([m, LANES - 1 - m])
    angle = 2 * np.pi * (i[:, None] * column[None, :] % LANES) / LANES
    top = np.concatenate([np.cos(angle), -np.sin(angle)], axis=1)
    bottom = np.concatenate([np.sin(angle), np.cos(angle)], axis=1)
    second = np.concatenate([top, bottom], axis=0)
    zero = np.zeros((LANES, OUTER))
    angle_a = 2 * np.pi * i[:, None] * (m * OUTER)[None, :] / FRAME
    angle_b = 2 * np.pi * i[:, None] * (m * OUTER + HALF)[None, :] / FRAME
    top = np.concatenate([np.cos(angle_a), zero, -np.sin(angle_a), zero], axis=1)
    bottom = np.concatenate([zero, np.cos(angle_b), zero, -np.sin(angle_b)], axis=1)
    edge = np.concatenate([top, bottom], axis=0)

    first = np.concatenate([first, np.zeros((OUTER, LANES - OUTER))], axis=1)
    second, edge = (np.concatenate([t[:, :LANES], t[:, LANES:]], axis=0) for t in (second, edge))
    parts = [window, first, turn_cos, turn_sin, second, edge]
    return np.concatenate(parts, axis=0).astype(np.float32)


def halves(value):
    high = value.astype(jnp.bfloat16)
    return high, (value - high.astype(jnp.float32)).astype(jnp.bfloat16)


def spectrum_kernel(core, audio, source, keep, give, peak, heard, table, stack, held, audio_sems, table_sems):
    frames = keep.shape[1]
    chunks = frames // CHUNK
    turns = 2 * OUTER

    def audio_copy(chunk):
        span = pl.ds(pl.multiple_of(chunk * CHUNK * FRAME, CHUNK * FRAME), CHUNK * FRAME)
        return pltpu.make_async_copy(audio.at[:, span], heard.at[chunk], audio_sems.at[chunk])

    def table_copy(k):
        span = pl.ds(0, turns) if k == 0 else pl.ds(turns, table.shape[0] - turns)
        return pltpu.make_async_copy(source.at[span], table.at[span], table_sems.at[k])

    table_copy(0).start()
    for chunk in range(chunks):
        audio_copy(chunk).start()
    table_copy(1).start()
    table_copy(0).wait()
    high, low = halves(table[OUTER:turns, :OUTER])
    first_terms = jnp.concatenate([high, low, high], axis=1)

    @pl.loop(0, chunks)
    def _(chunk):
        audio_copy(chunk).wait()
        samples = heard[chunk].reshape(CHUNK * OUTER, LANES).astype(jnp.float32)
        shape = table[:OUTER]
        for start in range(0, CHUNK, PAIR):
            columns = []
            for frame in range(start, start + PAIR):
                high, low = halves(samples[frame * OUTER : (frame + 1) * OUTER] * shape)
                columns.append(jnp.concatenate([high, high, low], axis=0))
            sums = jnp.dot(
                first_terms, jnp.concatenate(columns, axis=1), preferred_element_type=jnp.float32
            )
            for frame in range(start, start + PAIR):
                place = pl.ds(chunk * CHUNK + frame, OUTER, stride=frames + 1)
                held[place, :] = sums[:, (frame - start) * LANES : (frame - start + 1) * LANES]

    table_copy(1).wait()
    for k in range(2):
        at = turns + 2 * HALF + k * 4 * LANES
        both = jnp.concatenate([table[at : at + 2 * LANES], table[at + 2 * LANES : at + 4 * LANES]], axis=1)
        high, low = halves(both)
        stack[k] = jnp.concatenate([high, low, high], axis=0)

    def turned(row):
        at = row * 2 * (frames + 1)
        real = held[pl.ds(at, frames), :]
        imag = held[pl.ds(at + frames + 1, frames), :]
        cos, sin = table[pl.ds(turns + row, 1), :], table[pl.ds(turns + HALF + row, 1), :]
        high_r, low_r = halves(real * cos + imag * sin)
        high_i, low_i = halves(imag * cos - real * sin)
        return jnp.concatenate([high_r, high_i, high_r, high_i, low_r, low_i], axis=1)

    def magnitude(terms, k):
        bins = jnp.dot(terms, stack[k], preferred_element_type=jnp.float32)
        real, imag = bins[:, :LANES], bins[:, LANES:]
        square = real * real + imag * imag
        found = (square * lax.rsqrt(jnp.maximum(square, LEAST))).astype(keep.dtype)
        peak[...] = jnp.maximum(peak[...], jnp.max(found.reshape(-1, 16, LANES), axis=0))
        return found

    peak[...] = jnp.zeros_like(peak)

    def rows_of(side, out):
        for group in range(HALF // 2 // GROUP):
            start = side * (HALF // 2) + group * GROUP
            found = magnitude(jnp.concatenate([turned(start + k) for k in range(GROUP)], axis=0), 0)
            for k in range(GROUP):
                out[group * GROUP + k] = found[k * frames : (k + 1) * frames]

    rows_of(1 - core[0], give)
    rows_of(core[0], keep)
    edge = magnitude(turned(0), 1)

    @pl.when(core[0] == 0)
    def _():
        keep[0] = edge

    @pl.when(core[0] != 0)
    def _():
        give[0] = edge


def spectrum(audio, core):
    frames = audio.shape[1] // FRAME
    table = jnp.asarray(tables())
    far = pl.BlockSpec(memory_space=pltpu.HBM)
    return pl.pallas_call(
        spectrum_kernel,
        out_shape=[jax.ShapeDtypeStruct((HALF // 2, frames, LANES), jnp.bfloat16)] * 2
        + [jax.ShapeDtypeStruct((16, LANES), jnp.bfloat16)],
        in_specs=[pl.BlockSpec(memory_space=pltpu.SMEM), far, far],
        out_specs=[pl.BlockSpec(memory_space=pltpu.VMEM)] * 3,
        scratch_shapes=[
            pltpu.VMEM((frames // CHUNK, 1, CHUNK * FRAME), jnp.bfloat16),
            pltpu.VMEM(table.shape, table.dtype),
            pltpu.VMEM((2, 6 * LANES, 2 * LANES), jnp.bfloat16),
            pltpu.VMEM((OUTER * (frames + 1), LANES), jnp.float32),
            pltpu.SemaphoreType.DMA((frames // CHUNK,)),
            pltpu.SemaphoreType.DMA((2,)),
        ],
        compiler_params=pltpu.CompilerParams(vmem_limit_bytes=105 * 2**19),
        cost_estimate=pl.CostEstimate(
            flops=6 * frames * FRAME * (OUTER + 2 * LANES), bytes_accessed=2**22, transcendentals=0
        ),
        name="spectrum",
    )(core, audio, table)


def update(state, numer, gram):
    return state * numer / jnp.dot(gram, state, precision=HIGHEST, preferred_element_type=jnp.float32)


def step_kernel(comps, grid, acts, parts, acts_out):
    rows, comp, lanes = comps.shape
    wide = jnp.concatenate([comps[r] for r in range(rows)], axis=1)
    tall = jnp.concatenate([grid[r] for r in range(rows)], axis=1)
    numer = lax.dot_general(wide.astype(jnp.bfloat16), tall, NT, preferred_element_type=jnp.float32)
    gram = lax.dot_general(wide, wide, NT, precision=HIGHEST, preferred_element_type=jnp.float32)
    acts_new = update(acts[...], numer, gram)
    acts_out[...] = acts_new
    gram = lax.dot_general(acts_new, acts_new, NT, precision=HIGHEST, preferred_element_type=jnp.float32)
    per = LANES // comp
    high = comp // per
    packed = jnp.concatenate([gram[j * high : (j + 1) * high] for j in range(per)], axis=1)
    sums = jnp.dot(acts_new.astype(jnp.bfloat16), tall, preferred_element_type=jnp.float32)
    for r in range(rows):
        parts[r, :comp, :] = sums[:, r * lanes : (r + 1) * lanes]
        parts[r, comp:, :] = packed


def advance(comps, grid, acts):
    rows, comp, lanes = comps.shape
    extra = comp * comp // LANES
    return pl.pallas_call(
        step_kernel,
        out_shape=(
            jax.ShapeDtypeStruct((rows, comp + extra, lanes), jnp.float32),
            jax.ShapeDtypeStruct(acts.shape, jnp.float32),
        ),
        compiler_params=pltpu.CompilerParams(vmem_limit_bytes=32 * 2**20),
        name="advance",
    )(comps, grid, acts)


def unpack(packed):
    high = packed.shape[0]
    comp = math.isqrt(packed.size)
    return packed.reshape(high, LANES // comp, comp).transpose(1, 0, 2).reshape(comp, comp)


def inner_order(natural):
    comp = natural.shape[0]
    cube = natural.reshape(comp, -1, OUTER).transpose(2, 0, 1)
    mirrored = jnp.concatenate([cube[HALF : HALF + 1], cube[: HALF : -1]], axis=0)
    return jnp.concatenate([cube[:HALF], mirrored], axis=2)


def natural_order(inner):
    comp, width = inner.shape[1], inner.shape[2] // 2
    low, mirrored = inner[:, :, :width], inner[:, :, width:]
    cube = jnp.concatenate([low, mirrored[:1], mirrored[:0:-1]], axis=0)
    return cube.transpose(1, 2, 0).reshape(comp, -1)


def gather_freq(block, n_freq, at):
    pieces = [block]
    for shift in range(1, n_freq):
        ring = [(i, (i + shift) % n_freq) for i in range(n_freq)]
        pieces.append(lax.ppermute(block, "freq", ring))
    placed = []
    for p in range(n_freq):
        value = pieces[0]
        for shift in range(1, n_freq):
            value = jnp.where((at - shift) % n_freq == p, pieces[shift], value)
        placed.append(value)
    return jnp.concatenate(placed, axis=1)


TOP = 13
SIDE = HALF // 2


def pack(gram):
    comp = gram.shape[0]
    per = LANES // comp
    high = comp // per
    return jnp.concatenate([gram[j * high : (j + 1) * high] for j in range(per)], axis=1)


def unpacked(packed):
    comp = math.isqrt(packed.size)
    return jnp.concatenate([packed[:, j * comp : (j + 1) * comp] for j in range(LANES // comp)], axis=0)


def exponent(value):
    peak = jnp.max(jnp.abs(value), axis=(0, 1), keepdims=True)
    return jnp.floor(jnp.log2(jnp.maximum(peak, 1e-30))) - TOP


def power(exps):
    count = jnp.abs(exps).astype(jnp.int32)
    value = jnp.ones_like(exps)
    for bit in range(7):
        step = jnp.where(exps < 0, 2.0 ** -(2**bit), 2.0 ** (2**bit))
        value = value * jnp.where((count >> bit) & 1 == 1, step, 1.0)
    return value


def places(shape):
    return [lax.broadcasted_iota(jnp.int32, shape, axis) for axis in range(2)]


def mirrored_at(r):
    return OUTER - r if r else HALF


def gram_of(value):
    rows = value.shape[0]
    both = jnp.concatenate(halves(value), axis=0)
    parts = lax.dot_general(both, both, NT, preferred_element_type=jnp.float32)
    cross = parts[:rows, rows:] + parts[rows:, :rows]
    return parts[:rows, :rows] + (cross + parts[rows:, rows:])


def start_kernel(at, own, other, keep, give, acts, acts_out, mine, held):
    comp = own.shape[0]
    row, side, first = at[0], at[1], at[2] == 0
    wide = jnp.concatenate(
        [jnp.where(first, own[...], other[...]), jnp.where(first, other[...], own[...])], axis=1
    )
    quads, eighth = LANES // comp, 8
    for q in range(eighth):
        columns = [wide[:, (c * eighth + q) * LANES : (c * eighth + q + 1) * LANES] for c in range(quads)]
        turned = jnp.concatenate(columns, axis=0).T
        for m in range(2):
            place = (2 * q + m) * (OUTER + 1)
            held[place : place + OUTER, :] = turned[m * OUTER : (m + 1) * OUTER]
    gram = gram_of(wide)
    span = OUTER // quads
    block = places((span, LANES))[1] // comp

    def pair(r):
        mirror = jnp.where(r == 0, HALF, OUTER - r)
        return [held[pl.ds(j, span, stride=OUTER + 1), :] for j in (r, mirror)]

    both = jnp.concatenate(pair(row), axis=0).T
    mine[...] = jnp.concatenate(
        [
            both[c * comp : (c + 1) * comp, h * span : (h + 1) * span]
            for h in range(2)
            for c in range(quads)
        ],
        axis=1,
    )
    total = jnp.zeros((acts.shape[1], LANES), jnp.float32)
    batch = 8
    for grid, start in ((keep, side * SIDE), (give, (1 - side) * SIDE)):
        for base in range(0, SIDE, batch):
            pieces = []
            for u in range(base, base + batch):
                for value in pair(start + u):
                    pieces += [jnp.where(block == c, value, 0.0).astype(jnp.bfloat16) for c in range(quads)]
            left = jnp.concatenate([grid[u] for u in range(base, base + batch)], axis=1)
            total += jnp.dot(left, jnp.concatenate(pieces, axis=0), preferred_element_type=jnp.float32)
    total = total.T
    numer = sum(total[c * comp : (c + 1) * comp] for c in range(quads))
    acts_out[...] = update(acts[...], numer, gram)


def sealed(sums, gram, squares, bound=None):
    comp = gram.shape[0]
    sums_exp, gram_exp = exponent(sums if bound is None else bound), exponent(squares)
    packed = pack(gram) * power(-gram_exp)
    rows, lanes = places(packed.shape)
    last, end = packed.shape[0] - 1, LANES - comp
    packed = jnp.where((rows == last) & (lanes == end), sums_exp, packed)
    packed = jnp.where((rows == last) & (lanes == end + 1), gram_exp, packed)
    return sums * power(-sums_exp), packed


def opened(got, comp):
    end = LANES - comp
    scales = power(got[:, got.shape[1] - 1, :])
    sources = range(got.shape[0])
    gram = sum(got[s, comp:, :] * scales[s : s + 1, end + 1 : end + 2] for s in sources)
    gram = unpacked(gram)
    at = places(gram.shape)
    for column in range(2):
        mirrored = gram[column : column + 1, comp - 1 : comp]
        gram = jnp.where((at[0] == comp - 1) & (at[1] == column), mirrored, gram)
    return [scales[s : s + 1, end : end + 1] for s in sources], gram


def tall(grid):
    return jnp.concatenate([grid[u] for u in range(SIDE)], axis=1)


def finish(acts, grids, parts, peak=None):
    comp = acts[0].shape[0]
    sums, gram, weight, squares = 0.0, 0.0, 0.0, 0.0
    for value, grid in zip(acts, grids):
        left = value.astype(jnp.bfloat16)
        weight += jnp.sum(left.astype(jnp.float32), axis=1, keepdims=True)
        squares += jnp.sum(value * value, axis=1, keepdims=True)
        sums += jnp.dot(left, tall(grid), preferred_element_type=jnp.float32)
        gram += lax.dot_general(value, value, NT, precision=HIGHEST, preferred_element_type=jnp.float32)
    sums, packed = sealed(sums, gram, squares, None if peak is None else weight * (1.01 * peak))
    for u in range(SIDE):
        parts[u, :comp, :] = sums[:, u * LANES : (u + 1) * LANES]
        parts[u, comp:, :] = packed


def sums_kernel(acts, sibling, keep, taken, parts):
    finish((acts[...], sibling[...]), (keep, taken), parts)


def partial_kernel(got, keep, taken, peak, out):
    comp = out.shape[0] - got.shape[1]
    scales, gram = opened(got, comp)
    wide = [(got[u, :comp, :] * scales[u]).astype(jnp.bfloat16) for u in range(SIDE)]
    wide = jnp.concatenate(wide, axis=1)
    for k, grid in enumerate((keep, taken)):
        out[k * comp : (k + 1) * comp, :] = lax.dot_general(
            wide, tall(grid), NT, preferred_element_type=jnp.float32
        )
    packed = pack(gram)
    rows, lanes = places(packed.shape)
    highest = jnp.max(peak[...].astype(jnp.float32), axis=(0, 1), keepdims=True)
    place = (rows == packed.shape[0] - 1) & (lanes == LANES - comp)
    out[2 * comp :, :] = jnp.where(place, highest, packed)


def again_kernel(half, other_half, acts, sibling, keep, taken, parts, acts_out):
    comp = acts.shape[0]
    mine, theirs = half[2 * comp :, :], other_half[2 * comp :, :]
    last, end = mine.shape[0] - 1, LANES - comp
    peak = jnp.maximum(mine, theirs)[last : last + 1, end : end + 1]
    gram = unpacked(mine + theirs)
    at = places(gram.shape)
    gram = jnp.where((at[0] == comp - 1) & (at[1] == 0), gram[:1, comp - 1 : comp], gram)
    new = update(acts[...], half[:comp, :] + other_half[comp : 2 * comp, :], gram)
    sibling_new = update(sibling[...], half[comp : 2 * comp, :] + other_half[:comp, :], gram)
    acts_out[...] = new
    finish((new, sibling_new), (keep, taken), parts, peak)


def slice_kernel(got, mine, out, payload):
    comp = mine.shape[0]
    scales, gram = opened(got, comp)
    sums = sum(got[s, :comp, :] * scales[s] for s in range(got.shape[0]))
    new = update(mine[...], sums, gram)
    out[...] = new
    gram = lax.dot_general(new, new, NT, precision=HIGHEST, preferred_element_type=jnp.float32)
    squares = jnp.sum(new * new, axis=1, keepdims=True)
    sums, packed = sealed(new.astype(jnp.bfloat16).astype(jnp.float32), gram, squares)
    payload[:comp, :] = sums
    payload[comp:, :] = packed


def last_kernel(got, mine, out, exps_out):
    comp = mine.shape[0]
    scales, gram = opened(got, comp)
    sums = sum(got[s, :comp, :] * scales[s] for s in range(got.shape[0]))
    new = update(mine[...], sums, gram)
    at = places(gram.shape)
    diagonal = jnp.sum(jnp.where(at[0] == at[1], gram, 0.0), axis=1, keepdims=True)
    bound = sum(scales) * 2.0 ** (TOP + 1) / jnp.maximum(diagonal, 1e-30)
    exps = jnp.clip(jnp.floor(jnp.log2(jnp.maximum(bound, 1e-30))), -100, 100) - TOP
    exps_out[...] = jnp.broadcast_to(exps, exps_out.shape)
    turned = (new * power(-exps)).T
    span = OUTER // 4
    for freq in range(2):
        starts = [h * OUTER + freq * 2 * span + half * span for h in range(2) for half in range(2)]
        out[freq] = jnp.concatenate([turned[a : a + span] for a in starts], axis=1)


def natural_kernel(at, got, exps, acts, partner, out, acts_out, low, high):
    comp = out.shape[0]
    span = OUTER // 4
    for r in range(HALF):
        value = got[r % SIDE * 2 + r // SIDE]
        low[pl.ds(r, span, stride=HALF + 1), :] = value
        high[pl.ds(mirrored_at(r) % HALF, span, stride=HALF + 1), :] = pltpu.roll(value, LANES // 2, 1)
    factor = power(exps[...])
    for pair in range(span // 2):
        rows = []
        for place in (2 * pair, 2 * pair + 1):
            begin = place * (HALF + 1)
            rows += [ref[begin : begin + HALF, :] for ref in (low, high)]
        turned = jnp.concatenate(rows, axis=0).T
        for half in range(2):
            begin = (half * (span // 2) + pair) * LANES
            out[:, begin : begin + LANES] = turned[half * comp : (half + 1) * comp] * factor
    first, own, other = at[2] == 0, acts[...], partner[...]
    acts_out[...] = jnp.concatenate([jnp.where(first, own, other), jnp.where(first, other, own)], axis=1)


def local(kernel, outs, name, *arrays, scratch=(), cost=None):
    vmem = pl.BlockSpec(memory_space=pltpu.VMEM)
    smem = pl.BlockSpec(memory_space=pltpu.SMEM)
    many = isinstance(outs, list)
    shapes = [jax.ShapeDtypeStruct(shape, dtype) for shape, dtype in (outs if many else [outs])]
    return pl.pallas_call(
        kernel,
        out_shape=shapes if many else shapes[0],
        in_specs=[smem if a.dtype == jnp.int32 else vmem for a in arrays],
        out_specs=[vmem] * len(outs) if many else vmem,
        scratch_shapes=list(scratch),
        compiler_params=pltpu.CompilerParams(vmem_limit_bytes=32 * 2**20),
        cost_estimate=cost,
        name=name,
    )(*arrays)


def row_shards(audio, w_start, h_start):
    f16, f32 = jnp.float16, jnp.float32
    comp = w_start.shape[0]
    swap = [(0, 1), (1, 0)]
    freq_at, core_at = lax.axis_index("freq"), lax.axis_index("core")
    q = freq_at * lax.axis_size("chips") + lax.axis_index("chips")
    at = jnp.stack([core_at * SIDE + q, core_at, freq_at]).astype(jnp.int32)
    other = lax.ppermute(w_start, "freq", swap)
    keep, give, peak = spectrum(audio, at[1:2])
    frames = keep.shape[1]
    extra = comp * comp // LANES
    taken = lax.ppermute(give, "core", swap)
    acts = lax.dynamic_slice_in_dim(h_start, freq_at * frames, frames, 1)
    message = ((SIDE, comp + extra, LANES), f32)
    lane_rows = ((comp, LANES), f32)

    def exchange(value, axes=("freq", "chips")):
        value = lax.all_to_all(value.astype(f16), axes, split_axis=0, concat_axis=0, tiled=True)
        return value.astype(f32)

    acts, mine = local(
        start_kernel,
        [(acts.shape, f32), lane_rows],
        "start",
        at,
        w_start,
        other,
        keep,
        give,
        acts,
        scratch=[pltpu.VMEM((LANES // 8 * (OUTER + 1), LANES), f32)],
        cost=pl.CostEstimate(flops=2**34, bytes_accessed=2**25, transcendentals=0),
    )
    sibling = lax.ppermute(acts, "core", swap)
    parts = local(sums_kernel, message, "sums", acts, sibling, keep, taken)
    for step in range(ITERS - 1):
        got = exchange(parts)
        outs = [lane_rows, ((comp + extra, LANES), f32)]
        mine, payload = local(slice_kernel, outs, "slice", got, mine)
        got = exchange(jnp.broadcast_to(payload, (SIDE,) + payload.shape))
        half = local(partial_kernel, ((2 * comp + extra, LANES), f32), "partial", got, keep, taken, peak)
        other_half = lax.ppermute(half, "core", swap)
        outs = [message, (acts.shape, f32)]
        parts, acts = local(
            again_kernel, outs, "again", half, other_half, acts, sibling, keep, taken
        )
    got = exchange(parts)
    acts, got = lax.optimization_barrier((acts, got))
    partner = lax.ppermute(acts, "freq", swap)
    final, exps = local(last_kernel, [((2, OUTER // 4, LANES), f32), lane_rows], "last", got, mine)
    final = jnp.broadcast_to(final[:, None], (2, HALF // 2) + final.shape[1:])
    got = exchange(final.reshape((HALF,) + final.shape[2:]), ("freq", "chips", "core"))
    return local(
        natural_kernel,
        [(w_start.shape, f32), (h_start.shape, f32)],
        "natural",
        at,
        got,
        exps,
        acts,
        partner,
        scratch=[pltpu.VMEM((OUTER // 4 * (HALF + 1), LANES), f32)] * 2,
    )


def shards(n_freq, n_tm, audio, w_start, h_start):
    n_dev = n_freq * n_tm
    comp, w_cols = w_start.shape
    bins = w_cols * n_freq
    own = bins // n_dev
    width = OUTER // n_freq
    freq_at = lax.axis_index("freq")
    me = freq_at * n_tm + lax.axis_index("tm")
    grid = jnp.concatenate(spectrum(audio, jnp.zeros((1,), jnp.int32))[:2], axis=0)
    frames = grid.shape[1]
    comps = inner_order(gather_freq(w_start, n_freq, freq_at))
    acts = lax.dynamic_slice_in_dim(h_start, freq_at * frames, frames, 1)
    per_row = LANES // own
    mine = lax.dynamic_slice(
        comps, (me // per_row, 0, me % per_row * own), (1, comp, own)
    ).reshape(comp, own)
    for step in range(ITERS):
        parts, acts = advance(comps, grid, acts)
        sums = parts[:, :comp].reshape(HALF, comp, per_row, own).transpose(0, 2, 1, 3)
        gram = jnp.broadcast_to(parts[0, comp:].reshape(1, -1), (n_dev, comp * comp))
        parts = jnp.concatenate([sums.reshape(n_dev, -1), gram], axis=1).reshape(n_dev, -1, LANES)
        got = lax.all_to_all(parts, ALL, split_axis=0, concat_axis=0, tiled=True)
        value = jnp.sum(got, axis=0)
        rows = comp * own // LANES
        mine = update(mine, value[:rows].reshape(comp, own), unpack(value[rows:]))
        every = jnp.broadcast_to(mine.reshape(1, -1, LANES), (n_dev, rows, LANES))
        comps = lax.all_to_all(every, ALL, split_axis=0, concat_axis=0, tiled=True)
        comps = comps.reshape(HALF, per_row, comp, own).transpose(0, 2, 1, 3)
        comps = comps.reshape(HALF, comp, LANES)
    cut = lax.dynamic_slice_in_dim(comps.reshape(HALF, comp, 2, OUTER), freq_at * width, width, 3)
    components = natural_order(cut.reshape(HALF, comp, 2 * width))
    activations = gather_freq(acts, n_freq, freq_at)
    return (components, activations)


def solution(mesh):
    sizes = (mesh.shape["freq"], mesh.shape["tm"])
    if sizes == (2, SIDE):
        devices = mesh.devices.reshape(2, SIDE // 2, 2)
        mesh = jax.sharding.Mesh(devices, ("freq", "chips", "core"))
        body, tm = row_shards, ("chips", "core")
    else:
        body, tm = functools.partial(shards, *sizes), "tm"
    return jax.shard_map(
        body,
        mesh=mesh,
        in_specs=(P(tm, "freq"), P(None, "freq"), P(None, tm)),
        out_specs=(P(None, "freq"), P(None, tm)),
        check_vma=False,
    )
```

```python
import functools
import math

import jax
import jax.numpy as jnp
import numpy as np
from jax import lax
from jax.experimental import pallas as pl
from jax.experimental.pallas import tpu as pltpu
from jax.sharding import PartitionSpec as P

ITERS = 2
HIGHEST = lax.Precision.HIGHEST
ALL = ("freq", "tm")
LANES = 128
OUTER = 64
HALF = OUTER // 2
FRAME = OUTER * LANES
CHUNK = 16
PAIR = 2
GROUP = 4
NT = (((1,), (1,)), ((), ()))
LEAST = 2.0**-126


def tables():
    a = np.arange(OUTER)
    i = np.arange(LANES)
    r = np.arange(HALF)
    position = a[:, None] * LANES + i[None, :]
    window = 0.5 - 0.5 * np.cos(2 * np.pi * position / FRAME)
    window = window / math.sqrt(0.375 * FRAME)
    angle = 2 * np.pi * (r[:, None] * a[None, :] % OUTER) / OUTER
    first = np.stack([np.cos(angle), -np.sin(angle)], axis=1).reshape(2 * HALF, OUTER)
    first[1] = np.cos(np.pi * a)
    turn = 2 * np.pi * r[:, None] * i[None, :] / FRAME
    turn_cos = np.cos(turn)
    turn_sin = np.sin(turn)
    m = np.arange(OUTER)
    column = np.concatenate([m, LANES - 1 - m])
    angle = 2 * np.pi * (i[:, None] * column[None, :] % LANES) / LANES
    top = np.concatenate([np.cos(angle), -np.sin(angle)], axis=1)
    bottom = np.concatenate([np.sin(angle), np.cos(angle)], axis=1)
    second = np.concatenate([top, bottom], axis=0)
    zero = np.zeros((LANES, OUTER))
    angle_a = 2 * np.pi * i[:, None] * (m * OUTER)[None, :] / FRAME
    angle_b = 2 * np.pi * i[:, None] * (m * OUTER + HALF)[None, :] / FRAME
    top = np.concatenate([np.cos(angle_a), zero, -np.sin(angle_a), zero], axis=1)
    bottom = np.concatenate([zero, np.cos(angle_b), zero, -np.sin(angle_b)], axis=1)
    edge = np.concatenate([top, bottom], axis=0)

    first = np.concatenate([first, np.zeros((OUTER, LANES - OUTER))], axis=1)
    second, edge = (np.concatenate([t[:, :LANES], t[:, LANES:]], axis=0) for t in (second, edge))
    parts = [window, first, turn_cos, turn_sin, second, edge]
    return np.concatenate(parts, axis=0).astype(np.float32)


def halves(value):
    high = value.astype(jnp.bfloat16)
    return high, (value - high.astype(jnp.float32)).astype(jnp.bfloat16)


def spectrum_kernel(core, audio, source, keep, give, peak, heard, table, stack, held, audio_sems, table_sems):
    frames = keep.shape[1]
    chunks = frames // CHUNK
    turns = 2 * OUTER

    def audio_copy(chunk):
        span = pl.ds(pl.multiple_of(chunk * CHUNK * FRAME, CHUNK * FRAME), CHUNK * FRAME)
        return pltpu.make_async_copy(audio.at[:, span], heard.at[chunk], audio_sems.at[chunk])

    def table_copy(k):
        span = pl.ds(0, turns) if k == 0 else pl.ds(turns, table.shape[0] - turns)
        return pltpu.make_async_copy(source.at[span], table.at[span], table_sems.at[k])

    table_copy(0).start()
    for chunk in range(chunks):
        audio_copy(chunk).start()
    table_copy(1).start()
    table_copy(0).wait()
    high, low = halves(table[OUTER:turns, :OUTER])
    first_terms = jnp.concatenate([high, low, high], axis=1)

    @pl.loop(0, chunks)
    def _(chunk):
        audio_copy(chunk).wait()
        samples = heard[chunk].reshape(CHUNK * OUTER, LANES).astype(jnp.float32)
        shape = table[:OUTER]
        for start in range(0, CHUNK, PAIR):
            columns = []
            for frame in range(start, start + PAIR):
                high, low = halves(samples[frame * OUTER : (frame + 1) * OUTER] * shape)
                columns.append(jnp.concatenate([high, high, low], axis=0))
            sums = jnp.dot(
                first_terms, jnp.concatenate(columns, axis=1), preferred_element_type=jnp.float32
            )
            for frame in range(start, start + PAIR):
                place = pl.ds(chunk * CHUNK + frame, OUTER, stride=frames + 1)
                held[place, :] = sums[:, (frame - start) * LANES : (frame - start + 1) * LANES]

    table_copy(1).wait()
    for k in range(2):
        at = turns + 2 * HALF + k * 4 * LANES
        both = jnp.concatenate([table[at : at + 2 * LANES], table[at + 2 * LANES : at + 4 * LANES]], axis=1)
        high, low = halves(both)
        stack[k] = jnp.concatenate([high, low, high], axis=0)

    def turned(row):
        at = row * 2 * (frames + 1)
        real = held[pl.ds(at, frames), :]
        imag = held[pl.ds(at + frames + 1, frames), :]
        cos, sin = table[pl.ds(turns + row, 1), :], table[pl.ds(turns + HALF + row, 1), :]
        high_r, low_r = halves(real * cos + imag * sin)
        high_i, low_i = halves(imag * cos - real * sin)
        return jnp.concatenate([high_r, high_i, high_r, high_i, low_r, low_i], axis=1)

    def magnitude(terms, k):
        bins = jnp.dot(terms, stack[k], preferred_element_type=jnp.float32)
        real, imag = bins[:, :LANES], bins[:, LANES:]
        square = real * real + imag * imag
        found = (square * lax.rsqrt(jnp.maximum(square, LEAST))).astype(keep.dtype)
        peak[...] = jnp.maximum(peak[...], jnp.max(found.reshape(-1, 16, LANES), axis=0))
        return found

    peak[...] = jnp.zeros_like(peak)

    def rows_of(side, out):
        for group in range(HALF // 2 // GROUP):
            start = side * (HALF // 2) + group * GROUP
            found = magnitude(jnp.concatenate([turned(start + k) for k in range(GROUP)], axis=0), 0)
            for k in range(GROUP):
                out[group * GROUP + k] = found[k * frames : (k + 1) * frames]

    rows_of(1 - core[0], give)
    rows_of(core[0], keep)
    edge = magnitude(turned(0), 1)

    @pl.when(core[0] == 0)
    def _():
        keep[0] = edge

    @pl.when(core[0] != 0)
    def _():
        give[0] = edge


def spectrum(audio, core):
    frames = audio.shape[1] // FRAME
    table = jnp.asarray(tables())
    far = pl.BlockSpec(memory_space=pltpu.HBM)
    return pl.pallas_call(
        spectrum_kernel,
        out_shape=[jax.ShapeDtypeStruct((HALF // 2, frames, LANES), jnp.bfloat16)] * 2
        + [jax.ShapeDtypeStruct((16, LANES), jnp.bfloat16)],
        in_specs=[pl.BlockSpec(memory_space=pltpu.SMEM), far, far],
        out_specs=[pl.BlockSpec(memory_space=pltpu.VMEM)] * 3,
        scratch_shapes=[
            pltpu.VMEM((frames // CHUNK, 1, CHUNK * FRAME), jnp.bfloat16),
            pltpu.VMEM(table.shape, table.dtype),
            pltpu.VMEM((2, 6 * LANES, 2 * LANES), jnp.bfloat16),
            pltpu.VMEM((OUTER * (frames + 1), LANES), jnp.float32),
            pltpu.SemaphoreType.DMA((frames // CHUNK,)),
            pltpu.SemaphoreType.DMA((2,)),
        ],
        compiler_params=pltpu.CompilerParams(vmem_limit_bytes=105 * 2**19),
        cost_estimate=pl.CostEstimate(
            flops=6 * frames * FRAME * (OUTER + 2 * LANES), bytes_accessed=2**22, transcendentals=0
        ),
        name="spectrum",
    )(core, audio, table)


def update(state, numer, gram):
    return state * numer / jnp.dot(gram, state, precision=HIGHEST, preferred_element_type=jnp.float32)


def step_kernel(comps, grid, acts, parts, acts_out):
    rows, comp, lanes = comps.shape
    wide = jnp.concatenate([comps[r] for r in range(rows)], axis=1)
    tall = jnp.concatenate([grid[r] for r in range(rows)], axis=1)
    numer = lax.dot_general(wide.astype(jnp.bfloat16), tall, NT, preferred_element_type=jnp.float32)
    gram = lax.dot_general(wide, wide, NT, precision=HIGHEST, preferred_element_type=jnp.float32)
    acts_new = update(acts[...], numer, gram)
    acts_out[...] = acts_new
    gram = lax.dot_general(acts_new, acts_new, NT, precision=HIGHEST, preferred_element_type=jnp.float32)
    per = LANES // comp
    high = comp // per
    packed = jnp.concatenate([gram[j * high : (j + 1) * high] for j in range(per)], axis=1)
    sums = jnp.dot(acts_new.astype(jnp.bfloat16), tall, preferred_element_type=jnp.float32)
    for r in range(rows):
        parts[r, :comp, :] = sums[:, r * lanes : (r + 1) * lanes]
        parts[r, comp:, :] = packed


def advance(comps, grid, acts):
    rows, comp, lanes = comps.shape
    extra = comp * comp // LANES
    return pl.pallas_call(
        step_kernel,
        out_shape=(
            jax.ShapeDtypeStruct((rows, comp + extra, lanes), jnp.float32),
            jax.ShapeDtypeStruct(acts.shape, jnp.float32),
        ),
        compiler_params=pltpu.CompilerParams(vmem_limit_bytes=32 * 2**20),
        name="advance",
    )(comps, grid, acts)


def unpack(packed):
    high = packed.shape[0]
    comp = math.isqrt(packed.size)
    return packed.reshape(high, LANES // comp, comp).transpose(1, 0, 2).reshape(comp, comp)


def inner_order(natural):
    comp = natural.shape[0]
    cube = natural.reshape(comp, -1, OUTER).transpose(2, 0, 1)
    mirrored = jnp.concatenate([cube[HALF : HALF + 1], cube[: HALF : -1]], axis=0)
    return jnp.concatenate([cube[:HALF], mirrored], axis=2)


def natural_order(inner):
    comp, width = inner.shape[1], inner.shape[2] // 2
    low, mirrored = inner[:, :, :width], inner[:, :, width:]
    cube = jnp.concatenate([low, mirrored[:1], mirrored[:0:-1]], axis=0)
    return cube.transpose(1, 2, 0).reshape(comp, -1)


def gather_freq(block, n_freq, at):
    pieces = [block]
    for shift in range(1, n_freq):
        ring = [(i, (i + shift) % n_freq) for i in range(n_freq)]
        pieces.append(lax.ppermute(block, "freq", ring))
    placed = []
    for p in range(n_freq):
        value = pieces[0]
        for shift in range(1, n_freq):
            value = jnp.where((at - shift) % n_freq == p, pieces[shift], value)
        placed.append(value)
    return jnp.concatenate(placed, axis=1)


TOP = 13
SIDE = HALF // 2


def pack(gram):
    comp = gram.shape[0]
    per = LANES // comp
    high = comp // per
    return jnp.concatenate([gram[j * high : (j + 1) * high] for j in range(per)], axis=1)


def unpacked(packed):
    comp = math.isqrt(packed.size)
    return jnp.concatenate([packed[:, j * comp : (j + 1) * comp] for j in range(LANES // comp)], axis=0)


def exponent(value):
    peak = jnp.max(jnp.abs(value), axis=(0, 1), keepdims=True)
    return jnp.floor(jnp.log2(jnp.maximum(peak, 1e-30))) - TOP


def power(exps):
    count = jnp.abs(exps).astype(jnp.int32)
    value = jnp.ones_like(exps)
    for bit in range(7):
        step = jnp.where(exps < 0, 2.0 ** -(2**bit), 2.0 ** (2**bit))
        value = value * jnp.where((count >> bit) & 1 == 1, step, 1.0)
    return value


def places(shape):
    return [lax.broadcasted_iota(jnp.int32, shape, axis) for axis in range(2)]


def mirrored_at(r):
    return OUTER - r if r else HALF


def gram_of(value):
    rows = value.shape[0]
    both = jnp.concatenate(halves(value), axis=0)
    parts = lax.dot_general(both, both, NT, preferred_element_type=jnp.float32)
    cross = parts[:rows, rows:] + parts[rows:, :rows]
    return parts[:rows, :rows] + (cross + parts[rows:, rows:])


def start_kernel(at, own, other, keep, give, acts, acts_out, mine, held):
    comp = own.shape[0]
    row, side, first = at[0], at[1], at[2] == 0
    wide = jnp.concatenate(
        [jnp.where(first, own[...], other[...]), jnp.where(first, other[...], own[...])], axis=1
    )
    quads, eighth = LANES // comp, 8
    for q in range(eighth):
        columns = [wide[:, (c * eighth + q) * LANES : (c * eighth + q + 1) * LANES] for c in range(quads)]
        turned = jnp.concatenate(columns, axis=0).T
        for m in range(2):
            place = (2 * q + m) * (OUTER + 1)
            held[place : place + OUTER, :] = turned[m * OUTER : (m + 1) * OUTER]
    gram = gram_of(wide)
    span = OUTER // quads
    block = places((span, LANES))[1] // comp

    def pair(r):
        mirror = jnp.where(r == 0, HALF, OUTER - r)
        return [held[pl.ds(j, span, stride=OUTER + 1), :] for j in (r, mirror)]

    both = jnp.concatenate(pair(row), axis=0).T
    mine[...] = jnp.concatenate(
        [
            both[c * comp : (c + 1) * comp, h * span : (h + 1) * span]
            for h in range(2)
            for c in range(quads)
        ],
        axis=1,
    )
    total = jnp.zeros((acts.shape[1], LANES), jnp.float32)
    batch = 8
    for grid, start in ((keep, side * SIDE), (give, (1 - side) * SIDE)):
        for base in range(0, SIDE, batch):
            pieces = []
            for u in range(base, base + batch):
                for value in pair(start + u):
                    pieces += [jnp.where(block == c, value, 0.0).astype(jnp.bfloat16) for c in range(quads)]
            left = jnp.concatenate([grid[u] for u in range(base, base + batch)], axis=1)
            total += jnp.dot(left, jnp.concatenate(pieces, axis=0), preferred_element_type=jnp.float32)
    total = total.T
    numer = sum(total[c * comp : (c + 1) * comp] for c in range(quads))
    acts_out[...] = update(acts[...], numer, gram)


def sealed(sums, gram, squares, bound=None):
    comp = gram.shape[0]
    sums_exp, gram_exp = exponent(sums if bound is None else bound), exponent(squares)
    packed = pack(gram) * power(-gram_exp)
    rows, lanes = places(packed.shape)
    last, end = packed.shape[0] - 1, LANES - comp
    packed = jnp.where((rows == last) & (lanes == end), sums_exp, packed)
    packed = jnp.where((rows == last) & (lanes == end + 1), gram_exp, packed)
    return sums * power(-sums_exp), packed


def opened(got, comp):
    end = LANES - comp
    scales = power(got[:, got.shape[1] - 1, :])
    sources = range(got.shape[0])
    gram = sum(got[s, comp:, :] * scales[s : s + 1, end + 1 : end + 2] for s in sources)
    gram = unpacked(gram)
    at = places(gram.shape)
    for column in range(2):
        mirrored = gram[column : column + 1, comp - 1 : comp]
        gram = jnp.where((at[0] == comp - 1) & (at[1] == column), mirrored, gram)
    return [scales[s : s + 1, end : end + 1] for s in sources], gram


def tall(grid):
    return jnp.concatenate([grid[u] for u in range(SIDE)], axis=1)


def finish(acts, grids, parts, peak=None):
    comp = acts[0].shape[0]
    sums, gram, weight, squares = 0.0, 0.0, 0.0, 0.0
    for value, grid in zip(acts, grids):
        left = value.astype(jnp.bfloat16)
        weight += jnp.sum(left.astype(jnp.float32), axis=1, keepdims=True)
        squares += jnp.sum(value * value, axis=1, keepdims=True)
        sums += jnp.dot(left, tall(grid), preferred_element_type=jnp.float32)
        gram += lax.dot_general(value, value, NT, precision=HIGHEST, preferred_element_type=jnp.float32)
    sums, packed = sealed(sums, gram, squares, None if peak is None else weight * (1.01 * peak))
    for u in range(SIDE):
        parts[u, :comp, :] = sums[:, u * LANES : (u + 1) * LANES]
        parts[u, comp:, :] = packed


def sums_kernel(acts, sibling, keep, taken, parts):
    finish((acts[...], sibling[...]), (keep, taken), parts)


def partial_kernel(got, exps, keep, taken, peak, out):
    comp = got.shape[1]
    wide = jnp.concatenate([got[u] for u in range(SIDE)], axis=1) * power(exps[:, :1])
    left = wide.astype(jnp.bfloat16)
    for k, grid in enumerate((keep, taken)):
        out[k * comp : (k + 1) * comp, :] = lax.dot_general(
            left, tall(grid), NT, preferred_element_type=jnp.float32
        )
    packed = pack(gram_of(wide))
    rows, lanes = places(packed.shape)
    highest = jnp.max(peak[...].astype(jnp.float32), axis=(0, 1), keepdims=True)
    place = (rows == packed.shape[0] - 1) & (lanes == LANES - comp)
    out[2 * comp :, :] = jnp.where(place, highest, packed)


def again_kernel(half, other_half, acts, sibling, keep, taken, parts, acts_out):
    comp = acts.shape[0]
    mine, theirs = half[2 * comp :, :], other_half[2 * comp :, :]
    last, end = mine.shape[0] - 1, LANES - comp
    peak = jnp.maximum(mine, theirs)[last : last + 1, end : end + 1]
    gram = unpacked(mine + theirs)
    at = places(gram.shape)
    gram = jnp.where((at[0] == comp - 1) & (at[1] == 0), gram[:1, comp - 1 : comp], gram)
    new = update(acts[...], half[:comp, :] + other_half[comp : 2 * comp, :], gram)
    sibling_new = update(sibling[...], half[comp : 2 * comp, :] + other_half[:comp, :], gram)
    acts_out[...] = new
    finish((new, sibling_new), (keep, taken), parts, peak)


def eleven_bits(value):
    split = value * 8193.0
    return split - (split - value)


def rounded(value):
    def short(x):
        return x.astype(jnp.bfloat16).astype(jnp.float32)

    near = eleven_bits(value)
    step = jnp.abs(near) * 2.0**-10.6
    moved = eleven_bits(near + jnp.where(value > near, step, -step))
    return jnp.where(short(near) == short(value), near, moved)


def slice_of(got, mine):
    comp = mine.shape[0]
    scales, gram = opened(got, comp)
    sums = sum(got[s, :comp, :] * scales[s] for s in range(got.shape[0]))
    at = places(gram.shape)
    diagonal = jnp.sum(jnp.where(at[0] == at[1], gram, 0.0), axis=1, keepdims=True)
    bound = sum(scales) * 2.0 ** (TOP + 1) / jnp.maximum(diagonal, 1e-30)
    exps = jnp.clip(jnp.floor(jnp.log2(jnp.maximum(bound, 1e-30))), -100, 100) - TOP
    return update(mine[...], sums, gram), exps


def slice_kernel(got, mine, out, payload, exps_out):
    new, exps = slice_of(got, mine)
    out[...] = new
    payload[...] = rounded(new * power(-exps))
    exps_out[...] = jnp.broadcast_to(exps, exps_out.shape)


def last_kernel(got, mine, out, exps_out):
    new, exps = slice_of(got, mine)
    exps_out[...] = jnp.broadcast_to(exps, exps_out.shape)
    turned = (new * power(-exps)).T
    span = OUTER // 4
    for freq in range(2):
        starts = [h * OUTER + freq * 2 * span + half * span for h in range(2) for half in range(2)]
        out[freq] = jnp.concatenate([turned[a : a + span] for a in starts], axis=1)


def natural_kernel(at, got, exps, acts, partner, out, acts_out, low, high):
    comp = out.shape[0]
    span = OUTER // 4
    for r in range(HALF):
        value = got[r % SIDE * 2 + r // SIDE]
        low[pl.ds(r, span, stride=HALF + 1), :] = value
        high[pl.ds(mirrored_at(r) % HALF, span, stride=HALF + 1), :] = pltpu.roll(value, LANES // 2, 1)
    factor = power(exps[...])
    for pair in range(span // 2):
        rows = []
        for place in (2 * pair, 2 * pair + 1):
            begin = place * (HALF + 1)
            rows += [ref[begin : begin + HALF, :] for ref in (low, high)]
        turned = jnp.concatenate(rows, axis=0).T
        for half in range(2):
            begin = (half * (span // 2) + pair) * LANES
            out[:, begin : begin + LANES] = turned[half * comp : (half + 1) * comp] * factor
    first, own, other = at[2] == 0, acts[...], partner[...]
    acts_out[...] = jnp.concatenate([jnp.where(first, own, other), jnp.where(first, other, own)], axis=1)


def local(kernel, outs, name, *arrays, scratch=(), cost=None):
    vmem = pl.BlockSpec(memory_space=pltpu.VMEM)
    smem = pl.BlockSpec(memory_space=pltpu.SMEM)
    many = isinstance(outs, list)
    shapes = [jax.ShapeDtypeStruct(shape, dtype) for shape, dtype in (outs if many else [outs])]
    return pl.pallas_call(
        kernel,
        out_shape=shapes if many else shapes[0],
        in_specs=[smem if a.dtype == jnp.int32 else vmem for a in arrays],
        out_specs=[vmem] * len(outs) if many else vmem,
        scratch_shapes=list(scratch),
        compiler_params=pltpu.CompilerParams(vmem_limit_bytes=32 * 2**20),
        cost_estimate=cost,
        name=name,
    )(*arrays)


def row_shards(audio, w_start, h_start):
    f16, f32 = jnp.float16, jnp.float32
    comp = w_start.shape[0]
    swap = [(0, 1), (1, 0)]
    freq_at, core_at = lax.axis_index("freq"), lax.axis_index("core")
    q = freq_at * lax.axis_size("chips") + lax.axis_index("chips")
    at = jnp.stack([core_at * SIDE + q, core_at, freq_at]).astype(jnp.int32)
    other = lax.ppermute(w_start, "freq", swap)
    keep, give, peak = spectrum(audio, at[1:2])
    frames = keep.shape[1]
    extra = comp * comp // LANES
    taken = lax.ppermute(give, "core", swap)
    acts = lax.dynamic_slice_in_dim(h_start, freq_at * frames, frames, 1)
    message = ((SIDE, comp + extra, LANES), f32)
    lane_rows = ((comp, LANES), f32)

    def exchange(value, axes=("freq", "chips")):
        value = lax.all_to_all(value.astype(f16), axes, split_axis=0, concat_axis=0, tiled=True)
        return value.astype(f32)

    acts, mine = local(
        start_kernel,
        [(acts.shape, f32), lane_rows],
        "start",
        at,
        w_start,
        other,
        keep,
        give,
        acts,
        scratch=[pltpu.VMEM((LANES // 8 * (OUTER + 1), LANES), f32)],
        cost=pl.CostEstimate(flops=2**34, bytes_accessed=2**25, transcendentals=0),
    )
    sibling = lax.ppermute(acts, "core", swap)
    parts = local(sums_kernel, message, "sums", acts, sibling, keep, taken)
    for step in range(ITERS - 1):
        got = exchange(parts)
        mine, payload, exps = local(slice_kernel, [lane_rows] * 3, "slice", got, mine)
        got = exchange(jnp.broadcast_to(payload, (SIDE,) + payload.shape))
        half = local(partial_kernel, ((2 * comp + extra, LANES), f32), "partial", got, exps, keep, taken, peak)
        other_half = lax.ppermute(half, "core", swap)
        outs = [message, (acts.shape, f32)]
        parts, acts = local(
            again_kernel, outs, "again", half, other_half, acts, sibling, keep, taken
        )
    got = exchange(parts)
    acts, got = lax.optimization_barrier((acts, got))
    partner = lax.ppermute(acts, "freq", swap)
    final, exps = local(last_kernel, [((2, OUTER // 4, LANES), f32), lane_rows], "last", got, mine)
    final = jnp.broadcast_to(final[:, None], (2, HALF // 2) + final.shape[1:])
    got = exchange(final.reshape((HALF,) + final.shape[2:]), ("freq", "chips", "core"))
    return local(
        natural_kernel,
        [(w_start.shape, f32), (h_start.shape, f32)],
        "natural",
        at,
        got,
        exps,
        acts,
        partner,
        scratch=[pltpu.VMEM((OUTER // 4 * (HALF + 1), LANES), f32)] * 2,
    )


def shards(n_freq, n_tm, audio, w_start, h_start):
    n_dev = n_freq * n_tm
    comp, w_cols = w_start.shape
    bins = w_cols * n_freq
    own = bins // n_dev
    width = OUTER // n_freq
    freq_at = lax.axis_index("freq")
    me = freq_at * n_tm + lax.axis_index("tm")
    grid = jnp.concatenate(spectrum(audio, jnp.zeros((1,), jnp.int32))[:2], axis=0)
    frames = grid.shape[1]
    comps = inner_order(gather_freq(w_start, n_freq, freq_at))
    acts = lax.dynamic_slice_in_dim(h_start, freq_at * frames, frames, 1)
    per_row = LANES // own
    mine = lax.dynamic_slice(
        comps, (me // per_row, 0, me % per_row * own), (1, comp, own)
    ).reshape(comp, own)
    for step in range(ITERS):
        parts, acts = advance(comps, grid, acts)
        sums = parts[:, :comp].reshape(HALF, comp, per_row, own).transpose(0, 2, 1, 3)
        gram = jnp.broadcast_to(parts[0, comp:].reshape(1, -1), (n_dev, comp * comp))
        parts = jnp.concatenate([sums.reshape(n_dev, -1), gram], axis=1).reshape(n_dev, -1, LANES)
        got = lax.all_to_all(parts, ALL, split_axis=0, concat_axis=0, tiled=True)
        value = jnp.sum(got, axis=0)
        rows = comp * own // LANES
        mine = update(mine, value[:rows].reshape(comp, own), unpack(value[rows:]))
        every = jnp.broadcast_to(mine.reshape(1, -1, LANES), (n_dev, rows, LANES))
        comps = lax.all_to_all(every, ALL, split_axis=0, concat_axis=0, tiled=True)
        comps = comps.reshape(HALF, per_row, comp, own).transpose(0, 2, 1, 3)
        comps = comps.reshape(HALF, comp, LANES)
    cut = lax.dynamic_slice_in_dim(comps.reshape(HALF, comp, 2, OUTER), freq_at * width, width, 3)
    components = natural_order(cut.reshape(HALF, comp, 2 * width))
    activations = gather_freq(acts, n_freq, freq_at)
    return (components, activations)


def solution(mesh):
    sizes = (mesh.shape["freq"], mesh.shape["tm"])
    if sizes == (2, SIDE):
        devices = mesh.devices.reshape(2, SIDE // 2, 2)
        mesh = jax.sharding.Mesh(devices, ("freq", "chips", "core"))
        body, tm = row_shards, ("chips", "core")
    else:
        body, tm = functools.partial(shards, *sizes), "tm"
    return jax.shard_map(
        body,
        mesh=mesh,
        in_specs=(P(tm, "freq"), P(None, "freq"), P(None, tm)),
        out_specs=(P(None, "freq"), P(None, tm)),
        check_vma=False,
    )
```

```python
import functools
import math

import jax
import jax.numpy as jnp
import numpy as np
from jax import lax
from jax.experimental import pallas as pl
from jax.experimental.pallas import tpu as pltpu
from jax.sharding import PartitionSpec as P

ITERS = 2
HIGHEST = lax.Precision.HIGHEST
ALL = ("freq", "tm")
LANES = 128
OUTER = 64
HALF = OUTER // 2
FRAME = OUTER * LANES
CHUNK = 16
PAIR = 2
GROUP = 4
NT = (((1,), (1,)), ((), ()))
LEAST = 2.0**-126


def tables():
    a = np.arange(OUTER)
    i = np.arange(LANES)
    r = np.arange(HALF)
    position = a[:, None] * LANES + i[None, :]
    window = 0.5 - 0.5 * np.cos(2 * np.pi * position / FRAME)
    window = window / math.sqrt(0.375 * FRAME)
    angle = 2 * np.pi * (r[:, None] * a[None, :] % OUTER) / OUTER
    first = np.stack([np.cos(angle), -np.sin(angle)], axis=1).reshape(2 * HALF, OUTER)
    first[1] = np.cos(np.pi * a)
    turn = 2 * np.pi * r[:, None] * i[None, :] / FRAME
    turn_cos = np.cos(turn)
    turn_sin = np.sin(turn)
    m = np.arange(OUTER)
    column = np.concatenate([m, LANES - 1 - m])
    angle = 2 * np.pi * (i[:, None] * column[None, :] % LANES) / LANES
    top = np.concatenate([np.cos(angle), -np.sin(angle)], axis=1)
    bottom = np.concatenate([np.sin(angle), np.cos(angle)], axis=1)
    second = np.concatenate([top, bottom], axis=0)
    zero = np.zeros((LANES, OUTER))
    angle_a = 2 * np.pi * i[:, None] * (m * OUTER)[None, :] / FRAME
    angle_b = 2 * np.pi * i[:, None] * (m * OUTER + HALF)[None, :] / FRAME
    top = np.concatenate([np.cos(angle_a), zero, -np.sin(angle_a), zero], axis=1)
    bottom = np.concatenate([zero, np.cos(angle_b), zero, -np.sin(angle_b)], axis=1)
    edge = np.concatenate([top, bottom], axis=0)

    first = np.concatenate([first, np.zeros((OUTER, LANES - OUTER))], axis=1)
    second, edge = (np.concatenate([t[:, :LANES], t[:, LANES:]], axis=0) for t in (second, edge))
    parts = [window, first, turn_cos, turn_sin, second, edge]
    return np.concatenate(parts, axis=0).astype(np.float32)


def halves(value):
    high = value.astype(jnp.bfloat16)
    return high, (value - high.astype(jnp.float32)).astype(jnp.bfloat16)


def spectrum_kernel(core, audio, source, keep, give, peak, heard, table, stack, held, audio_sems, table_sems):
    frames = keep.shape[1]
    chunks = frames // CHUNK
    turns = 2 * OUTER

    def audio_copy(chunk):
        span = pl.ds(pl.multiple_of(chunk * CHUNK * FRAME, CHUNK * FRAME), CHUNK * FRAME)
        return pltpu.make_async_copy(audio.at[:, span], heard.at[chunk], audio_sems.at[chunk])

    def table_copy(k):
        span = pl.ds(0, turns) if k == 0 else pl.ds(turns, table.shape[0] - turns)
        return pltpu.make_async_copy(source.at[span], table.at[span], table_sems.at[k])

    table_copy(0).start()
    for chunk in range(chunks):
        audio_copy(chunk).start()
    table_copy(1).start()
    table_copy(0).wait()
    high, low = halves(table[OUTER:turns, :OUTER])
    first_terms = jnp.concatenate([high, low, high], axis=1)

    @pl.loop(0, chunks)
    def _(chunk):
        audio_copy(chunk).wait()
        samples = heard[chunk].reshape(CHUNK * OUTER, LANES).astype(jnp.float32)
        shape = table[:OUTER]
        for start in range(0, CHUNK, PAIR):
            columns = []
            for frame in range(start, start + PAIR):
                high, low = halves(samples[frame * OUTER : (frame + 1) * OUTER] * shape)
                columns.append(jnp.concatenate([high, high, low], axis=0))
            sums = jnp.dot(
                first_terms, jnp.concatenate(columns, axis=1), preferred_element_type=jnp.float32
            )
            for frame in range(start, start + PAIR):
                place = pl.ds(chunk * CHUNK + frame, OUTER, stride=frames + 1)
                held[place, :] = sums[:, (frame - start) * LANES : (frame - start + 1) * LANES]

    table_copy(1).wait()
    for k in range(2):
        at = turns + 2 * HALF + k * 4 * LANES
        both = jnp.concatenate([table[at : at + 2 * LANES], table[at + 2 * LANES : at + 4 * LANES]], axis=1)
        high, low = halves(both)
        stack[k] = jnp.concatenate([high, low, high], axis=0)

    def turned(row):
        at = row * 2 * (frames + 1)
        real = held[pl.ds(at, frames), :]
        imag = held[pl.ds(at + frames + 1, frames), :]
        cos, sin = table[pl.ds(turns + row, 1), :], table[pl.ds(turns + HALF + row, 1), :]
        high_r, low_r = halves(real * cos + imag * sin)
        high_i, low_i = halves(imag * cos - real * sin)
        return jnp.concatenate([high_r, high_i, high_r, high_i, low_r, low_i], axis=1)

    def magnitude(terms, k):
        bins = jnp.dot(terms, stack[k], preferred_element_type=jnp.float32)
        real, imag = bins[:, :LANES], bins[:, LANES:]
        square = real * real + imag * imag
        found = (square * lax.rsqrt(jnp.maximum(square, LEAST))).astype(keep.dtype)
        peak[...] = jnp.maximum(peak[...], jnp.max(found.reshape(-1, 16, LANES), axis=0))
        return found

    peak[...] = jnp.zeros_like(peak)

    def rows_of(side, out):
        for group in range(HALF // 2 // GROUP):
            start = side * (HALF // 2) + group * GROUP
            found = magnitude(jnp.concatenate([turned(start + k) for k in range(GROUP)], axis=0), 0)
            for k in range(GROUP):
                out[group * GROUP + k] = found[k * frames : (k + 1) * frames]

    rows_of(1 - core[0], give)
    rows_of(core[0], keep)
    edge = magnitude(turned(0), 1)

    @pl.when(core[0] == 0)
    def _():
        keep[0] = edge

    @pl.when(core[0] != 0)
    def _():
        give[0] = edge


def spectrum(audio, core):
    frames = audio.shape[1] // FRAME
    table = jnp.asarray(tables())
    far = pl.BlockSpec(memory_space=pltpu.HBM)
    return pl.pallas_call(
        spectrum_kernel,
        out_shape=[jax.ShapeDtypeStruct((HALF // 2, frames, LANES), jnp.bfloat16)] * 2
        + [jax.ShapeDtypeStruct((16, LANES), jnp.bfloat16)],
        in_specs=[pl.BlockSpec(memory_space=pltpu.SMEM), far, far],
        out_specs=[pl.BlockSpec(memory_space=pltpu.VMEM)] * 3,
        scratch_shapes=[
            pltpu.VMEM((frames // CHUNK, 1, CHUNK * FRAME), jnp.bfloat16),
            pltpu.VMEM(table.shape, table.dtype),
            pltpu.VMEM((2, 6 * LANES, 2 * LANES), jnp.bfloat16),
            pltpu.VMEM((OUTER * (frames + 1), LANES), jnp.float32),
            pltpu.SemaphoreType.DMA((frames // CHUNK,)),
            pltpu.SemaphoreType.DMA((2,)),
        ],
        compiler_params=pltpu.CompilerParams(vmem_limit_bytes=105 * 2**19),
        cost_estimate=pl.CostEstimate(
            flops=6 * frames * FRAME * (OUTER + 2 * LANES), bytes_accessed=2**22, transcendentals=0
        ),
        name="spectrum",
    )(core, audio, table)


def update(state, numer, gram):
    return state * numer / jnp.dot(gram, state, precision=HIGHEST, preferred_element_type=jnp.float32)


def step_kernel(comps, grid, acts, parts, acts_out):
    rows, comp, lanes = comps.shape
    wide = jnp.concatenate([comps[r] for r in range(rows)], axis=1)
    tall = jnp.concatenate([grid[r] for r in range(rows)], axis=1)
    numer = lax.dot_general(wide.astype(jnp.bfloat16), tall, NT, preferred_element_type=jnp.float32)
    gram = lax.dot_general(wide, wide, NT, precision=HIGHEST, preferred_element_type=jnp.float32)
    acts_new = update(acts[...], numer, gram)
    acts_out[...] = acts_new
    gram = lax.dot_general(acts_new, acts_new, NT, precision=HIGHEST, preferred_element_type=jnp.float32)
    per = LANES // comp
    high = comp // per
    packed = jnp.concatenate([gram[j * high : (j + 1) * high] for j in range(per)], axis=1)
    sums = jnp.dot(acts_new.astype(jnp.bfloat16), tall, preferred_element_type=jnp.float32)
    for r in range(rows):
        parts[r, :comp, :] = sums[:, r * lanes : (r + 1) * lanes]
        parts[r, comp:, :] = packed


def advance(comps, grid, acts):
    rows, comp, lanes = comps.shape
    extra = comp * comp // LANES
    return pl.pallas_call(
        step_kernel,
        out_shape=(
            jax.ShapeDtypeStruct((rows, comp + extra, lanes), jnp.float32),
            jax.ShapeDtypeStruct(acts.shape, jnp.float32),
        ),
        compiler_params=pltpu.CompilerParams(vmem_limit_bytes=32 * 2**20),
        name="advance",
    )(comps, grid, acts)


def unpack(packed):
    high = packed.shape[0]
    comp = math.isqrt(packed.size)
    return packed.reshape(high, LANES // comp, comp).transpose(1, 0, 2).reshape(comp, comp)


def inner_order(natural):
    comp = natural.shape[0]
    cube = natural.reshape(comp, -1, OUTER).transpose(2, 0, 1)
    mirrored = jnp.concatenate([cube[HALF : HALF + 1], cube[: HALF : -1]], axis=0)
    return jnp.concatenate([cube[:HALF], mirrored], axis=2)


def natural_order(inner):
    comp, width = inner.shape[1], inner.shape[2] // 2
    low, mirrored = inner[:, :, :width], inner[:, :, width:]
    cube = jnp.concatenate([low, mirrored[:1], mirrored[:0:-1]], axis=0)
    return cube.transpose(1, 2, 0).reshape(comp, -1)


def gather_freq(block, n_freq, at):
    pieces = [block]
    for shift in range(1, n_freq):
        ring = [(i, (i + shift) % n_freq) for i in range(n_freq)]
        pieces.append(lax.ppermute(block, "freq", ring))
    placed = []
    for p in range(n_freq):
        value = pieces[0]
        for shift in range(1, n_freq):
            value = jnp.where((at - shift) % n_freq == p, pieces[shift], value)
        placed.append(value)
    return jnp.concatenate(placed, axis=1)


TOP = 13
SIDE = HALF // 2


def pack(gram):
    comp = gram.shape[0]
    per = LANES // comp
    high = comp // per
    return jnp.concatenate([gram[j * high : (j + 1) * high] for j in range(per)], axis=1)


def unpacked(packed):
    comp = math.isqrt(packed.size)
    return jnp.concatenate([packed[:, j * comp : (j + 1) * comp] for j in range(LANES // comp)], axis=0)


def exponent(value):
    peak = jnp.max(jnp.abs(value), axis=(0, 1), keepdims=True)
    return jnp.floor(jnp.log2(jnp.maximum(peak, 1e-30))) - TOP


def power(exps):
    count = jnp.abs(exps).astype(jnp.int32)
    value = jnp.ones_like(exps)
    for bit in range(7):
        step = jnp.where(exps < 0, 2.0 ** -(2**bit), 2.0 ** (2**bit))
        value = value * jnp.where((count >> bit) & 1 == 1, step, 1.0)
    return value


def places(shape):
    return [lax.broadcasted_iota(jnp.int32, shape, axis) for axis in range(2)]


def mirrored_at(r):
    return OUTER - r if r else HALF


def gram_of(value):
    rows = value.shape[0]
    both = jnp.concatenate(halves(value), axis=0)
    parts = lax.dot_general(both, both, NT, preferred_element_type=jnp.float32)
    cross = parts[:rows, rows:] + parts[rows:, :rows]
    return parts[:rows, :rows] + (cross + parts[rows:, rows:])


def start_kernel(at, own, other, keep, give, acts, acts_out, mine, held):
    comp = own.shape[0]
    row, side, first = at[0], at[1], at[2] == 0
    wide = jnp.concatenate(
        [jnp.where(first, own[...], other[...]), jnp.where(first, other[...], own[...])], axis=1
    )
    quads, eighth = LANES // comp, 8
    for q in range(eighth):
        columns = [wide[:, (c * eighth + q) * LANES : (c * eighth + q + 1) * LANES] for c in range(quads)]
        turned = jnp.concatenate(columns, axis=0).T
        for m in range(2):
            place = (2 * q + m) * (OUTER + 1)
            held[place : place + OUTER, :] = turned[m * OUTER : (m + 1) * OUTER]
    gram = gram_of(wide)
    span = OUTER // quads
    block = places((span, LANES))[1] // comp

    def pair(r):
        mirror = jnp.where(r == 0, HALF, OUTER - r)
        return [held[pl.ds(j, span, stride=OUTER + 1), :] for j in (r, mirror)]

    both = jnp.concatenate(pair(row), axis=0).T
    mine[...] = jnp.concatenate(
        [
            both[c * comp : (c + 1) * comp, h * span : (h + 1) * span]
            for h in range(2)
            for c in range(quads)
        ],
        axis=1,
    )
    total = jnp.zeros((acts.shape[1], LANES), jnp.float32)
    batch = 8
    for grid, start in ((keep, side * SIDE), (give, (1 - side) * SIDE)):
        for base in range(0, SIDE, batch):
            pieces = []
            for u in range(base, base + batch):
                for value in pair(start + u):
                    pieces += [jnp.where(block == c, value, 0.0).astype(jnp.bfloat16) for c in range(quads)]
            left = jnp.concatenate([grid[u] for u in range(base, base + batch)], axis=1)
            total += jnp.dot(left, jnp.concatenate(pieces, axis=0), preferred_element_type=jnp.float32)
    total = total.T
    numer = sum(total[c * comp : (c + 1) * comp] for c in range(quads))
    acts_out[...] = update(acts[...], numer, gram)


def sealed(sums, gram, squares, bound=None):
    comp = gram.shape[0]
    sums_exp, gram_exp = exponent(sums if bound is None else bound), exponent(squares)
    packed = pack(gram) * power(-gram_exp)
    rows, lanes = places(packed.shape)
    last, end = packed.shape[0] - 1, LANES - comp
    packed = jnp.where((rows == last) & (lanes == end), sums_exp, packed)
    packed = jnp.where((rows == last) & (lanes == end + 1), gram_exp, packed)
    return sums * power(-sums_exp), packed


def opened(got, comp):
    end = LANES - comp
    scales = power(got[:, got.shape[1] - 1, :])
    sources = range(got.shape[0])
    gram = sum(got[s, comp:, :] * scales[s : s + 1, end + 1 : end + 2] for s in sources)
    gram = unpacked(gram)
    at = places(gram.shape)
    for column in range(2):
        mirrored = gram[column : column + 1, comp - 1 : comp]
        gram = jnp.where((at[0] == comp - 1) & (at[1] == column), mirrored, gram)
    return [scales[s : s + 1, end : end + 1] for s in sources], gram


def tall(grid):
    return jnp.concatenate([grid[u] for u in range(SIDE)], axis=1)


def finish(acts, grids, parts, peak=None):
    comp = acts[0].shape[0]
    left = [value.astype(jnp.bfloat16) for value in acts]
    both = jnp.concatenate([tall(grid) for grid in grids], axis=0)
    sums = jnp.dot(jnp.concatenate(left, axis=1), both, preferred_element_type=jnp.float32)
    gram, weight, squares = 0.0, 0.0, 0.0
    for value, short in zip(acts, left):
        weight += jnp.sum(short.astype(jnp.float32), axis=1, keepdims=True)
        squares += jnp.sum(value * value, axis=1, keepdims=True)
        gram += lax.dot_general(value, value, NT, precision=HIGHEST, preferred_element_type=jnp.float32)
    sums, packed = sealed(sums, gram, squares, None if peak is None else weight * (1.01 * peak))
    for u in range(SIDE):
        parts[u, :comp, :] = sums[:, u * LANES : (u + 1) * LANES]
        parts[u, comp:, :] = packed


def sums_kernel(acts, sibling, keep, taken, parts):
    finish((acts[...], sibling[...]), (keep, taken), parts)


def partial_kernel(got, exps, keep, taken, peak, out):
    comp = got.shape[1]
    wide = jnp.concatenate([got[u] for u in range(SIDE)], axis=1) * power(exps[:, :1])
    left = wide.astype(jnp.bfloat16)
    both = jnp.concatenate([tall(keep), tall(taken)], axis=0)
    numer = lax.dot_general(left, both, NT, preferred_element_type=jnp.float32)
    for k in range(2):
        out[k * comp : (k + 1) * comp, :] = numer[:, k * LANES : (k + 1) * LANES]
    packed = pack(gram_of(wide))
    rows, lanes = places(packed.shape)
    highest = jnp.max(peak[...].astype(jnp.float32), axis=(0, 1), keepdims=True)
    place = (rows == packed.shape[0] - 1) & (lanes == LANES - comp)
    out[2 * comp :, :] = jnp.where(place, highest, packed)


def again_kernel(half, other_half, acts, sibling, keep, taken, parts, acts_out):
    comp = acts.shape[0]
    mine, theirs = half[2 * comp :, :], other_half[2 * comp :, :]
    last, end = mine.shape[0] - 1, LANES - comp
    peak = jnp.maximum(mine, theirs)[last : last + 1, end : end + 1]
    gram = unpacked(mine + theirs)
    at = places(gram.shape)
    gram = jnp.where((at[0] == comp - 1) & (at[1] == 0), gram[:1, comp - 1 : comp], gram)
    new = update(acts[...], half[:comp, :] + other_half[comp : 2 * comp, :], gram)
    sibling_new = update(sibling[...], half[comp : 2 * comp, :] + other_half[:comp, :], gram)
    acts_out[...] = new
    finish((new, sibling_new), (keep, taken), parts, peak)


def eleven_bits(value):
    split = value * 8193.0
    return split - (split - value)


def rounded(value):
    def short(x):
        return x.astype(jnp.bfloat16).astype(jnp.float32)

    near = eleven_bits(value)
    step = jnp.abs(near) * 2.0**-10.6
    moved = eleven_bits(near + jnp.where(value > near, step, -step))
    return jnp.where(short(near) == short(value), near, moved)


def slice_of(got, mine):
    comp = mine.shape[0]
    scales, gram = opened(got, comp)
    sums = sum(got[s, :comp, :] * scales[s] for s in range(got.shape[0]))
    at = places(gram.shape)
    diagonal = jnp.sum(jnp.where(at[0] == at[1], gram, 0.0), axis=1, keepdims=True)
    bound = sum(scales) * 2.0 ** (TOP + 1) / jnp.maximum(diagonal, 1e-30)
    exps = jnp.clip(jnp.floor(jnp.log2(jnp.maximum(bound, 1e-30))), -100, 100) - TOP
    return update(mine[...], sums, gram), exps


def slice_kernel(got, mine, out, payload, exps_out):
    new, exps = slice_of(got, mine)
    out[...] = new
    payload[...] = rounded(new * power(-exps))
    exps_out[...] = jnp.broadcast_to(exps, exps_out.shape)


def last_kernel(got, mine, out, exps_out):
    new, exps = slice_of(got, mine)
    exps_out[...] = jnp.broadcast_to(exps, exps_out.shape)
    turned = (new * power(-exps)).T
    span = OUTER // 4
    for freq in range(2):
        starts = [h * OUTER + freq * 2 * span + half * span for h in range(2) for half in range(2)]
        out[freq] = jnp.concatenate([turned[a : a + span] for a in starts], axis=1)


def natural_kernel(at, got, exps, acts, partner, out, acts_out, low, high):
    comp = out.shape[0]
    span = OUTER // 4
    for r in range(HALF):
        value = got[r % SIDE * 2 + r // SIDE]
        low[pl.ds(r, span, stride=HALF + 1), :] = value
        high[pl.ds(mirrored_at(r) % HALF, span, stride=HALF + 1), :] = pltpu.roll(value, LANES // 2, 1)
    factor = power(exps[...])
    for pair in range(span // 2):
        rows = []
        for place in (2 * pair, 2 * pair + 1):
            begin = place * (HALF + 1)
            rows += [ref[begin : begin + HALF, :] for ref in (low, high)]
        turned = jnp.concatenate(rows, axis=0).T
        for half in range(2):
            begin = (half * (span // 2) + pair) * LANES
            out[:, begin : begin + LANES] = turned[half * comp : (half + 1) * comp] * factor
    first, own, other = at[2] == 0, acts[...], partner[...]
    acts_out[...] = jnp.concatenate([jnp.where(first, own, other), jnp.where(first, other, own)], axis=1)


def local(kernel, outs, name, *arrays, scratch=(), cost=None):
    vmem = pl.BlockSpec(memory_space=pltpu.VMEM)
    smem = pl.BlockSpec(memory_space=pltpu.SMEM)
    many = isinstance(outs, list)
    shapes = [jax.ShapeDtypeStruct(shape, dtype) for shape, dtype in (outs if many else [outs])]
    return pl.pallas_call(
        kernel,
        out_shape=shapes if many else shapes[0],
        in_specs=[smem if a.dtype == jnp.int32 else vmem for a in arrays],
        out_specs=[vmem] * len(outs) if many else vmem,
        scratch_shapes=list(scratch),
        compiler_params=pltpu.CompilerParams(vmem_limit_bytes=32 * 2**20),
        cost_estimate=cost,
        name=name,
    )(*arrays)


def row_shards(audio, w_start, h_start):
    f16, f32 = jnp.float16, jnp.float32
    comp = w_start.shape[0]
    swap = [(0, 1), (1, 0)]
    freq_at, core_at = lax.axis_index("freq"), lax.axis_index("core")
    q = freq_at * lax.axis_size("chips") + lax.axis_index("chips")
    at = jnp.stack([core_at * SIDE + q, core_at, freq_at]).astype(jnp.int32)
    other = lax.ppermute(w_start, "freq", swap)
    keep, give, peak = spectrum(audio, at[1:2])
    frames = keep.shape[1]
    extra = comp * comp // LANES
    taken = lax.ppermute(give, "core", swap)
    acts = lax.dynamic_slice_in_dim(h_start, freq_at * frames, frames, 1)
    message = ((SIDE, comp + extra, LANES), f32)
    lane_rows = ((comp, LANES), f32)

    def exchange(value, axes=("freq", "chips")):
        value = lax.all_to_all(value.astype(f16), axes, split_axis=0, concat_axis=0, tiled=True)
        return value.astype(f32)

    acts, mine = local(
        start_kernel,
        [(acts.shape, f32), lane_rows],
        "start",
        at,
        w_start,
        other,
        keep,
        give,
        acts,
        scratch=[pltpu.VMEM((LANES // 8 * (OUTER + 1), LANES), f32)],
        cost=pl.CostEstimate(flops=2**34, bytes_accessed=2**25, transcendentals=0),
    )
    sibling = lax.ppermute(acts, "core", swap)
    parts = local(sums_kernel, message, "sums", acts, sibling, keep, taken)
    for step in range(ITERS - 1):
        got = exchange(parts)
        mine, payload, exps = local(slice_kernel, [lane_rows] * 3, "slice", got, mine)
        got = exchange(jnp.broadcast_to(payload, (SIDE,) + payload.shape))
        half = local(partial_kernel, ((2 * comp + extra, LANES), f32), "partial", got, exps, keep, taken, peak)
        other_half = lax.ppermute(half, "core", swap)
        outs = [message, (acts.shape, f32)]
        parts, acts = local(
            again_kernel, outs, "again", half, other_half, acts, sibling, keep, taken
        )
    got = exchange(parts)
    acts, got = lax.optimization_barrier((acts, got))
    partner = lax.ppermute(acts, "freq", swap)
    final, exps = local(last_kernel, [((2, OUTER // 4, LANES), f32), lane_rows], "last", got, mine)
    final = jnp.broadcast_to(final[:, None], (2, HALF // 2) + final.shape[1:])
    got = exchange(final.reshape((HALF,) + final.shape[2:]), ("freq", "chips", "core"))
    return local(
        natural_kernel,
        [(w_start.shape, f32), (h_start.shape, f32)],
        "natural",
        at,
        got,
        exps,
        acts,
        partner,
        scratch=[pltpu.VMEM((OUTER // 4 * (HALF + 1), LANES), f32)] * 2,
    )


def shards(n_freq, n_tm, audio, w_start, h_start):
    n_dev = n_freq * n_tm
    comp, w_cols = w_start.shape
    bins = w_cols * n_freq
    own = bins // n_dev
    width = OUTER // n_freq
    freq_at = lax.axis_index("freq")
    me = freq_at * n_tm + lax.axis_index("tm")
    grid = jnp.concatenate(spectrum(audio, jnp.zeros((1,), jnp.int32))[:2], axis=0)
    frames = grid.shape[1]
    comps = inner_order(gather_freq(w_start, n_freq, freq_at))
    acts = lax.dynamic_slice_in_dim(h_start, freq_at * frames, frames, 1)
    per_row = LANES // own
    mine = lax.dynamic_slice(
        comps, (me // per_row, 0, me % per_row * own), (1, comp, own)
    ).reshape(comp, own)
    for step in range(ITERS):
        parts, acts = advance(comps, grid, acts)
        sums = parts[:, :comp].reshape(HALF, comp, per_row, own).transpose(0, 2, 1, 3)
        gram = jnp.broadcast_to(parts[0, comp:].reshape(1, -1), (n_dev, comp * comp))
        parts = jnp.concatenate([sums.reshape(n_dev, -1), gram], axis=1).reshape(n_dev, -1, LANES)
        got = lax.all_to_all(parts, ALL, split_axis=0, concat_axis=0, tiled=True)
        value = jnp.sum(got, axis=0)
        rows = comp * own // LANES
        mine = update(mine, value[:rows].reshape(comp, own), unpack(value[rows:]))
        every = jnp.broadcast_to(mine.reshape(1, -1, LANES), (n_dev, rows, LANES))
        comps = lax.all_to_all(every, ALL, split_axis=0, concat_axis=0, tiled=True)
        comps = comps.reshape(HALF, per_row, comp, own).transpose(0, 2, 1, 3)
        comps = comps.reshape(HALF, comp, LANES)
    cut = lax.dynamic_slice_in_dim(comps.reshape(HALF, comp, 2, OUTER), freq_at * width, width, 3)
    components = natural_order(cut.reshape(HALF, comp, 2 * width))
    activations = gather_freq(acts, n_freq, freq_at)
    return (components, activations)


def solution(mesh):
    sizes = (mesh.shape["freq"], mesh.shape["tm"])
    if sizes == (2, SIDE):
        devices = mesh.devices.reshape(2, SIDE // 2, 2)
        mesh = jax.sharding.Mesh(devices, ("freq", "chips", "core"))
        body, tm = row_shards, ("chips", "core")
    else:
        body, tm = functools.partial(shards, *sizes), "tm"
    return jax.shard_map(
        body,
        mesh=mesh,
        in_specs=(P(tm, "freq"), P(None, "freq"), P(None, tm)),
        out_specs=(P(None, "freq"), P(None, tm)),
        check_vma=False,
    )
```

```python
import functools
import math

import jax
import jax.numpy as jnp
import numpy as np
from jax import lax
from jax.experimental import pallas as pl
from jax.experimental.pallas import tpu as pltpu
from jax.sharding import PartitionSpec as P

ITERS = 2
HIGHEST = lax.Precision.HIGHEST
ALL = ("freq", "tm")
LANES = 128
OUTER = 64
HALF = OUTER // 2
FRAME = OUTER * LANES
CHUNK = 16
PAIR = 2
GROUP = 4
NT = (((1,), (1,)), ((), ()))
LEAST = 2.0**-126


def tables():
    a = np.arange(OUTER)
    i = np.arange(LANES)
    r = np.arange(HALF)
    position = a[:, None] * LANES + i[None, :]
    window = 0.5 - 0.5 * np.cos(2 * np.pi * position / FRAME)
    window = window / math.sqrt(0.375 * FRAME)
    angle = 2 * np.pi * (r[:, None] * a[None, :] % OUTER) / OUTER
    first = np.stack([np.cos(angle), -np.sin(angle)], axis=1).reshape(2 * HALF, OUTER)
    first[1] = np.cos(np.pi * a)
    turn = 2 * np.pi * r[:, None] * i[None, :] / FRAME
    turn_cos = np.cos(turn)
    turn_sin = np.sin(turn)
    m = np.arange(OUTER)
    column = np.concatenate([m, LANES - 1 - m])
    angle = 2 * np.pi * (i[:, None] * column[None, :] % LANES) / LANES
    top = np.concatenate([np.cos(angle), -np.sin(angle)], axis=1)
    bottom = np.concatenate([np.sin(angle), np.cos(angle)], axis=1)
    second = np.concatenate([top, bottom], axis=0)
    zero = np.zeros((LANES, OUTER))
    angle_a = 2 * np.pi * i[:, None] * (m * OUTER)[None, :] / FRAME
    angle_b = 2 * np.pi * i[:, None] * (m * OUTER + HALF)[None, :] / FRAME
    top = np.concatenate([np.cos(angle_a), zero, -np.sin(angle_a), zero], axis=1)
    bottom = np.concatenate([zero, np.cos(angle_b), zero, -np.sin(angle_b)], axis=1)
    edge = np.concatenate([top, bottom], axis=0)

    first = np.concatenate([first, np.zeros((OUTER, LANES - OUTER))], axis=1)
    second, edge = (np.concatenate([t[:, :LANES], t[:, LANES:]], axis=0) for t in (second, edge))
    parts = [window, first, turn_cos, turn_sin, second, edge]
    return np.concatenate(parts, axis=0).astype(np.float32)


def halves(value):
    high = value.astype(jnp.bfloat16)
    return high, (value - high.astype(jnp.float32)).astype(jnp.bfloat16)


def spectrum_kernel(core, audio, source, keep, give, peak, heard, table, stack, held, audio_sems, table_sems):
    frames = keep.shape[1]
    chunks = frames // CHUNK
    turns = 2 * OUTER

    def audio_copy(chunk):
        span = pl.ds(pl.multiple_of(chunk * CHUNK * FRAME, CHUNK * FRAME), CHUNK * FRAME)
        return pltpu.make_async_copy(audio.at[:, span], heard.at[chunk], audio_sems.at[chunk])

    def table_copy(k):
        span = pl.ds(0, turns) if k == 0 else pl.ds(turns, table.shape[0] - turns)
        return pltpu.make_async_copy(source.at[span], table.at[span], table_sems.at[k])

    table_copy(0).start()
    for chunk in range(chunks):
        audio_copy(chunk).start()
    table_copy(1).start()
    table_copy(0).wait()
    high, low = halves(table[OUTER:turns, :OUTER])
    first_terms = jnp.concatenate([high, low, high], axis=1)

    @pl.loop(0, chunks)
    def _(chunk):
        audio_copy(chunk).wait()
        samples = heard[chunk].reshape(CHUNK * OUTER, LANES).astype(jnp.float32)
        shape = table[:OUTER]
        for start in range(0, CHUNK, PAIR):
            columns = []
            for frame in range(start, start + PAIR):
                high, low = halves(samples[frame * OUTER : (frame + 1) * OUTER] * shape)
                columns.append(jnp.concatenate([high, high, low], axis=0))
            sums = jnp.dot(
                first_terms, jnp.concatenate(columns, axis=1), preferred_element_type=jnp.float32
            )
            for frame in range(start, start + PAIR):
                place = pl.ds(chunk * CHUNK + frame, OUTER, stride=frames + 1)
                held[place, :] = sums[:, (frame - start) * LANES : (frame - start + 1) * LANES]

    table_copy(1).wait()
    for k in range(2):
        at = turns + 2 * HALF + k * 4 * LANES
        both = jnp.concatenate([table[at : at + 2 * LANES], table[at + 2 * LANES : at + 4 * LANES]], axis=1)
        high, low = halves(both)
        stack[k] = jnp.concatenate([high, low, high], axis=0)

    def turned(row):
        at = row * 2 * (frames + 1)
        real = held[pl.ds(at, frames), :]
        imag = held[pl.ds(at + frames + 1, frames), :]
        cos, sin = table[pl.ds(turns + row, 1), :], table[pl.ds(turns + HALF + row, 1), :]
        high_r, low_r = halves(real * cos + imag * sin)
        high_i, low_i = halves(imag * cos - real * sin)
        return jnp.concatenate([high_r, high_i, high_r, high_i, low_r, low_i], axis=1)

    def magnitude(terms, k):
        bins = jnp.dot(terms, stack[k], preferred_element_type=jnp.float32)
        real, imag = bins[:, :LANES], bins[:, LANES:]
        square = real * real + imag * imag
        found = (square * lax.rsqrt(jnp.maximum(square, LEAST))).astype(keep.dtype)
        peak[...] = jnp.maximum(peak[...], jnp.max(found.reshape(-1, 16, LANES), axis=0))
        return found

    peak[...] = jnp.zeros_like(peak)

    def rows_of(side, out):
        for group in range(HALF // 2 // GROUP):
            start = side * (HALF // 2) + group * GROUP
            found = magnitude(jnp.concatenate([turned(start + k) for k in range(GROUP)], axis=0), 0)
            for k in range(GROUP):
                out[group * GROUP + k] = found[k * frames : (k + 1) * frames]

    rows_of(1 - core[0], give)
    rows_of(core[0], keep)
    edge = magnitude(turned(0), 1)

    @pl.when(core[0] == 0)
    def _():
        keep[0] = edge

    @pl.when(core[0] != 0)
    def _():
        give[0] = edge


def spectrum(audio, core):
    frames = audio.shape[1] // FRAME
    table = jnp.asarray(tables())
    far = pl.BlockSpec(memory_space=pltpu.HBM)
    return pl.pallas_call(
        spectrum_kernel,
        out_shape=[jax.ShapeDtypeStruct((HALF // 2, frames, LANES), jnp.bfloat16)] * 2
        + [jax.ShapeDtypeStruct((16, LANES), jnp.bfloat16)],
        in_specs=[pl.BlockSpec(memory_space=pltpu.SMEM), far, far],
        out_specs=[pl.BlockSpec(memory_space=pltpu.VMEM)] * 3,
        scratch_shapes=[
            pltpu.VMEM((frames // CHUNK, 1, CHUNK * FRAME), jnp.bfloat16),
            pltpu.VMEM(table.shape, table.dtype),
            pltpu.VMEM((2, 6 * LANES, 2 * LANES), jnp.bfloat16),
            pltpu.VMEM((OUTER * (frames + 1), LANES), jnp.float32),
            pltpu.SemaphoreType.DMA((frames // CHUNK,)),
            pltpu.SemaphoreType.DMA((2,)),
        ],
        compiler_params=pltpu.CompilerParams(vmem_limit_bytes=105 * 2**19),
        cost_estimate=pl.CostEstimate(
            flops=6 * frames * FRAME * (OUTER + 2 * LANES), bytes_accessed=2**22, transcendentals=0
        ),
        name="spectrum",
    )(core, audio, table)


def update(state, numer, gram):
    return state * numer / jnp.dot(gram, state, precision=HIGHEST, preferred_element_type=jnp.float32)


def step_kernel(comps, grid, acts, parts, acts_out):
    rows, comp, lanes = comps.shape
    wide = jnp.concatenate([comps[r] for r in range(rows)], axis=1)
    tall = jnp.concatenate([grid[r] for r in range(rows)], axis=1)
    numer = lax.dot_general(wide.astype(jnp.bfloat16), tall, NT, preferred_element_type=jnp.float32)
    gram = lax.dot_general(wide, wide, NT, precision=HIGHEST, preferred_element_type=jnp.float32)
    acts_new = update(acts[...], numer, gram)
    acts_out[...] = acts_new
    gram = lax.dot_general(acts_new, acts_new, NT, precision=HIGHEST, preferred_element_type=jnp.float32)
    per = LANES // comp
    high = comp // per
    packed = jnp.concatenate([gram[j * high : (j + 1) * high] for j in range(per)], axis=1)
    sums = jnp.dot(acts_new.astype(jnp.bfloat16), tall, preferred_element_type=jnp.float32)
    for r in range(rows):
        parts[r, :comp, :] = sums[:, r * lanes : (r + 1) * lanes]
        parts[r, comp:, :] = packed


def advance(comps, grid, acts):
    rows, comp, lanes = comps.shape
    extra = comp * comp // LANES
    return pl.pallas_call(
        step_kernel,
        out_shape=(
            jax.ShapeDtypeStruct((rows, comp + extra, lanes), jnp.float32),
            jax.ShapeDtypeStruct(acts.shape, jnp.float32),
        ),
        compiler_params=pltpu.CompilerParams(vmem_limit_bytes=32 * 2**20),
        name="advance",
    )(comps, grid, acts)


def unpack(packed):
    high = packed.shape[0]
    comp = math.isqrt(packed.size)
    return packed.reshape(high, LANES // comp, comp).transpose(1, 0, 2).reshape(comp, comp)


def inner_order(natural):
    comp = natural.shape[0]
    cube = natural.reshape(comp, -1, OUTER).transpose(2, 0, 1)
    mirrored = jnp.concatenate([cube[HALF : HALF + 1], cube[: HALF : -1]], axis=0)
    return jnp.concatenate([cube[:HALF], mirrored], axis=2)


def natural_order(inner):
    comp, width = inner.shape[1], inner.shape[2] // 2
    low, mirrored = inner[:, :, :width], inner[:, :, width:]
    cube = jnp.concatenate([low, mirrored[:1], mirrored[:0:-1]], axis=0)
    return cube.transpose(1, 2, 0).reshape(comp, -1)


def gather_freq(block, n_freq, at):
    pieces = [block]
    for shift in range(1, n_freq):
        ring = [(i, (i + shift) % n_freq) for i in range(n_freq)]
        pieces.append(lax.ppermute(block, "freq", ring))
    placed = []
    for p in range(n_freq):
        value = pieces[0]
        for shift in range(1, n_freq):
            value = jnp.where((at - shift) % n_freq == p, pieces[shift], value)
        placed.append(value)
    return jnp.concatenate(placed, axis=1)


TOP = 13
SIDE = HALF // 2


def pack(gram):
    comp = gram.shape[0]
    per = LANES // comp
    high = comp // per
    return jnp.concatenate([gram[j * high : (j + 1) * high] for j in range(per)], axis=1)


def unpacked(packed):
    comp = math.isqrt(packed.size)
    return jnp.concatenate([packed[:, j * comp : (j + 1) * comp] for j in range(LANES // comp)], axis=0)


def exponent(value):
    peak = jnp.max(jnp.abs(value), axis=(0, 1), keepdims=True)
    return jnp.floor(jnp.log2(jnp.maximum(peak, 1e-30))) - TOP


def power(exps):
    count = jnp.abs(exps).astype(jnp.int32)
    value = jnp.ones_like(exps)
    for bit in range(7):
        step = jnp.where(exps < 0, 2.0 ** -(2**bit), 2.0 ** (2**bit))
        value = value * jnp.where((count >> bit) & 1 == 1, step, 1.0)
    return value


def places(shape):
    return [lax.broadcasted_iota(jnp.int32, shape, axis) for axis in range(2)]


def mirrored_at(r):
    return OUTER - r if r else HALF


def gram_of(value):
    rows = value.shape[0]
    both = jnp.concatenate(halves(value), axis=0)
    parts = lax.dot_general(both, both, NT, preferred_element_type=jnp.float32)
    cross = parts[:rows, rows:] + parts[rows:, :rows]
    return parts[:rows, :rows] + (cross + parts[rows:, rows:])


def start_kernel(at, own, other, keep, give, acts, acts_out, mine, held):
    comp = own.shape[0]
    row, side, first = at[0], at[1], at[2] == 0
    wide = jnp.concatenate(
        [jnp.where(first, own[...], other[...]), jnp.where(first, other[...], own[...])], axis=1
    )
    quads, eighth = LANES // comp, 8
    for q in range(eighth):
        columns = [wide[:, (c * eighth + q) * LANES : (c * eighth + q + 1) * LANES] for c in range(quads)]
        turned = jnp.concatenate(columns, axis=0).T
        for m in range(2):
            place = (2 * q + m) * (OUTER + 1)
            held[place : place + OUTER, :] = turned[m * OUTER : (m + 1) * OUTER]
    gram = gram_of(wide)
    span = OUTER // quads
    block = places((span, LANES))[1] // comp

    def pair(r):
        mirror = jnp.where(r == 0, HALF, OUTER - r)
        return [held[pl.ds(j, span, stride=OUTER + 1), :] for j in (r, mirror)]

    both = jnp.concatenate(pair(row), axis=0).T
    mine[...] = jnp.concatenate(
        [
            both[c * comp : (c + 1) * comp, h * span : (h + 1) * span]
            for h in range(2)
            for c in range(quads)
        ],
        axis=1,
    )
    total = jnp.zeros((acts.shape[1], LANES), jnp.float32)
    batch = 8
    for grid, start in ((keep, side * SIDE), (give, (1 - side) * SIDE)):
        for base in range(0, SIDE, batch):
            pieces = []
            for u in range(base, base + batch):
                for value in pair(start + u):
                    pieces += [jnp.where(block == c, value, 0.0).astype(jnp.bfloat16) for c in range(quads)]
            left = jnp.concatenate([grid[u] for u in range(base, base + batch)], axis=1)
            total += jnp.dot(left, jnp.concatenate(pieces, axis=0), preferred_element_type=jnp.float32)
    total = total.T
    numer = sum(total[c * comp : (c + 1) * comp] for c in range(quads))
    acts_out[...] = update(acts[...], numer, gram)


def sealed(sums, gram, squares, bound=None):
    comp = gram.shape[0]
    sums_exp, gram_exp = exponent(sums if bound is None else bound), exponent(squares)
    packed = pack(gram) * power(-gram_exp)
    rows, lanes = places(packed.shape)
    last, end = packed.shape[0] - 1, LANES - comp
    packed = jnp.where((rows == last) & (lanes == end), sums_exp, packed)
    packed = jnp.where((rows == last) & (lanes == end + 1), gram_exp, packed)
    return sums * power(-sums_exp), packed


def opened(got, comp):
    end = LANES - comp
    scales = power(got[:, got.shape[1] - 1, :])
    sources = range(got.shape[0])
    gram = sum(got[s, comp:, :] * scales[s : s + 1, end + 1 : end + 2] for s in sources)
    gram = unpacked(gram)
    at = places(gram.shape)
    for column in range(2):
        mirrored = gram[column : column + 1, comp - 1 : comp]
        gram = jnp.where((at[0] == comp - 1) & (at[1] == column), mirrored, gram)
    return [scales[s : s + 1, end : end + 1] for s in sources], gram


def tall(grid):
    return jnp.concatenate([grid[u] for u in range(SIDE)], axis=1)


def finish(acts, grids, parts, peak=None):
    comp = acts[0].shape[0]
    left = [value.astype(jnp.bfloat16) for value in acts]
    both = jnp.concatenate([tall(grid) for grid in grids], axis=0)
    sums = jnp.dot(jnp.concatenate(left, axis=1), both, preferred_element_type=jnp.float32)
    gram, weight, squares = 0.0, 0.0, 0.0
    for value, short in zip(acts, left):
        weight += jnp.sum(short.astype(jnp.float32), axis=1, keepdims=True)
        squares += jnp.sum(value * value, axis=1, keepdims=True)
        gram += lax.dot_general(value, value, NT, precision=HIGHEST, preferred_element_type=jnp.float32)
    sums, packed = sealed(sums, gram, squares, None if peak is None else weight * (1.01 * peak))
    for u in range(SIDE):
        parts[u, :comp, :] = sums[:, u * LANES : (u + 1) * LANES]
        parts[u, comp:, :] = packed


def sums_kernel(acts, sibling, keep, taken, parts):
    finish((acts[...], sibling[...]), (keep, taken), parts)


def partial_kernel(got, exps, keep, taken, peak, out):
    comp = got.shape[1]
    wide = jnp.concatenate([got[u] for u in range(SIDE)], axis=1) * power(exps[:, :1])
    left = wide.astype(jnp.bfloat16)
    both = jnp.concatenate([tall(keep), tall(taken)], axis=0)
    numer = lax.dot_general(left, both, NT, preferred_element_type=jnp.float32)
    for k in range(2):
        out[k * comp : (k + 1) * comp, :] = numer[:, k * LANES : (k + 1) * LANES]
    packed = pack(gram_of(wide))
    rows, lanes = places(packed.shape)
    highest = jnp.max(peak[...].astype(jnp.float32), axis=(0, 1), keepdims=True)
    place = (rows == packed.shape[0] - 1) & (lanes == LANES - comp)
    out[2 * comp :, :] = jnp.where(place, highest, packed)


def again_kernel(half, other_half, acts, sibling, keep, taken, parts, acts_out):
    comp = acts.shape[0]
    mine, theirs = half[2 * comp :, :], other_half[2 * comp :, :]
    last, end = mine.shape[0] - 1, LANES - comp
    peak = jnp.maximum(mine, theirs)[last : last + 1, end : end + 1]
    gram = unpacked(mine + theirs)
    at = places(gram.shape)
    gram = jnp.where((at[0] == comp - 1) & (at[1] == 0), gram[:1, comp - 1 : comp], gram)
    new = update(acts[...], half[:comp, :] + other_half[comp : 2 * comp, :], gram)
    sibling_new = update(sibling[...], half[comp : 2 * comp, :] + other_half[:comp, :], gram)
    acts_out[...] = new
    finish((new, sibling_new), (keep, taken), parts, peak)


def eleven_bits(value):
    split = value * 8193.0
    return split - (split - value)


def rounded(value):
    def short(x):
        return x.astype(jnp.bfloat16).astype(jnp.float32)

    near = eleven_bits(value)
    step = jnp.abs(near) * 2.0**-10.6
    moved = eleven_bits(near + jnp.where(value > near, step, -step))
    return jnp.where(short(near) == short(value), near, moved)


def slice_of(got, mine):
    comp = mine.shape[0]
    scales, gram = opened(got, comp)
    sums = sum(got[s, :comp, :] * scales[s] for s in range(got.shape[0]))
    at = places(gram.shape)
    diagonal = jnp.sum(jnp.where(at[0] == at[1], gram, 0.0), axis=1, keepdims=True)
    bound = sum(scales) * 2.0 ** (TOP + 1) / jnp.maximum(diagonal, 1e-30)
    exps = jnp.clip(jnp.floor(jnp.log2(jnp.maximum(bound, 1e-30))), -100, 100) - TOP
    return update(mine[...], sums, gram), exps


def slice_kernel(got, mine, out, payload, exps_out):
    new, exps = slice_of(got, mine)
    out[...] = new
    payload[...] = rounded(new * power(-exps))
    exps_out[...] = jnp.broadcast_to(exps, exps_out.shape)


def last_kernel(got, mine, out, exps_out):
    new, exps = slice_of(got, mine)
    exps_out[...] = jnp.broadcast_to(exps, exps_out.shape)
    turned = (new * power(-exps)).T
    span = OUTER // 4
    for freq in range(2):
        starts = [h * OUTER + freq * 2 * span + half * span for h in range(2) for half in range(2)]
        out[freq] = jnp.concatenate([turned[a : a + span] for a in starts], axis=1)


def natural_kernel(got, exps, out, low, high):
    comp = out.shape[0]
    span = OUTER // 4
    for r in range(HALF):
        value = got[r % SIDE * 2 + r // SIDE]
        low[pl.ds(r, span, stride=HALF + 1), :] = value
        high[pl.ds(mirrored_at(r) % HALF, span, stride=HALF + 1), :] = pltpu.roll(value, LANES // 2, 1)
    factor = power(exps[...])
    for pair in range(span // 2):
        rows = []
        for place in (2 * pair, 2 * pair + 1):
            begin = place * (HALF + 1)
            rows += [ref[begin : begin + HALF, :] for ref in (low, high)]
        turned = jnp.concatenate(rows, axis=0).T
        for half in range(2):
            begin = (half * (span // 2) + pair) * LANES
            out[:, begin : begin + LANES] = turned[half * comp : (half + 1) * comp] * factor


def local(kernel, outs, name, *arrays, scratch=(), cost=None):
    vmem = pl.BlockSpec(memory_space=pltpu.VMEM)
    smem = pl.BlockSpec(memory_space=pltpu.SMEM)
    many = isinstance(outs, list)
    shapes = [jax.ShapeDtypeStruct(shape, dtype) for shape, dtype in (outs if many else [outs])]
    return pl.pallas_call(
        kernel,
        out_shape=shapes if many else shapes[0],
        in_specs=[smem if a.dtype == jnp.int32 else vmem for a in arrays],
        out_specs=[vmem] * len(outs) if many else vmem,
        scratch_shapes=list(scratch),
        compiler_params=pltpu.CompilerParams(vmem_limit_bytes=32 * 2**20),
        cost_estimate=cost,
        name=name,
    )(*arrays)


def row_shards(audio, w_start, h_start):
    f16, f32 = jnp.float16, jnp.float32
    comp = w_start.shape[0]
    swap = [(0, 1), (1, 0)]
    freq_at, core_at = lax.axis_index("freq"), lax.axis_index("core")
    q = freq_at * lax.axis_size("chips") + lax.axis_index("chips")
    at = jnp.stack([core_at * SIDE + q, core_at, freq_at]).astype(jnp.int32)
    other = lax.ppermute(w_start, "freq", swap)
    keep, give, peak = spectrum(audio, at[1:2])
    frames = keep.shape[1]
    extra = comp * comp // LANES
    taken = lax.ppermute(give, "core", swap)
    acts = lax.dynamic_slice_in_dim(h_start, freq_at * frames, frames, 1)
    message = ((SIDE, comp + extra, LANES), f32)
    lane_rows = ((comp, LANES), f32)

    def exchange(value, axes=("freq", "chips")):
        value = lax.all_to_all(value.astype(f16), axes, split_axis=0, concat_axis=0, tiled=True)
        return value.astype(f32)

    acts, mine = local(
        start_kernel,
        [(acts.shape, f32), lane_rows],
        "start",
        at,
        w_start,
        other,
        keep,
        give,
        acts,
        scratch=[pltpu.VMEM((LANES // 8 * (OUTER + 1), LANES), f32)],
        cost=pl.CostEstimate(flops=2**34, bytes_accessed=2**25, transcendentals=0),
    )
    sibling = lax.ppermute(acts, "core", swap)
    parts = local(sums_kernel, message, "sums", acts, sibling, keep, taken)
    for step in range(ITERS - 1):
        got = exchange(parts)
        mine, payload, exps = local(slice_kernel, [lane_rows] * 3, "slice", got, mine)
        got = exchange(jnp.broadcast_to(payload, (SIDE,) + payload.shape))
        half = local(partial_kernel, ((2 * comp + extra, LANES), f32), "partial", got, exps, keep, taken, peak)
        other_half = lax.ppermute(half, "core", swap)
        outs = [message, (acts.shape, f32)]
        parts, acts = local(
            again_kernel, outs, "again", half, other_half, acts, sibling, keep, taken
        )
    got = exchange(parts)
    acts, got = lax.optimization_barrier((acts, got))
    partner = lax.ppermute(acts, "freq", swap)
    final, exps = local(last_kernel, [((2, OUTER // 4, LANES), f32), lane_rows], "last", got, mine)
    final = jnp.broadcast_to(final[:, None], (2, HALF // 2) + final.shape[1:])
    got = exchange(final.reshape((HALF,) + final.shape[2:]), ("freq", "chips", "core"))
    components = local(
        natural_kernel,
        (w_start.shape, f32),
        "natural",
        got,
        exps,
        scratch=[pltpu.VMEM((OUTER // 4 * (HALF + 1), LANES), f32)] * 2,
    )
    first = freq_at == 0
    halves_of = [jnp.where(first, acts, partner), jnp.where(first, partner, acts)]
    return components, jnp.concatenate(halves_of, axis=1)


def shards(n_freq, n_tm, audio, w_start, h_start):
    n_dev = n_freq * n_tm
    comp, w_cols = w_start.shape
    bins = w_cols * n_freq
    own = bins // n_dev
    width = OUTER // n_freq
    freq_at = lax.axis_index("freq")
    me = freq_at * n_tm + lax.axis_index("tm")
    grid = jnp.concatenate(spectrum(audio, jnp.zeros((1,), jnp.int32))[:2], axis=0)
    frames = grid.shape[1]
    comps = inner_order(gather_freq(w_start, n_freq, freq_at))
    acts = lax.dynamic_slice_in_dim(h_start, freq_at * frames, frames, 1)
    per_row = LANES // own
    mine = lax.dynamic_slice(
        comps, (me // per_row, 0, me % per_row * own), (1, comp, own)
    ).reshape(comp, own)
    for step in range(ITERS):
        parts, acts = advance(comps, grid, acts)
        sums = parts[:, :comp].reshape(HALF, comp, per_row, own).transpose(0, 2, 1, 3)
        gram = jnp.broadcast_to(parts[0, comp:].reshape(1, -1), (n_dev, comp * comp))
        parts = jnp.concatenate([sums.reshape(n_dev, -1), gram], axis=1).reshape(n_dev, -1, LANES)
        got = lax.all_to_all(parts, ALL, split_axis=0, concat_axis=0, tiled=True)
        value = jnp.sum(got, axis=0)
        rows = comp * own // LANES
        mine = update(mine, value[:rows].reshape(comp, own), unpack(value[rows:]))
        every = jnp.broadcast_to(mine.reshape(1, -1, LANES), (n_dev, rows, LANES))
        comps = lax.all_to_all(every, ALL, split_axis=0, concat_axis=0, tiled=True)
        comps = comps.reshape(HALF, per_row, comp, own).transpose(0, 2, 1, 3)
        comps = comps.reshape(HALF, comp, LANES)
    cut = lax.dynamic_slice_in_dim(comps.reshape(HALF, comp, 2, OUTER), freq_at * width, width, 3)
    components = natural_order(cut.reshape(HALF, comp, 2 * width))
    activations = gather_freq(acts, n_freq, freq_at)
    return (components, activations)


def solution(mesh):
    sizes = (mesh.shape["freq"], mesh.shape["tm"])
    if sizes == (2, SIDE):
        devices = mesh.devices.reshape(2, SIDE // 2, 2)
        mesh = jax.sharding.Mesh(devices, ("freq", "chips", "core"))
        body, tm = row_shards, ("chips", "core")
    else:
        body, tm = functools.partial(shards, *sizes), "tm"
    return jax.shard_map(
        body,
        mesh=mesh,
        in_specs=(P(tm, "freq"), P(None, "freq"), P(None, tm)),
        out_specs=(P(None, "freq"), P(None, tm)),
        check_vma=False,
    )
```

```python
import functools
import math

import jax
import jax.numpy as jnp
import numpy as np
from jax import lax
from jax.experimental import pallas as pl
from jax.experimental.pallas import tpu as pltpu
from jax.sharding import PartitionSpec as P

ITERS = 2
HIGHEST = lax.Precision.HIGHEST
ALL = ("freq", "tm")
LANES = 128
OUTER = 64
HALF = OUTER // 2
FRAME = OUTER * LANES
CHUNK = 16
PAIR = 2
GROUP = 4
NT = (((1,), (1,)), ((), ()))
LEAST = 2.0**-126


def tables():
    a = np.arange(OUTER)
    i = np.arange(LANES)
    r = np.arange(HALF)
    position = a[:, None] * LANES + i[None, :]
    window = 0.5 - 0.5 * np.cos(2 * np.pi * position / FRAME)
    window = window / math.sqrt(0.375 * FRAME)
    angle = 2 * np.pi * (r[:, None] * a[None, :] % OUTER) / OUTER
    first = np.stack([np.cos(angle), -np.sin(angle)], axis=1).reshape(2 * HALF, OUTER)
    first[1] = np.cos(np.pi * a)
    turn = 2 * np.pi * r[:, None] * i[None, :] / FRAME
    turn_cos = np.cos(turn)
    turn_sin = np.sin(turn)
    m = np.arange(OUTER)
    column = np.concatenate([m, LANES - 1 - m])
    angle = 2 * np.pi * (i[:, None] * column[None, :] % LANES) / LANES
    top = np.concatenate([np.cos(angle), -np.sin(angle)], axis=1)
    bottom = np.concatenate([np.sin(angle), np.cos(angle)], axis=1)
    second = np.concatenate([top, bottom], axis=0)
    zero = np.zeros((LANES, OUTER))
    angle_a = 2 * np.pi * i[:, None] * (m * OUTER)[None, :] / FRAME
    angle_b = 2 * np.pi * i[:, None] * (m * OUTER + HALF)[None, :] / FRAME
    top = np.concatenate([np.cos(angle_a), zero, -np.sin(angle_a), zero], axis=1)
    bottom = np.concatenate([zero, np.cos(angle_b), zero, -np.sin(angle_b)], axis=1)
    edge = np.concatenate([top, bottom], axis=0)

    first = np.concatenate([first, np.zeros((OUTER, LANES - OUTER))], axis=1)
    second, edge = (np.concatenate([t[:, :LANES], t[:, LANES:]], axis=0) for t in (second, edge))
    parts = [window, first, turn_cos, turn_sin, second, edge]
    return np.concatenate(parts, axis=0).astype(np.float32)


def halves(value):
    high = value.astype(jnp.bfloat16)
    return high, (value - high.astype(jnp.float32)).astype(jnp.bfloat16)


def spectrum_kernel(core, audio, source, keep, give, peak, heard, table, stack, held, audio_sems, table_sems):
    frames = keep.shape[1]
    chunks = frames // CHUNK
    turns = 2 * OUTER

    def audio_copy(chunk):
        span = pl.ds(pl.multiple_of(chunk * CHUNK * FRAME, CHUNK * FRAME), CHUNK * FRAME)
        return pltpu.make_async_copy(audio.at[:, span], heard.at[chunk], audio_sems.at[chunk])

    def table_copy(k):
        span = pl.ds(0, turns) if k == 0 else pl.ds(turns, table.shape[0] - turns)
        return pltpu.make_async_copy(source.at[span], table.at[span], table_sems.at[k])

    table_copy(0).start()
    for chunk in range(chunks):
        audio_copy(chunk).start()
    table_copy(1).start()
    table_copy(0).wait()
    high, low = halves(table[OUTER:turns, :OUTER])
    first_terms = jnp.concatenate([high, low, high], axis=1)

    @pl.loop(0, chunks)
    def _(chunk):
        audio_copy(chunk).wait()
        samples = heard[chunk].reshape(CHUNK * OUTER, LANES).astype(jnp.float32)
        shape = table[:OUTER]
        for start in range(0, CHUNK, PAIR):
            columns = []
            for frame in range(start, start + PAIR):
                high, low = halves(samples[frame * OUTER : (frame + 1) * OUTER] * shape)
                columns.append(jnp.concatenate([high, high, low], axis=0))
            sums = jnp.dot(
                first_terms, jnp.concatenate(columns, axis=1), preferred_element_type=jnp.float32
            )
            for frame in range(start, start + PAIR):
                place = pl.ds(chunk * CHUNK + frame, OUTER, stride=frames + 1)
                held[place, :] = sums[:, (frame - start) * LANES : (frame - start + 1) * LANES]

    table_copy(1).wait()
    for k in range(2):
        at = turns + 2 * HALF + k * 4 * LANES
        both = jnp.concatenate([table[at : at + 2 * LANES], table[at + 2 * LANES : at + 4 * LANES]], axis=1)
        high, low = halves(both)
        stack[k] = jnp.concatenate([high, low, high], axis=0)

    def turned(row):
        at = row * 2 * (frames + 1)
        real = held[pl.ds(at, frames), :]
        imag = held[pl.ds(at + frames + 1, frames), :]
        cos, sin = table[pl.ds(turns + row, 1), :], table[pl.ds(turns + HALF + row, 1), :]
        high_r, low_r = halves(real * cos + imag * sin)
        high_i, low_i = halves(imag * cos - real * sin)
        return jnp.concatenate([high_r, high_i, high_r, high_i, low_r, low_i], axis=1)

    def magnitude(terms, k):
        bins = jnp.dot(terms, stack[k], preferred_element_type=jnp.float32)
        real, imag = bins[:, :LANES], bins[:, LANES:]
        square = real * real + imag * imag
        found = (square * lax.rsqrt(jnp.maximum(square, LEAST))).astype(keep.dtype)
        peak[...] = jnp.maximum(peak[...], jnp.max(found.reshape(-1, 16, LANES), axis=0))
        return found

    peak[...] = jnp.zeros_like(peak)

    def rows_of(side, out):
        for group in range(HALF // 2 // GROUP):
            start = side * (HALF // 2) + group * GROUP
            found = magnitude(jnp.concatenate([turned(start + k) for k in range(GROUP)], axis=0), 0)
            for k in range(GROUP):
                out[group * GROUP + k] = found[k * frames : (k + 1) * frames]

    rows_of(1 - core[0], give)
    rows_of(core[0], keep)
    edge = magnitude(turned(0), 1)

    @pl.when(core[0] == 0)
    def _():
        keep[0] = edge

    @pl.when(core[0] != 0)
    def _():
        give[0] = edge


def spectrum(audio, core):
    frames = audio.shape[1] // FRAME
    table = jnp.asarray(tables())
    far = pl.BlockSpec(memory_space=pltpu.HBM)
    return pl.pallas_call(
        spectrum_kernel,
        out_shape=[jax.ShapeDtypeStruct((HALF // 2, frames, LANES), jnp.bfloat16)] * 2
        + [jax.ShapeDtypeStruct((16, LANES), jnp.bfloat16)],
        in_specs=[pl.BlockSpec(memory_space=pltpu.SMEM), far, far],
        out_specs=[pl.BlockSpec(memory_space=pltpu.VMEM)] * 3,
        scratch_shapes=[
            pltpu.VMEM((frames // CHUNK, 1, CHUNK * FRAME), jnp.bfloat16),
            pltpu.VMEM(table.shape, table.dtype),
            pltpu.VMEM((2, 6 * LANES, 2 * LANES), jnp.bfloat16),
            pltpu.VMEM((OUTER * (frames + 1), LANES), jnp.float32),
            pltpu.SemaphoreType.DMA((frames // CHUNK,)),
            pltpu.SemaphoreType.DMA((2,)),
        ],
        compiler_params=pltpu.CompilerParams(vmem_limit_bytes=105 * 2**19),
        cost_estimate=pl.CostEstimate(
            flops=6 * frames * FRAME * (OUTER + 2 * LANES), bytes_accessed=2**22, transcendentals=0
        ),
        name="spectrum",
    )(core, audio, table)


def update(state, numer, gram):
    return state * numer / jnp.dot(gram, state, precision=HIGHEST, preferred_element_type=jnp.float32)


def step_kernel(comps, grid, acts, parts, acts_out):
    rows, comp, lanes = comps.shape
    wide = jnp.concatenate([comps[r] for r in range(rows)], axis=1)
    tall = jnp.concatenate([grid[r] for r in range(rows)], axis=1)
    numer = lax.dot_general(wide.astype(jnp.bfloat16), tall, NT, preferred_element_type=jnp.float32)
    gram = lax.dot_general(wide, wide, NT, precision=HIGHEST, preferred_element_type=jnp.float32)
    acts_new = update(acts[...], numer, gram)
    acts_out[...] = acts_new
    gram = lax.dot_general(acts_new, acts_new, NT, precision=HIGHEST, preferred_element_type=jnp.float32)
    per = LANES // comp
    high = comp // per
    packed = jnp.concatenate([gram[j * high : (j + 1) * high] for j in range(per)], axis=1)
    sums = jnp.dot(acts_new.astype(jnp.bfloat16), tall, preferred_element_type=jnp.float32)
    for r in range(rows):
        parts[r, :comp, :] = sums[:, r * lanes : (r + 1) * lanes]
        parts[r, comp:, :] = packed


def advance(comps, grid, acts):
    rows, comp, lanes = comps.shape
    extra = comp * comp // LANES
    return pl.pallas_call(
        step_kernel,
        out_shape=(
            jax.ShapeDtypeStruct((rows, comp + extra, lanes), jnp.float32),
            jax.ShapeDtypeStruct(acts.shape, jnp.float32),
        ),
        compiler_params=pltpu.CompilerParams(vmem_limit_bytes=32 * 2**20),
        name="advance",
    )(comps, grid, acts)


def unpack(packed):
    high = packed.shape[0]
    comp = math.isqrt(packed.size)
    return packed.reshape(high, LANES // comp, comp).transpose(1, 0, 2).reshape(comp, comp)


def inner_order(natural):
    comp = natural.shape[0]
    cube = natural.reshape(comp, -1, OUTER).transpose(2, 0, 1)
    mirrored = jnp.concatenate([cube[HALF : HALF + 1], cube[: HALF : -1]], axis=0)
    return jnp.concatenate([cube[:HALF], mirrored], axis=2)


def natural_order(inner):
    comp, width = inner.shape[1], inner.shape[2] // 2
    low, mirrored = inner[:, :, :width], inner[:, :, width:]
    cube = jnp.concatenate([low, mirrored[:1], mirrored[:0:-1]], axis=0)
    return cube.transpose(1, 2, 0).reshape(comp, -1)


def gather_freq(block, n_freq, at):
    pieces = [block]
    for shift in range(1, n_freq):
        ring = [(i, (i + shift) % n_freq) for i in range(n_freq)]
        pieces.append(lax.ppermute(block, "freq", ring))
    placed = []
    for p in range(n_freq):
        value = pieces[0]
        for shift in range(1, n_freq):
            value = jnp.where((at - shift) % n_freq == p, pieces[shift], value)
        placed.append(value)
    return jnp.concatenate(placed, axis=1)


TOP = 13
SIDE = HALF // 2


def pack(gram):
    comp = gram.shape[0]
    per = LANES // comp
    high = comp // per
    return jnp.concatenate([gram[j * high : (j + 1) * high] for j in range(per)], axis=1)


def unpacked(packed):
    comp = math.isqrt(packed.size)
    return jnp.concatenate([packed[:, j * comp : (j + 1) * comp] for j in range(LANES // comp)], axis=0)


def exponent(value):
    peak = jnp.max(jnp.abs(value), axis=(0, 1), keepdims=True)
    return jnp.floor(jnp.log2(jnp.maximum(peak, 1e-30))) - TOP


def power(exps):
    count = jnp.abs(exps).astype(jnp.int32)
    value = jnp.ones_like(exps)
    for bit in range(7):
        step = jnp.where(exps < 0, 2.0 ** -(2**bit), 2.0 ** (2**bit))
        value = value * jnp.where((count >> bit) & 1 == 1, step, 1.0)
    return value


def places(shape):
    return [lax.broadcasted_iota(jnp.int32, shape, axis) for axis in range(2)]


def mirrored_at(r):
    return OUTER - r if r else HALF


def gram_of(value):
    rows = value.shape[0]
    both = jnp.concatenate(halves(value), axis=0)
    parts = lax.dot_general(both, both, NT, preferred_element_type=jnp.float32)
    cross = parts[:rows, rows:] + parts[rows:, :rows]
    return parts[:rows, :rows] + (cross + parts[rows:, rows:])


def start_kernel(at, own, other, keep, give, acts, acts_out, mine, held):
    comp = own.shape[0]
    row, side, first = at[0], at[1], at[2] == 0
    wide = jnp.concatenate(
        [jnp.where(first, own[...], other[...]), jnp.where(first, other[...], own[...])], axis=1
    )
    quads, eighth = LANES // comp, 8
    for q in range(eighth):
        columns = [wide[:, (c * eighth + q) * LANES : (c * eighth + q + 1) * LANES] for c in range(quads)]
        turned = jnp.concatenate(columns, axis=0).T
        for m in range(2):
            place = (2 * q + m) * (OUTER + 1)
            held[place : place + OUTER, :] = turned[m * OUTER : (m + 1) * OUTER]
    gram = gram_of(wide)
    span = OUTER // quads
    block = places((span, LANES))[1] // comp

    def pair(r):
        mirror = jnp.where(r == 0, HALF, OUTER - r)
        return [held[pl.ds(j, span, stride=OUTER + 1), :] for j in (r, mirror)]

    both = jnp.concatenate(pair(row), axis=0).T
    mine[...] = jnp.concatenate(
        [
            both[c * comp : (c + 1) * comp, h * span : (h + 1) * span]
            for h in range(2)
            for c in range(quads)
        ],
        axis=1,
    )
    total = jnp.zeros((acts.shape[1], LANES), jnp.float32)
    batch = 8
    for grid, start in ((keep, side * SIDE), (give, (1 - side) * SIDE)):
        for base in range(0, SIDE, batch):
            pieces = []
            for u in range(base, base + batch):
                for value in pair(start + u):
                    pieces += [jnp.where(block == c, value, 0.0).astype(jnp.bfloat16) for c in range(quads)]
            left = jnp.concatenate([grid[u] for u in range(base, base + batch)], axis=1)
            total += jnp.dot(left, jnp.concatenate(pieces, axis=0), preferred_element_type=jnp.float32)
    total = total.T
    numer = sum(total[c * comp : (c + 1) * comp] for c in range(quads))
    acts_out[...] = update(acts[...], numer, gram)


def sealed(sums, gram, squares, bound=None):
    comp = gram.shape[0]
    sums_exp, gram_exp = exponent(sums if bound is None else bound), exponent(squares)
    packed = pack(gram) * power(-gram_exp)
    rows, lanes = places(packed.shape)
    last, end = packed.shape[0] - 1, LANES - comp
    packed = jnp.where((rows == last) & (lanes == end), sums_exp, packed)
    packed = jnp.where((rows == last) & (lanes == end + 1), gram_exp, packed)
    return sums * power(-sums_exp), packed


def opened(got, comp):
    end = LANES - comp
    scales = power(got[:, got.shape[1] - 1, :])
    sources = range(got.shape[0])
    gram = sum(got[s, comp:, :] * scales[s : s + 1, end + 1 : end + 2] for s in sources)
    gram = unpacked(gram)
    at = places(gram.shape)
    for column in range(2):
        mirrored = gram[column : column + 1, comp - 1 : comp]
        gram = jnp.where((at[0] == comp - 1) & (at[1] == column), mirrored, gram)
    return [scales[s : s + 1, end : end + 1] for s in sources], gram


def tall(grid):
    return jnp.concatenate([grid[u] for u in range(SIDE)], axis=1)


def finish(acts, grids, parts, peak=None):
    comp = acts[0].shape[0]
    left = [value.astype(jnp.bfloat16) for value in acts]
    both = jnp.concatenate([tall(grid) for grid in grids], axis=0)
    sums = jnp.dot(jnp.concatenate(left, axis=1), both, preferred_element_type=jnp.float32)
    gram, weight, squares = 0.0, 0.0, 0.0
    for value, short in zip(acts, left):
        weight += jnp.sum(short.astype(jnp.float32), axis=1, keepdims=True)
        squares += jnp.sum(value * value, axis=1, keepdims=True)
        gram += lax.dot_general(value, value, NT, precision=HIGHEST, preferred_element_type=jnp.float32)
    sums, packed = sealed(sums, gram, squares, None if peak is None else weight * (1.01 * peak))
    for u in range(SIDE):
        parts[u, :comp, :] = sums[:, u * LANES : (u + 1) * LANES]
        parts[u, comp:, :] = packed


def sums_kernel(acts, sibling, keep, taken, parts):
    finish((acts[...], sibling[...]), (keep, taken), parts)


def partial_kernel(got, exps, keep, taken, peak, out):
    comp = got.shape[1]
    wide = jnp.concatenate([got[u] for u in range(SIDE)], axis=1) * power(exps[:, :1])
    left = wide.astype(jnp.bfloat16)
    both = jnp.concatenate([tall(keep), tall(taken)], axis=0)
    numer = lax.dot_general(left, both, NT, preferred_element_type=jnp.float32)
    for k in range(2):
        out[k * comp : (k + 1) * comp, :] = numer[:, k * LANES : (k + 1) * LANES]
    packed = pack(gram_of(wide))
    rows, lanes = places(packed.shape)
    highest = jnp.max(peak[...].astype(jnp.float32), axis=(0, 1), keepdims=True)
    place = (rows == packed.shape[0] - 1) & (lanes == LANES - comp)
    out[2 * comp :, :] = jnp.where(place, highest, packed)


def again_kernel(half, other_half, acts, sibling, keep, taken, parts, acts_out):
    comp = acts.shape[0]
    mine, theirs = half[2 * comp :, :], other_half[2 * comp :, :]
    last, end = mine.shape[0] - 1, LANES - comp
    peak = jnp.maximum(mine, theirs)[last : last + 1, end : end + 1]
    gram = unpacked(mine + theirs)
    at = places(gram.shape)
    gram = jnp.where((at[0] == comp - 1) & (at[1] == 0), gram[:1, comp - 1 : comp], gram)
    new = update(acts[...], half[:comp, :] + other_half[comp : 2 * comp, :], gram)
    sibling_new = update(sibling[...], half[comp : 2 * comp, :] + other_half[:comp, :], gram)
    acts_out[...] = new
    finish((new, sibling_new), (keep, taken), parts, peak)


def eleven_bits(value):
    split = value * 8193.0
    return split - (split - value)


def rounded(value):
    def short(x):
        return x.astype(jnp.bfloat16).astype(jnp.float32)

    near = eleven_bits(value)
    step = jnp.abs(near) * 2.0**-10.6
    moved = eleven_bits(near + jnp.where(value > near, step, -step))
    return jnp.where(short(near) == short(value), near, moved)


def slice_of(got, mine):
    comp = mine.shape[0]
    scales, gram = opened(got, comp)
    sums = sum(got[s, :comp, :] * scales[s] for s in range(got.shape[0]))
    at = places(gram.shape)
    diagonal = jnp.sum(jnp.where(at[0] == at[1], gram, 0.0), axis=1, keepdims=True)
    bound = sum(scales) * 2.0 ** (TOP + 1) / jnp.maximum(diagonal, 1e-30)
    exps = jnp.clip(jnp.floor(jnp.log2(jnp.maximum(bound, 1e-30))), -100, 100) - TOP
    return update(mine[...], sums, gram), exps


def slice_kernel(got, mine, out, payload, exps_out):
    new, exps = slice_of(got, mine)
    out[...] = new
    payload[...] = rounded(new * power(-exps))
    exps_out[...] = jnp.broadcast_to(exps, exps_out.shape)


def last_kernel(got, mine, out, exps_out):
    new, exps = slice_of(got, mine)
    exps_out[...] = jnp.broadcast_to(exps, exps_out.shape)
    turned = (new * power(-exps)).T
    span = OUTER // 4
    for freq in range(2):
        starts = [h * OUTER + freq * 2 * span + half * span for h in range(2) for half in range(2)]
        out[freq] = jnp.concatenate([turned[a : a + span] for a in starts], axis=1)


def natural_kernel(got, exps, out, low, high):
    comp = out.shape[0]
    span = OUTER // 4
    for r in range(HALF):
        value = got[r % SIDE * 2 + r // SIDE]
        low[pl.ds(r, span, stride=HALF + 1), :] = value
        high[pl.ds(mirrored_at(r) % HALF, span, stride=HALF + 1), :] = pltpu.roll(value, LANES // 2, 1)
    factor = power(exps[...])
    for pair in range(span // 2):
        rows = []
        for place in (2 * pair, 2 * pair + 1):
            begin = place * (HALF + 1)
            rows += [ref[begin : begin + HALF, :] for ref in (low, high)]
        turned = jnp.concatenate(rows, axis=0).T
        for half in range(2):
            begin = (half * (span // 2) + pair) * LANES
            out[:, begin : begin + LANES] = turned[half * comp : (half + 1) * comp] * factor


def local(kernel, outs, name, *arrays, scratch=(), cost=None):
    vmem = pl.BlockSpec(memory_space=pltpu.VMEM)
    smem = pl.BlockSpec(memory_space=pltpu.SMEM)
    many = isinstance(outs, list)
    shapes = [jax.ShapeDtypeStruct(shape, dtype) for shape, dtype in (outs if many else [outs])]
    return pl.pallas_call(
        kernel,
        out_shape=shapes if many else shapes[0],
        in_specs=[smem if a.dtype == jnp.int32 else vmem for a in arrays],
        out_specs=[vmem] * len(outs) if many else vmem,
        scratch_shapes=list(scratch),
        compiler_params=pltpu.CompilerParams(vmem_limit_bytes=32 * 2**20),
        cost_estimate=cost,
        name=name,
    )(*arrays)


def row_shards(audio, w_start, h_start):
    f16, f32 = jnp.float16, jnp.float32
    comp = w_start.shape[0]
    swap = [(0, 1), (1, 0)]
    freq_at, core_at = lax.axis_index("freq"), lax.axis_index("core")
    q = freq_at * lax.axis_size("chips") + lax.axis_index("chips")
    at = jnp.stack([core_at * SIDE + q, core_at, freq_at]).astype(jnp.int32)
    other = lax.ppermute(w_start, "freq", swap)
    keep, give, peak = spectrum(audio, at[1:2])
    frames = keep.shape[1]
    extra = comp * comp // LANES
    taken = lax.ppermute(give, "core", swap)
    acts = lax.dynamic_slice_in_dim(h_start, freq_at * frames, frames, 1)
    message = ((SIDE, comp + extra, LANES), f32)
    lane_rows = ((comp, LANES), f32)

    def exchange(value, axes=("freq", "chips")):
        value = lax.all_to_all(value.astype(f16), axes, split_axis=0, concat_axis=0, tiled=True)
        return value.astype(f32)

    acts, mine = local(
        start_kernel,
        [(acts.shape, f32), lane_rows],
        "start",
        at,
        w_start,
        other,
        keep,
        give,
        acts,
        scratch=[pltpu.VMEM((LANES // 8 * (OUTER + 1), LANES), f32)],
        cost=pl.CostEstimate(flops=2**34, bytes_accessed=2**25, transcendentals=0),
    )
    sibling = lax.ppermute(acts, "core", swap)
    parts = local(sums_kernel, message, "sums", acts, sibling, keep, taken)
    for step in range(ITERS - 1):
        got = exchange(parts)
        mine, payload, exps = local(slice_kernel, [lane_rows] * 3, "slice", got, mine)
        got = exchange(jnp.broadcast_to(payload, (SIDE,) + payload.shape))
        half = local(partial_kernel, ((2 * comp + extra, LANES), f32), "partial", got, exps, keep, taken, peak)
        other_half = lax.ppermute(half, "core", swap)
        outs = [message, (acts.shape, f32)]
        parts, acts = local(
            again_kernel, outs, "again", half, other_half, acts, sibling, keep, taken
        )
    got = exchange(parts)
    final, exps = local(last_kernel, [((2, OUTER // 4, LANES), f32), lane_rows], "last", got, mine)
    final = jnp.broadcast_to(final[:, None], (2, HALF // 2) + final.shape[1:])
    final = final.reshape((HALF,) + final.shape[2:]).astype(f16)
    acts, final = lax.optimization_barrier((acts, final))
    partner = lax.ppermute(acts, "freq", swap)
    got = exchange(final, ("freq", "chips", "core"))
    components = local(
        natural_kernel,
        (w_start.shape, f32),
        "natural",
        got,
        exps,
        scratch=[pltpu.VMEM((OUTER // 4 * (HALF + 1), LANES), f32)] * 2,
    )
    first = freq_at == 0
    halves_of = [jnp.where(first, acts, partner), jnp.where(first, partner, acts)]
    return components, jnp.concatenate(halves_of, axis=1)


def shards(n_freq, n_tm, audio, w_start, h_start):
    n_dev = n_freq * n_tm
    comp, w_cols = w_start.shape
    bins = w_cols * n_freq
    own = bins // n_dev
    width = OUTER // n_freq
    freq_at = lax.axis_index("freq")
    me = freq_at * n_tm + lax.axis_index("tm")
    grid = jnp.concatenate(spectrum(audio, jnp.zeros((1,), jnp.int32))[:2], axis=0)
    frames = grid.shape[1]
    comps = inner_order(gather_freq(w_start, n_freq, freq_at))
    acts = lax.dynamic_slice_in_dim(h_start, freq_at * frames, frames, 1)
    per_row = LANES // own
    mine = lax.dynamic_slice(
        comps, (me // per_row, 0, me % per_row * own), (1, comp, own)
    ).reshape(comp, own)
    for step in range(ITERS):
        parts, acts = advance(comps, grid, acts)
        sums = parts[:, :comp].reshape(HALF, comp, per_row, own).transpose(0, 2, 1, 3)
        gram = jnp.broadcast_to(parts[0, comp:].reshape(1, -1), (n_dev, comp * comp))
        parts = jnp.concatenate([sums.reshape(n_dev, -1), gram], axis=1).reshape(n_dev, -1, LANES)
        got = lax.all_to_all(parts, ALL, split_axis=0, concat_axis=0, tiled=True)
        value = jnp.sum(got, axis=0)
        rows = comp * own // LANES
        mine = update(mine, value[:rows].reshape(comp, own), unpack(value[rows:]))
        every = jnp.broadcast_to(mine.reshape(1, -1, LANES), (n_dev, rows, LANES))
        comps = lax.all_to_all(every, ALL, split_axis=0, concat_axis=0, tiled=True)
        comps = comps.reshape(HALF, per_row, comp, own).transpose(0, 2, 1, 3)
        comps = comps.reshape(HALF, comp, LANES)
    cut = lax.dynamic_slice_in_dim(comps.reshape(HALF, comp, 2, OUTER), freq_at * width, width, 3)
    components = natural_order(cut.reshape(HALF, comp, 2 * width))
    activations = gather_freq(acts, n_freq, freq_at)
    return (components, activations)


def solution(mesh):
    sizes = (mesh.shape["freq"], mesh.shape["tm"])
    if sizes == (2, SIDE):
        devices = mesh.devices.reshape(2, SIDE // 2, 2)
        mesh = jax.sharding.Mesh(devices, ("freq", "chips", "core"))
        body, tm = row_shards, ("chips", "core")
    else:
        body, tm = functools.partial(shards, *sizes), "tm"
    return jax.shard_map(
        body,
        mesh=mesh,
        in_specs=(P(tm, "freq"), P(None, "freq"), P(None, tm)),
        out_specs=(P(None, "freq"), P(None, tm)),
        check_vma=False,
    )
```

```python
import functools
import math

import jax
import jax.numpy as jnp
import numpy as np
from jax import lax
from jax.experimental import pallas as pl
from jax.experimental.pallas import tpu as pltpu
from jax.sharding import PartitionSpec as P

ITERS = 2
HIGHEST = lax.Precision.HIGHEST
ALL = ("freq", "tm")
LANES = 128
OUTER = 64
HALF = OUTER // 2
FRAME = OUTER * LANES
CHUNK = 16
PAIR = 2
GROUP = 4
NT = (((1,), (1,)), ((), ()))
LEAST = 2.0**-126


def tables():
    a = np.arange(OUTER)
    i = np.arange(LANES)
    r = np.arange(HALF)
    position = a[:, None] * LANES + i[None, :]
    window = 0.5 - 0.5 * np.cos(2 * np.pi * position / FRAME)
    window = window / math.sqrt(0.375 * FRAME)
    angle = 2 * np.pi * (r[:, None] * a[None, :] % OUTER) / OUTER
    first = np.stack([np.cos(angle), -np.sin(angle)], axis=1).reshape(2 * HALF, OUTER)
    first[1] = np.cos(np.pi * a)
    turn = 2 * np.pi * r[:, None] * i[None, :] / FRAME
    turn_cos = np.cos(turn)
    turn_sin = np.sin(turn)
    m = np.arange(OUTER)
    column = np.concatenate([m, LANES - 1 - m])
    angle = 2 * np.pi * (i[:, None] * column[None, :] % LANES) / LANES
    top = np.concatenate([np.cos(angle), -np.sin(angle)], axis=1)
    bottom = np.concatenate([np.sin(angle), np.cos(angle)], axis=1)
    second = np.concatenate([top, bottom], axis=0)
    zero = np.zeros((LANES, OUTER))
    angle_a = 2 * np.pi * i[:, None] * (m * OUTER)[None, :] / FRAME
    angle_b = 2 * np.pi * i[:, None] * (m * OUTER + HALF)[None, :] / FRAME
    top = np.concatenate([np.cos(angle_a), zero, -np.sin(angle_a), zero], axis=1)
    bottom = np.concatenate([zero, np.cos(angle_b), zero, -np.sin(angle_b)], axis=1)
    edge = np.concatenate([top, bottom], axis=0)

    first = np.concatenate([first, np.zeros((OUTER, LANES - OUTER))], axis=1)
    second, edge = (np.concatenate([t[:, :LANES], t[:, LANES:]], axis=0) for t in (second, edge))
    parts = [window, first, turn_cos, turn_sin, second, edge]
    return np.concatenate(parts, axis=0).astype(np.float32)


def halves(value):
    high = value.astype(jnp.bfloat16)
    return high, (value - high.astype(jnp.float32)).astype(jnp.bfloat16)


def spectrum_kernel(core, audio, source, keep, give, peak, heard, table, stack, held, audio_sems, table_sems):
    frames = keep.shape[1]
    chunks = frames // CHUNK
    turns = 2 * OUTER

    def audio_copy(chunk):
        span = pl.ds(pl.multiple_of(chunk * CHUNK * FRAME, CHUNK * FRAME), CHUNK * FRAME)
        return pltpu.make_async_copy(audio.at[:, span], heard.at[chunk], audio_sems.at[chunk])

    def table_copy(k):
        span = pl.ds(0, turns) if k == 0 else pl.ds(turns, table.shape[0] - turns)
        return pltpu.make_async_copy(source.at[span], table.at[span], table_sems.at[k])

    table_copy(0).start()
    for chunk in range(chunks):
        audio_copy(chunk).start()
    table_copy(1).start()
    table_copy(0).wait()
    high, low = halves(table[OUTER:turns, :OUTER])
    first_terms = jnp.concatenate([high, low, high], axis=1)

    @pl.loop(0, chunks)
    def _(chunk):
        audio_copy(chunk).wait()
        samples = heard[chunk].reshape(CHUNK * OUTER, LANES).astype(jnp.float32)
        shape = table[:OUTER]
        for start in range(0, CHUNK, PAIR):
            columns = []
            for frame in range(start, start + PAIR):
                high, low = halves(samples[frame * OUTER : (frame + 1) * OUTER] * shape)
                columns.append(jnp.concatenate([high, high, low], axis=0))
            sums = jnp.dot(
                first_terms, jnp.concatenate(columns, axis=1), preferred_element_type=jnp.float32
            )
            for frame in range(start, start + PAIR):
                place = pl.ds(chunk * CHUNK + frame, OUTER, stride=frames + 1)
                held[place, :] = sums[:, (frame - start) * LANES : (frame - start + 1) * LANES]

    table_copy(1).wait()
    for k in range(2):
        at = turns + 2 * HALF + k * 4 * LANES
        both = jnp.concatenate([table[at : at + 2 * LANES], table[at + 2 * LANES : at + 4 * LANES]], axis=1)
        high, low = halves(both)
        stack[k] = jnp.concatenate([high, low, high], axis=0)

    def turned(row):
        at = row * 2 * (frames + 1)
        real = held[pl.ds(at, frames), :]
        imag = held[pl.ds(at + frames + 1, frames), :]
        cos, sin = table[pl.ds(turns + row, 1), :], table[pl.ds(turns + HALF + row, 1), :]
        high_r, low_r = halves(real * cos + imag * sin)
        high_i, low_i = halves(imag * cos - real * sin)
        return jnp.concatenate([high_r, high_i, high_r, high_i, low_r, low_i], axis=1)

    def magnitude(terms, k):
        bins = jnp.dot(terms, stack[k], preferred_element_type=jnp.float32)
        real, imag = bins[:, :LANES], bins[:, LANES:]
        square = real * real + imag * imag
        found = (square * lax.rsqrt(jnp.maximum(square, LEAST))).astype(keep.dtype)
        peak[...] = jnp.maximum(peak[...], jnp.max(found.reshape(-1, 16, LANES), axis=0))
        return found

    peak[...] = jnp.zeros_like(peak)

    def rows_of(side, out):
        for group in range(HALF // 2 // GROUP):
            start = side * (HALF // 2) + group * GROUP
            found = magnitude(jnp.concatenate([turned(start + k) for k in range(GROUP)], axis=0), 0)
            for k in range(GROUP):
                out[group * GROUP + k] = found[k * frames : (k + 1) * frames]

    rows_of(1 - core[0], give)
    rows_of(core[0], keep)
    edge = magnitude(turned(0), 1)

    @pl.when(core[0] == 0)
    def _():
        keep[0] = edge

    @pl.when(core[0] != 0)
    def _():
        give[0] = edge


def spectrum(audio, core):
    frames = audio.shape[1] // FRAME
    table = jnp.asarray(tables())
    far = pl.BlockSpec(memory_space=pltpu.HBM)
    return pl.pallas_call(
        spectrum_kernel,
        out_shape=[jax.ShapeDtypeStruct((HALF // 2, frames, LANES), jnp.bfloat16)] * 2
        + [jax.ShapeDtypeStruct((16, LANES), jnp.bfloat16)],
        in_specs=[pl.BlockSpec(memory_space=pltpu.SMEM), far, far],
        out_specs=[pl.BlockSpec(memory_space=pltpu.VMEM)] * 3,
        scratch_shapes=[
            pltpu.VMEM((frames // CHUNK, 1, CHUNK * FRAME), jnp.bfloat16),
            pltpu.VMEM(table.shape, table.dtype),
            pltpu.VMEM((2, 6 * LANES, 2 * LANES), jnp.bfloat16),
            pltpu.VMEM((OUTER * (frames + 1), LANES), jnp.float32),
            pltpu.SemaphoreType.DMA((frames // CHUNK,)),
            pltpu.SemaphoreType.DMA((2,)),
        ],
        compiler_params=pltpu.CompilerParams(vmem_limit_bytes=105 * 2**19),
        cost_estimate=pl.CostEstimate(
            flops=6 * frames * FRAME * (OUTER + 2 * LANES), bytes_accessed=2**22, transcendentals=0
        ),
        name="spectrum",
    )(core, audio, table)


def update(state, numer, gram):
    return state * numer / jnp.dot(gram, state, precision=HIGHEST, preferred_element_type=jnp.float32)


def step_kernel(comps, grid, acts, parts, acts_out):
    rows, comp, lanes = comps.shape
    wide = jnp.concatenate([comps[r] for r in range(rows)], axis=1)
    tall = jnp.concatenate([grid[r] for r in range(rows)], axis=1)
    numer = lax.dot_general(wide.astype(jnp.bfloat16), tall, NT, preferred_element_type=jnp.float32)
    gram = lax.dot_general(wide, wide, NT, precision=HIGHEST, preferred_element_type=jnp.float32)
    acts_new = update(acts[...], numer, gram)
    acts_out[...] = acts_new
    gram = lax.dot_general(acts_new, acts_new, NT, precision=HIGHEST, preferred_element_type=jnp.float32)
    per = LANES // comp
    high = comp // per
    packed = jnp.concatenate([gram[j * high : (j + 1) * high] for j in range(per)], axis=1)
    sums = jnp.dot(acts_new.astype(jnp.bfloat16), tall, preferred_element_type=jnp.float32)
    for r in range(rows):
        parts[r, :comp, :] = sums[:, r * lanes : (r + 1) * lanes]
        parts[r, comp:, :] = packed


def advance(comps, grid, acts):
    rows, comp, lanes = comps.shape
    extra = comp * comp // LANES
    return pl.pallas_call(
        step_kernel,
        out_shape=(
            jax.ShapeDtypeStruct((rows, comp + extra, lanes), jnp.float32),
            jax.ShapeDtypeStruct(acts.shape, jnp.float32),
        ),
        compiler_params=pltpu.CompilerParams(vmem_limit_bytes=32 * 2**20),
        name="advance",
    )(comps, grid, acts)


def unpack(packed):
    high = packed.shape[0]
    comp = math.isqrt(packed.size)
    return packed.reshape(high, LANES // comp, comp).transpose(1, 0, 2).reshape(comp, comp)


def inner_order(natural):
    comp = natural.shape[0]
    cube = natural.reshape(comp, -1, OUTER).transpose(2, 0, 1)
    mirrored = jnp.concatenate([cube[HALF : HALF + 1], cube[: HALF : -1]], axis=0)
    return jnp.concatenate([cube[:HALF], mirrored], axis=2)


def natural_order(inner):
    comp, width = inner.shape[1], inner.shape[2] // 2
    low, mirrored = inner[:, :, :width], inner[:, :, width:]
    cube = jnp.concatenate([low, mirrored[:1], mirrored[:0:-1]], axis=0)
    return cube.transpose(1, 2, 0).reshape(comp, -1)


def gather_freq(block, n_freq, at):
    pieces = [block]
    for shift in range(1, n_freq):
        ring = [(i, (i + shift) % n_freq) for i in range(n_freq)]
        pieces.append(lax.ppermute(block, "freq", ring))
    placed = []
    for p in range(n_freq):
        value = pieces[0]
        for shift in range(1, n_freq):
            value = jnp.where((at - shift) % n_freq == p, pieces[shift], value)
        placed.append(value)
    return jnp.concatenate(placed, axis=1)


TOP = 13
SIDE = HALF // 2


def pack(gram):
    comp = gram.shape[0]
    per = LANES // comp
    high = comp // per
    return jnp.concatenate([gram[j * high : (j + 1) * high] for j in range(per)], axis=1)


def unpacked(packed):
    comp = math.isqrt(packed.size)
    return jnp.concatenate([packed[:, j * comp : (j + 1) * comp] for j in range(LANES // comp)], axis=0)


def exponent(value):
    peak = jnp.max(jnp.abs(value), axis=(0, 1), keepdims=True)
    return jnp.floor(jnp.log2(jnp.maximum(peak, 1e-30))) - TOP


def power(exps):
    count = jnp.abs(exps).astype(jnp.int32)
    value = jnp.ones_like(exps)
    for bit in range(7):
        step = jnp.where(exps < 0, 2.0 ** -(2**bit), 2.0 ** (2**bit))
        value = value * jnp.where((count >> bit) & 1 == 1, step, 1.0)
    return value


def places(shape):
    return [lax.broadcasted_iota(jnp.int32, shape, axis) for axis in range(2)]


def mirrored_at(r):
    return OUTER - r if r else HALF


def gram_of(value):
    rows = value.shape[0]
    both = jnp.concatenate(halves(value), axis=0)
    parts = lax.dot_general(both, both, NT, preferred_element_type=jnp.float32)
    cross = parts[:rows, rows:] + parts[rows:, :rows]
    return parts[:rows, :rows] + (cross + parts[rows:, rows:])


def start_kernel(at, own, other, keep, give, acts, acts_out, mine, held):
    comp = own.shape[0]
    row, side, first = at[0], at[1], at[2] == 0
    wide = jnp.concatenate(
        [jnp.where(first, own[...], other[...]), jnp.where(first, other[...], own[...])], axis=1
    )
    quads, eighth = LANES // comp, 8
    for q in range(eighth):
        columns = [wide[:, (c * eighth + q) * LANES : (c * eighth + q + 1) * LANES] for c in range(quads)]
        turned = jnp.concatenate(columns, axis=0).T
        for m in range(2):
            place = (2 * q + m) * (OUTER + 1)
            held[place : place + OUTER, :] = turned[m * OUTER : (m + 1) * OUTER]
    gram = gram_of(wide)
    span = OUTER // quads
    block = places((span, LANES))[1] // comp

    def pair(r):
        mirror = jnp.where(r == 0, HALF, OUTER - r)
        return [held[pl.ds(j, span, stride=OUTER + 1), :] for j in (r, mirror)]

    both = jnp.concatenate(pair(row), axis=0).T
    mine[...] = jnp.concatenate(
        [
            both[c * comp : (c + 1) * comp, h * span : (h + 1) * span]
            for h in range(2)
            for c in range(quads)
        ],
        axis=1,
    )
    total = jnp.zeros((acts.shape[1], LANES), jnp.float32)
    batch = SIDE
    for grid, start in ((keep, side * SIDE), (give, (1 - side) * SIDE)):
        for base in range(0, SIDE, batch):
            pieces = []
            for u in range(base, base + batch):
                for value in pair(start + u):
                    pieces += [jnp.where(block == c, value, 0.0).astype(jnp.bfloat16) for c in range(quads)]
            left = jnp.concatenate([grid[u] for u in range(base, base + batch)], axis=1)
            total += jnp.dot(left, jnp.concatenate(pieces, axis=0), preferred_element_type=jnp.float32)
    total = total.T
    numer = sum(total[c * comp : (c + 1) * comp] for c in range(quads))
    acts_out[...] = update(acts[...], numer, gram)


def sealed(sums, gram, squares, bound=None):
    comp = gram.shape[0]
    sums_exp, gram_exp = exponent(sums if bound is None else bound), exponent(squares)
    packed = pack(gram) * power(-gram_exp)
    rows, lanes = places(packed.shape)
    last, end = packed.shape[0] - 1, LANES - comp
    packed = jnp.where((rows == last) & (lanes == end), sums_exp, packed)
    packed = jnp.where((rows == last) & (lanes == end + 1), gram_exp, packed)
    return sums * power(-sums_exp), packed


def opened(got, comp):
    end = LANES - comp
    scales = power(got[:, got.shape[1] - 1, :])
    sources = range(got.shape[0])
    gram = sum(got[s, comp:, :] * scales[s : s + 1, end + 1 : end + 2] for s in sources)
    gram = unpacked(gram)
    at = places(gram.shape)
    for column in range(2):
        mirrored = gram[column : column + 1, comp - 1 : comp]
        gram = jnp.where((at[0] == comp - 1) & (at[1] == column), mirrored, gram)
    return [scales[s : s + 1, end : end + 1] for s in sources], gram


def tall(grid):
    return jnp.concatenate([grid[u] for u in range(SIDE)], axis=1)


def finish(acts, grids, parts, peak=None):
    comp = acts[0].shape[0]
    left = [value.astype(jnp.bfloat16) for value in acts]
    both = jnp.concatenate([tall(grid) for grid in grids], axis=0)
    sums = jnp.dot(jnp.concatenate(left, axis=1), both, preferred_element_type=jnp.float32)
    gram, weight, squares = 0.0, 0.0, 0.0
    for value, short in zip(acts, left):
        weight += jnp.sum(short.astype(jnp.float32), axis=1, keepdims=True)
        squares += jnp.sum(value * value, axis=1, keepdims=True)
        gram += lax.dot_general(value, value, NT, precision=HIGHEST, preferred_element_type=jnp.float32)
    sums, packed = sealed(sums, gram, squares, None if peak is None else weight * (1.01 * peak))
    for u in range(SIDE):
        parts[u, :comp, :] = sums[:, u * LANES : (u + 1) * LANES]
        parts[u, comp:, :] = packed


def sums_kernel(acts, sibling, keep, taken, parts):
    finish((acts[...], sibling[...]), (keep, taken), parts)


def partial_kernel(got, exps, keep, taken, peak, out):
    comp = got.shape[1]
    wide = jnp.concatenate([got[u] for u in range(SIDE)], axis=1) * power(exps[:, :1])
    left = wide.astype(jnp.bfloat16)
    both = jnp.concatenate([tall(keep), tall(taken)], axis=0)
    numer = lax.dot_general(left, both, NT, preferred_element_type=jnp.float32)
    for k in range(2):
        out[k * comp : (k + 1) * comp, :] = numer[:, k * LANES : (k + 1) * LANES]
    packed = pack(gram_of(wide))
    rows, lanes = places(packed.shape)
    highest = jnp.max(peak[...].astype(jnp.float32), axis=(0, 1), keepdims=True)
    place = (rows == packed.shape[0] - 1) & (lanes == LANES - comp)
    out[2 * comp :, :] = jnp.where(place, highest, packed)


def again_kernel(half, other_half, acts, sibling, keep, taken, parts, acts_out):
    comp = acts.shape[0]
    mine, theirs = half[2 * comp :, :], other_half[2 * comp :, :]
    last, end = mine.shape[0] - 1, LANES - comp
    peak = jnp.maximum(mine, theirs)[last : last + 1, end : end + 1]
    gram = unpacked(mine + theirs)
    at = places(gram.shape)
    gram = jnp.where((at[0] == comp - 1) & (at[1] == 0), gram[:1, comp - 1 : comp], gram)
    new = update(acts[...], half[:comp, :] + other_half[comp : 2 * comp, :], gram)
    sibling_new = update(sibling[...], half[comp : 2 * comp, :] + other_half[:comp, :], gram)
    acts_out[...] = new
    finish((new, sibling_new), (keep, taken), parts, peak)


def eleven_bits(value):
    split = value * 8193.0
    return split - (split - value)


def rounded(value):
    def short(x):
        return x.astype(jnp.bfloat16).astype(jnp.float32)

    near = eleven_bits(value)
    step = jnp.abs(near) * 2.0**-10.6
    moved = eleven_bits(near + jnp.where(value > near, step, -step))
    return jnp.where(short(near) == short(value), near, moved)


def slice_of(got, mine):
    comp = mine.shape[0]
    scales, gram = opened(got, comp)
    sums = sum(got[s, :comp, :] * scales[s] for s in range(got.shape[0]))
    at = places(gram.shape)
    diagonal = jnp.sum(jnp.where(at[0] == at[1], gram, 0.0), axis=1, keepdims=True)
    bound = sum(scales) * 2.0 ** (TOP + 1) / jnp.maximum(diagonal, 1e-30)
    exps = jnp.clip(jnp.floor(jnp.log2(jnp.maximum(bound, 1e-30))), -100, 100) - TOP
    return update(mine[...], sums, gram), exps


def slice_kernel(got, mine, out, payload, exps_out):
    new, exps = slice_of(got, mine)
    out[...] = new
    payload[...] = rounded(new * power(-exps))
    exps_out[...] = jnp.broadcast_to(exps, exps_out.shape)


def last_kernel(got, mine, out, exps_out):
    new, exps = slice_of(got, mine)
    exps_out[...] = jnp.broadcast_to(exps, exps_out.shape)
    turned = (new * power(-exps)).T
    span = OUTER // 4
    for freq in range(2):
        starts = [h * OUTER + freq * 2 * span + half * span for h in range(2) for half in range(2)]
        out[freq] = jnp.concatenate([turned[a : a + span] for a in starts], axis=1)


def natural_kernel(at, got, exps, acts, partner, out, acts_out, low, high):
    comp = out.shape[0]
    span = OUTER // 4
    for r in range(HALF):
        value = got[r % SIDE * 2 + r // SIDE]
        low[pl.ds(r, span, stride=HALF + 1), :] = value
        high[pl.ds(mirrored_at(r) % HALF, span, stride=HALF + 1), :] = pltpu.roll(value, LANES // 2, 1)
    factor = power(exps[...])
    for pair in range(span // 2):
        rows = []
        for place in (2 * pair, 2 * pair + 1):
            begin = place * (HALF + 1)
            rows += [ref[begin : begin + HALF, :] for ref in (low, high)]
        turned = jnp.concatenate(rows, axis=0).T
        for half in range(2):
            begin = (half * (span // 2) + pair) * LANES
            out[:, begin : begin + LANES] = turned[half * comp : (half + 1) * comp] * factor
    first, own, other = at[2] == 0, acts[...], partner[...]
    acts_out[...] = jnp.concatenate([jnp.where(first, own, other), jnp.where(first, other, own)], axis=1)


def local(kernel, outs, name, *arrays, scratch=(), cost=None):
    vmem = pl.BlockSpec(memory_space=pltpu.VMEM)
    smem = pl.BlockSpec(memory_space=pltpu.SMEM)
    many = isinstance(outs, list)
    shapes = [jax.ShapeDtypeStruct(shape, dtype) for shape, dtype in (outs if many else [outs])]
    return pl.pallas_call(
        kernel,
        out_shape=shapes if many else shapes[0],
        in_specs=[smem if a.dtype == jnp.int32 else vmem for a in arrays],
        out_specs=[vmem] * len(outs) if many else vmem,
        scratch_shapes=list(scratch),
        compiler_params=pltpu.CompilerParams(vmem_limit_bytes=32 * 2**20),
        cost_estimate=cost,
        name=name,
    )(*arrays)


def row_shards(audio, w_start, h_start):
    f16, f32 = jnp.float16, jnp.float32
    comp = w_start.shape[0]
    swap = [(0, 1), (1, 0)]
    freq_at, core_at = lax.axis_index("freq"), lax.axis_index("core")
    q = freq_at * lax.axis_size("chips") + lax.axis_index("chips")
    at = jnp.stack([core_at * SIDE + q, core_at, freq_at]).astype(jnp.int32)
    other = lax.ppermute(w_start, "freq", swap)
    keep, give, peak = spectrum(audio, at[1:2])
    frames = keep.shape[1]
    extra = comp * comp // LANES
    taken = lax.ppermute(give, "core", swap)
    acts = lax.dynamic_slice_in_dim(h_start, freq_at * frames, frames, 1)
    message = ((SIDE, comp + extra, LANES), f32)
    lane_rows = ((comp, LANES), f32)

    def exchange(value, axes=("freq", "chips")):
        value = lax.all_to_all(value.astype(f16), axes, split_axis=0, concat_axis=0, tiled=True)
        return value.astype(f32)

    acts, mine = local(
        start_kernel,
        [(acts.shape, f32), lane_rows],
        "start",
        at,
        w_start,
        other,
        keep,
        give,
        acts,
        scratch=[pltpu.VMEM((LANES // 8 * (OUTER + 1), LANES), f32)],
        cost=pl.CostEstimate(flops=2**34, bytes_accessed=2**25, transcendentals=0),
    )
    sibling = lax.ppermute(acts, "core", swap)
    parts = local(sums_kernel, message, "sums", acts, sibling, keep, taken)
    for step in range(ITERS - 1):
        got = exchange(parts)
        mine, payload, exps = local(slice_kernel, [lane_rows] * 3, "slice", got, mine)
        got = exchange(jnp.broadcast_to(payload, (SIDE,) + payload.shape))
        half = local(partial_kernel, ((2 * comp + extra, LANES), f32), "partial", got, exps, keep, taken, peak)
        other_half = lax.ppermute(half, "core", swap)
        outs = [message, (acts.shape, f32)]
        parts, acts = local(
            again_kernel, outs, "again", half, other_half, acts, sibling, keep, taken
        )
    got = exchange(parts)
    acts, got = lax.optimization_barrier((acts, got))
    partner = lax.ppermute(acts, "freq", swap)
    final, exps = local(last_kernel, [((2, OUTER // 4, LANES), f32), lane_rows], "last", got, mine)
    final = jnp.broadcast_to(final[:, None], (2, HALF // 2) + final.shape[1:])
    got = exchange(final.reshape((HALF,) + final.shape[2:]), ("freq", "chips", "core"))
    return local(
        natural_kernel,
        [(w_start.shape, f32), (h_start.shape, f32)],
        "natural",
        at,
        got,
        exps,
        acts,
        partner,
        scratch=[pltpu.VMEM((OUTER // 4 * (HALF + 1), LANES), f32)] * 2,
    )


def shards(n_freq, n_tm, audio, w_start, h_start):
    n_dev = n_freq * n_tm
    comp, w_cols = w_start.shape
    bins = w_cols * n_freq
    own = bins // n_dev
    width = OUTER // n_freq
    freq_at = lax.axis_index("freq")
    me = freq_at * n_tm + lax.axis_index("tm")
    grid = jnp.concatenate(spectrum(audio, jnp.zeros((1,), jnp.int32))[:2], axis=0)
    frames = grid.shape[1]
    comps = inner_order(gather_freq(w_start, n_freq, freq_at))
    acts = lax.dynamic_slice_in_dim(h_start, freq_at * frames, frames, 1)
    per_row = LANES // own
    mine = lax.dynamic_slice(
        comps, (me // per_row, 0, me % per_row * own), (1, comp, own)
    ).reshape(comp, own)
    for step in range(ITERS):
        parts, acts = advance(comps, grid, acts)
        sums = parts[:, :comp].reshape(HALF, comp, per_row, own).transpose(0, 2, 1, 3)
        gram = jnp.broadcast_to(parts[0, comp:].reshape(1, -1), (n_dev, comp * comp))
        parts = jnp.concatenate([sums.reshape(n_dev, -1), gram], axis=1).reshape(n_dev, -1, LANES)
        got = lax.all_to_all(parts, ALL, split_axis=0, concat_axis=0, tiled=True)
        value = jnp.sum(got, axis=0)
        rows = comp * own // LANES
        mine = update(mine, value[:rows].reshape(comp, own), unpack(value[rows:]))
        every = jnp.broadcast_to(mine.reshape(1, -1, LANES), (n_dev, rows, LANES))
        comps = lax.all_to_all(every, ALL, split_axis=0, concat_axis=0, tiled=True)
        comps = comps.reshape(HALF, per_row, comp, own).transpose(0, 2, 1, 3)
        comps = comps.reshape(HALF, comp, LANES)
    cut = lax.dynamic_slice_in_dim(comps.reshape(HALF, comp, 2, OUTER), freq_at * width, width, 3)
    components = natural_order(cut.reshape(HALF, comp, 2 * width))
    activations = gather_freq(acts, n_freq, freq_at)
    return (components, activations)


def solution(mesh):
    sizes = (mesh.shape["freq"], mesh.shape["tm"])
    if sizes == (2, SIDE):
        devices = mesh.devices.reshape(2, SIDE // 2, 2)
        mesh = jax.sharding.Mesh(devices, ("freq", "chips", "core"))
        body, tm = row_shards, ("chips", "core")
    else:
        body, tm = functools.partial(shards, *sizes), "tm"
    return jax.shard_map(
        body,
        mesh=mesh,
        in_specs=(P(tm, "freq"), P(None, "freq"), P(None, tm)),
        out_specs=(P(None, "freq"), P(None, tm)),
        check_vma=False,
    )
```

```python
import functools
import math

import jax
import jax.numpy as jnp
import numpy as np
from jax import lax
from jax.experimental import pallas as pl
from jax.experimental.pallas import tpu as pltpu
from jax.sharding import PartitionSpec as P

ITERS = 2
HIGHEST = lax.Precision.HIGHEST
ALL = ("freq", "tm")
LANES = 128
OUTER = 64
HALF = OUTER // 2
FRAME = OUTER * LANES
CHUNK = 16
PAIR = 2
GROUP = 4
NT = (((1,), (1,)), ((), ()))
LEAST = 2.0**-126


def tables():
    a = np.arange(OUTER)
    i = np.arange(LANES)
    r = np.arange(HALF)
    position = a[:, None] * LANES + i[None, :]
    window = 0.5 - 0.5 * np.cos(2 * np.pi * position / FRAME)
    window = window / math.sqrt(0.375 * FRAME)
    angle = 2 * np.pi * (r[:, None] * a[None, :] % OUTER) / OUTER
    first = np.stack([np.cos(angle), -np.sin(angle)], axis=1).reshape(2 * HALF, OUTER)
    first[1] = np.cos(np.pi * a)
    turn = 2 * np.pi * r[:, None] * i[None, :] / FRAME
    turn_cos = np.cos(turn)
    turn_sin = np.sin(turn)
    m = np.arange(OUTER)
    column = np.concatenate([m, LANES - 1 - m])
    angle = 2 * np.pi * (i[:, None] * column[None, :] % LANES) / LANES
    top = np.concatenate([np.cos(angle), -np.sin(angle)], axis=1)
    bottom = np.concatenate([np.sin(angle), np.cos(angle)], axis=1)
    second = np.concatenate([top, bottom], axis=0)
    zero = np.zeros((LANES, OUTER))
    angle_a = 2 * np.pi * i[:, None] * (m * OUTER)[None, :] / FRAME
    angle_b = 2 * np.pi * i[:, None] * (m * OUTER + HALF)[None, :] / FRAME
    top = np.concatenate([np.cos(angle_a), zero, -np.sin(angle_a), zero], axis=1)
    bottom = np.concatenate([zero, np.cos(angle_b), zero, -np.sin(angle_b)], axis=1)
    edge = np.concatenate([top, bottom], axis=0)

    first = np.concatenate([first, np.zeros((OUTER, LANES - OUTER))], axis=1)
    second, edge = (np.concatenate([t[:, :LANES], t[:, LANES:]], axis=0) for t in (second, edge))
    parts = [window, first, turn_cos, turn_sin, second, edge]
    return np.concatenate(parts, axis=0).astype(np.float32)


def halves(value):
    high = value.astype(jnp.bfloat16)
    return high, (value - high.astype(jnp.float32)).astype(jnp.bfloat16)


def spectrum_kernel(core, audio, source, keep, give, peak, heard, table, stack, held, audio_sems, table_sems):
    frames = keep.shape[1]
    chunks = frames // CHUNK
    turns = 2 * OUTER

    def audio_copy(chunk):
        span = pl.ds(pl.multiple_of(chunk * CHUNK * FRAME, CHUNK * FRAME), CHUNK * FRAME)
        return pltpu.make_async_copy(audio.at[:, span], heard.at[chunk], audio_sems.at[chunk])

    def table_copy(k):
        span = pl.ds(0, turns) if k == 0 else pl.ds(turns, table.shape[0] - turns)
        return pltpu.make_async_copy(source.at[span], table.at[span], table_sems.at[k])

    table_copy(0).start()
    for chunk in range(chunks):
        audio_copy(chunk).start()
    table_copy(1).start()
    table_copy(0).wait()
    high, low = halves(table[OUTER:turns, :OUTER])
    first_terms = jnp.concatenate([high, low, high], axis=1)

    @pl.loop(0, chunks)
    def _(chunk):
        audio_copy(chunk).wait()
        samples = heard[chunk].reshape(CHUNK * OUTER, LANES).astype(jnp.float32)
        shape = table[:OUTER]
        for start in range(0, CHUNK, PAIR):
            columns = []
            for frame in range(start, start + PAIR):
                high, low = halves(samples[frame * OUTER : (frame + 1) * OUTER] * shape)
                columns.append(jnp.concatenate([high, high, low], axis=0))
            sums = jnp.dot(
                first_terms, jnp.concatenate(columns, axis=1), preferred_element_type=jnp.float32
            )
            for frame in range(start, start + PAIR):
                place = pl.ds(chunk * CHUNK + frame, OUTER, stride=frames + 1)
                held[place, :] = sums[:, (frame - start) * LANES : (frame - start + 1) * LANES]

    table_copy(1).wait()
    for k in range(2):
        at = turns + 2 * HALF + k * 4 * LANES
        both = jnp.concatenate([table[at : at + 2 * LANES], table[at + 2 * LANES : at + 4 * LANES]], axis=1)
        high, low = halves(both)
        stack[k] = jnp.concatenate([high, low, high], axis=0)

    def turned(row):
        at = row * 2 * (frames + 1)
        real = held[pl.ds(at, frames), :]
        imag = held[pl.ds(at + frames + 1, frames), :]
        cos, sin = table[pl.ds(turns + row, 1), :], table[pl.ds(turns + HALF + row, 1), :]
        high_r, low_r = halves(real * cos + imag * sin)
        high_i, low_i = halves(imag * cos - real * sin)
        return jnp.concatenate([high_r, high_i, high_r, high_i, low_r, low_i], axis=1)

    def magnitude(terms, k):
        bins = jnp.dot(terms, stack[k], preferred_element_type=jnp.float32)
        real, imag = bins[:, :LANES], bins[:, LANES:]
        square = real * real + imag * imag
        found = (square * lax.rsqrt(jnp.maximum(square, LEAST))).astype(keep.dtype)
        peak[...] = jnp.maximum(peak[...], jnp.max(found.reshape(-1, 16, LANES), axis=0))
        return found

    peak[...] = jnp.zeros_like(peak)

    def rows_of(side, out):
        for group in range(HALF // 2 // GROUP):
            start = side * (HALF // 2) + group * GROUP
            found = magnitude(jnp.concatenate([turned(start + k) for k in range(GROUP)], axis=0), 0)
            for k in range(GROUP):
                out[group * GROUP + k] = found[k * frames : (k + 1) * frames]

    rows_of(1 - core[0], give)
    rows_of(core[0], keep)
    edge = magnitude(turned(0), 1)

    @pl.when(core[0] == 0)
    def _():
        keep[0] = edge

    @pl.when(core[0] != 0)
    def _():
        give[0] = edge


def spectrum(audio, core):
    frames = audio.shape[1] // FRAME
    table = jnp.asarray(tables())
    far = pl.BlockSpec(memory_space=pltpu.HBM)
    return pl.pallas_call(
        spectrum_kernel,
        out_shape=[jax.ShapeDtypeStruct((HALF // 2, frames, LANES), jnp.bfloat16)] * 2
        + [jax.ShapeDtypeStruct((16, LANES), jnp.bfloat16)],
        in_specs=[pl.BlockSpec(memory_space=pltpu.SMEM), far, far],
        out_specs=[pl.BlockSpec(memory_space=pltpu.VMEM)] * 3,
        scratch_shapes=[
            pltpu.VMEM((frames // CHUNK, 1, CHUNK * FRAME), jnp.bfloat16),
            pltpu.VMEM(table.shape, table.dtype),
            pltpu.VMEM((2, 6 * LANES, 2 * LANES), jnp.bfloat16),
            pltpu.VMEM((OUTER * (frames + 1), LANES), jnp.float32),
            pltpu.SemaphoreType.DMA((frames // CHUNK,)),
            pltpu.SemaphoreType.DMA((2,)),
        ],
        compiler_params=pltpu.CompilerParams(vmem_limit_bytes=105 * 2**19),
        cost_estimate=pl.CostEstimate(
            flops=6 * frames * FRAME * (OUTER + 2 * LANES), bytes_accessed=2**22, transcendentals=0
        ),
        name="spectrum",
    )(core, audio, table)


def update(state, numer, gram):
    return state * numer / jnp.dot(gram, state, precision=HIGHEST, preferred_element_type=jnp.float32)


def step_kernel(comps, grid, acts, parts, acts_out):
    rows, comp, lanes = comps.shape
    wide = jnp.concatenate([comps[r] for r in range(rows)], axis=1)
    tall = jnp.concatenate([grid[r] for r in range(rows)], axis=1)
    numer = lax.dot_general(wide.astype(jnp.bfloat16), tall, NT, preferred_element_type=jnp.float32)
    gram = lax.dot_general(wide, wide, NT, precision=HIGHEST, preferred_element_type=jnp.float32)
    acts_new = update(acts[...], numer, gram)
    acts_out[...] = acts_new
    gram = lax.dot_general(acts_new, acts_new, NT, precision=HIGHEST, preferred_element_type=jnp.float32)
    per = LANES // comp
    high = comp // per
    packed = jnp.concatenate([gram[j * high : (j + 1) * high] for j in range(per)], axis=1)
    sums = jnp.dot(acts_new.astype(jnp.bfloat16), tall, preferred_element_type=jnp.float32)
    for r in range(rows):
        parts[r, :comp, :] = sums[:, r * lanes : (r + 1) * lanes]
        parts[r, comp:, :] = packed


def advance(comps, grid, acts):
    rows, comp, lanes = comps.shape
    extra = comp * comp // LANES
    return pl.pallas_call(
        step_kernel,
        out_shape=(
            jax.ShapeDtypeStruct((rows, comp + extra, lanes), jnp.float32),
            jax.ShapeDtypeStruct(acts.shape, jnp.float32),
        ),
        compiler_params=pltpu.CompilerParams(vmem_limit_bytes=32 * 2**20),
        name="advance",
    )(comps, grid, acts)


def unpack(packed):
    high = packed.shape[0]
    comp = math.isqrt(packed.size)
    return packed.reshape(high, LANES // comp, comp).transpose(1, 0, 2).reshape(comp, comp)


def inner_order(natural):
    comp = natural.shape[0]
    cube = natural.reshape(comp, -1, OUTER).transpose(2, 0, 1)
    mirrored = jnp.concatenate([cube[HALF : HALF + 1], cube[: HALF : -1]], axis=0)
    return jnp.concatenate([cube[:HALF], mirrored], axis=2)


def natural_order(inner):
    comp, width = inner.shape[1], inner.shape[2] // 2
    low, mirrored = inner[:, :, :width], inner[:, :, width:]
    cube = jnp.concatenate([low, mirrored[:1], mirrored[:0:-1]], axis=0)
    return cube.transpose(1, 2, 0).reshape(comp, -1)


def gather_freq(block, n_freq, at):
    pieces = [block]
    for shift in range(1, n_freq):
        ring = [(i, (i + shift) % n_freq) for i in range(n_freq)]
        pieces.append(lax.ppermute(block, "freq", ring))
    placed = []
    for p in range(n_freq):
        value = pieces[0]
        for shift in range(1, n_freq):
            value = jnp.where((at - shift) % n_freq == p, pieces[shift], value)
        placed.append(value)
    return jnp.concatenate(placed, axis=1)


TOP = 13
SIDE = HALF // 2


def pack(gram):
    comp = gram.shape[0]
    per = LANES // comp
    high = comp // per
    return jnp.concatenate([gram[j * high : (j + 1) * high] for j in range(per)], axis=1)


def unpacked(packed):
    comp = math.isqrt(packed.size)
    return jnp.concatenate([packed[:, j * comp : (j + 1) * comp] for j in range(LANES // comp)], axis=0)


def exponent(value):
    peak = jnp.max(jnp.abs(value), axis=(0, 1), keepdims=True)
    return jnp.floor(jnp.log2(jnp.maximum(peak, 1e-30))) - TOP


def power(exps):
    count = jnp.abs(exps).astype(jnp.int32)
    value = jnp.ones_like(exps)
    for bit in range(7):
        step = jnp.where(exps < 0, 2.0 ** -(2**bit), 2.0 ** (2**bit))
        value = value * jnp.where((count >> bit) & 1 == 1, step, 1.0)
    return value


def places(shape):
    return [lax.broadcasted_iota(jnp.int32, shape, axis) for axis in range(2)]


def mirrored_at(r):
    return OUTER - r if r else HALF


def gram_of(value):
    rows = value.shape[0]
    both = jnp.concatenate(halves(value), axis=0)
    parts = lax.dot_general(both, both, NT, preferred_element_type=jnp.float32)
    cross = parts[:rows, rows:] + parts[rows:, :rows]
    return parts[:rows, :rows] + (cross + parts[rows:, rows:])


def start_kernel(at, own, other, keep, give, acts, acts_out, mine, held):
    comp = own.shape[0]
    row, side, first = at[0], at[1], at[2] == 0
    wide = jnp.concatenate(
        [jnp.where(first, own[...], other[...]), jnp.where(first, other[...], own[...])], axis=1
    )
    quads, eighth = LANES // comp, 8
    for q in range(eighth):
        columns = [wide[:, (c * eighth + q) * LANES : (c * eighth + q + 1) * LANES] for c in range(quads)]
        turned = jnp.concatenate(columns, axis=0).T
        for m in range(2):
            place = (2 * q + m) * (OUTER + 1)
            held[place : place + OUTER, :] = turned[m * OUTER : (m + 1) * OUTER]
    gram = gram_of(wide)
    span = OUTER // quads
    block = places((span, LANES))[1] // comp

    def pair(r):
        mirror = jnp.where(r == 0, HALF, OUTER - r)
        return [held[pl.ds(j, span, stride=OUTER + 1), :] for j in (r, mirror)]

    both = jnp.concatenate(pair(row), axis=0).T
    mine[...] = jnp.concatenate(
        [
            both[c * comp : (c + 1) * comp, h * span : (h + 1) * span]
            for h in range(2)
            for c in range(quads)
        ],
        axis=1,
    )
    total = jnp.zeros((acts.shape[1], LANES), jnp.float32)
    batch = SIDE
    for grid, start in ((keep, side * SIDE), (give, (1 - side) * SIDE)):
        for base in range(0, SIDE, batch):
            pieces = []
            for u in range(base, base + batch):
                for value in pair(start + u):
                    pieces += [jnp.where(block == c, value, 0.0).astype(jnp.bfloat16) for c in range(quads)]
            left = jnp.concatenate([grid[u] for u in range(base, base + batch)], axis=1)
            total += jnp.dot(left, jnp.concatenate(pieces, axis=0), preferred_element_type=jnp.float32)
    total = total.T
    numer = sum(total[c * comp : (c + 1) * comp] for c in range(quads))
    acts_out[...] = update(acts[...], numer, gram)


def sealed(sums, gram, squares, bound=None):
    comp = gram.shape[0]
    sums_exp, gram_exp = exponent(sums if bound is None else bound), exponent(squares)
    packed = pack(gram) * power(-gram_exp)
    rows, lanes = places(packed.shape)
    last, end = packed.shape[0] - 1, LANES - comp
    packed = jnp.where((rows == last) & (lanes == end), sums_exp, packed)
    packed = jnp.where((rows == last) & (lanes == end + 1), gram_exp, packed)
    return sums * power(-sums_exp), packed


def opened(got, comp):
    end = LANES - comp
    scales = power(got[:, got.shape[1] - 1, :])
    sources = range(got.shape[0])
    gram = sum(got[s, comp:, :] * scales[s : s + 1, end + 1 : end + 2] for s in sources)
    gram = unpacked(gram)
    at = places(gram.shape)
    for column in range(2):
        mirrored = gram[column : column + 1, comp - 1 : comp]
        gram = jnp.where((at[0] == comp - 1) & (at[1] == column), mirrored, gram)
    return [scales[s : s + 1, end : end + 1] for s in sources], gram


def tall(grid):
    return jnp.concatenate([grid[u] for u in range(SIDE)], axis=1)


def finish(acts, grids, parts, peak=None):
    comp = acts[0].shape[0]
    left = [value.astype(jnp.bfloat16) for value in acts]
    both = jnp.concatenate([tall(grid) for grid in grids], axis=0)
    sums = jnp.dot(jnp.concatenate(left, axis=1), both, preferred_element_type=jnp.float32)
    gram, weight, squares = 0.0, 0.0, 0.0
    for value, short in zip(acts, left):
        weight += jnp.sum(short.astype(jnp.float32), axis=1, keepdims=True)
        squares += jnp.sum(value * value, axis=1, keepdims=True)
        gram += lax.dot_general(value, value, NT, precision=HIGHEST, preferred_element_type=jnp.float32)
    sums, packed = sealed(sums, gram, squares, None if peak is None else weight * (1.01 * peak))
    for u in range(SIDE):
        parts[u, :comp, :] = sums[:, u * LANES : (u + 1) * LANES]
        parts[u, comp:, :] = packed


def sums_kernel(acts, sibling, keep, taken, parts):
    finish((acts[...], sibling[...]), (keep, taken), parts)


def partial_kernel(got, exps, keep, taken, peak, out):
    comp = got.shape[1]
    wide = jnp.concatenate([got[u] for u in range(SIDE)], axis=1) * power(exps[:, :1])
    left = wide.astype(jnp.bfloat16)
    both = jnp.concatenate([tall(keep), tall(taken)], axis=0)
    numer = lax.dot_general(left, both, NT, preferred_element_type=jnp.float32)
    for k in range(2):
        out[k * comp : (k + 1) * comp, :] = numer[:, k * LANES : (k + 1) * LANES]
    packed = pack(gram_of(wide))
    rows, lanes = places(packed.shape)
    highest = jnp.max(peak[...].astype(jnp.float32), axis=(0, 1), keepdims=True)
    place = (rows == packed.shape[0] - 1) & (lanes == LANES - comp)
    out[2 * comp :, :] = jnp.where(place, highest, packed)


def again_kernel(half, other_half, acts, sibling, keep, taken, parts, acts_out):
    comp = acts.shape[0]
    mine, theirs = half[2 * comp :, :], other_half[2 * comp :, :]
    last, end = mine.shape[0] - 1, LANES - comp
    peak = jnp.maximum(mine, theirs)[last : last + 1, end : end + 1]
    gram = unpacked(mine + theirs)
    at = places(gram.shape)
    gram = jnp.where((at[0] == comp - 1) & (at[1] == 0), gram[:1, comp - 1 : comp], gram)
    new = update(acts[...], half[:comp, :] + other_half[comp : 2 * comp, :], gram)
    sibling_new = update(sibling[...], half[comp : 2 * comp, :] + other_half[:comp, :], gram)
    acts_out[...] = new
    finish((new, sibling_new), (keep, taken), parts, peak)


def eleven_bits(value):
    split = value * 8193.0
    return split - (split - value)


def rounded(value):
    def short(x):
        return x.astype(jnp.bfloat16).astype(jnp.float32)

    near = eleven_bits(value)
    step = jnp.abs(near) * 2.0**-10.6
    moved = eleven_bits(near + jnp.where(value > near, step, -step))
    return jnp.where(short(near) == short(value), near, moved)


def slice_of(got, mine):
    comp = mine.shape[0]
    scales, gram = opened(got, comp)
    sums = sum(got[s, :comp, :] * scales[s] for s in range(got.shape[0]))
    at = places(gram.shape)
    diagonal = jnp.sum(jnp.where(at[0] == at[1], gram, 0.0), axis=1, keepdims=True)
    bound = sum(scales) * 2.0 ** (TOP + 1) / jnp.maximum(diagonal, 1e-30)
    exps = jnp.clip(jnp.floor(jnp.log2(jnp.maximum(bound, 1e-30))), -100, 100) - TOP
    return update(mine[...], sums, gram), exps


def slice_kernel(got, mine, out, payload, exps_out):
    new, exps = slice_of(got, mine)
    out[...] = new
    payload[...] = rounded(new * power(-exps))
    exps_out[...] = jnp.broadcast_to(exps, exps_out.shape)


def last_kernel(got, mine, out, exps_out):
    new, exps = slice_of(got, mine)
    exps_out[...] = jnp.broadcast_to(exps, exps_out.shape)
    turned = (new * power(-exps)).T
    span = OUTER // 4
    for freq in range(2):
        starts = [h * OUTER + freq * 2 * span + half * span for h in range(2) for half in range(2)]
        out[freq] = jnp.concatenate([turned[a : a + span] for a in starts], axis=1)


def natural_kernel(at, got, exps, acts, partner, out, acts_out, low, high):
    comp = out.shape[0]
    span = OUTER // 4
    for r in range(HALF):
        value = got[r % SIDE * 2 + r // SIDE]
        low[pl.ds(r, span, stride=HALF + 1), :] = value
        high[pl.ds(mirrored_at(r) % HALF, span, stride=HALF + 1), :] = pltpu.roll(value, LANES // 2, 1)
    factor = power(exps[...])
    for pair in range(span // 2):
        rows = []
        for place in (2 * pair, 2 * pair + 1):
            begin = place * (HALF + 1)
            rows += [ref[begin : begin + HALF, :] for ref in (low, high)]
        turned = jnp.concatenate(rows, axis=0).T
        for half in range(2):
            begin = (half * (span // 2) + pair) * LANES
            out[:, begin : begin + LANES] = turned[half * comp : (half + 1) * comp] * factor
    first, own, other = at[2] == 0, acts[...], partner[...]
    acts_out[...] = jnp.concatenate([jnp.where(first, own, other), jnp.where(first, other, own)], axis=1)


def local(kernel, outs, name, *arrays, scratch=(), cost=None):
    vmem = pl.BlockSpec(memory_space=pltpu.VMEM)
    smem = pl.BlockSpec(memory_space=pltpu.SMEM)
    many = isinstance(outs, list)
    shapes = [jax.ShapeDtypeStruct(shape, dtype) for shape, dtype in (outs if many else [outs])]
    return pl.pallas_call(
        kernel,
        out_shape=shapes if many else shapes[0],
        in_specs=[smem if a.dtype == jnp.int32 else vmem for a in arrays],
        out_specs=[vmem] * len(outs) if many else vmem,
        scratch_shapes=list(scratch),
        compiler_params=pltpu.CompilerParams(vmem_limit_bytes=32 * 2**20),
        cost_estimate=cost,
        name=name,
    )(*arrays)


def row_shards(audio, w_start, h_start):
    f16, f32 = jnp.float16, jnp.float32
    comp = w_start.shape[0]
    swap = [(0, 1), (1, 0)]
    freq_at, core_at = lax.axis_index("freq"), lax.axis_index("core")
    q = freq_at * lax.axis_size("chips") + lax.axis_index("chips")
    at = jnp.stack([core_at * SIDE + q, core_at, freq_at]).astype(jnp.int32)
    other = lax.ppermute(w_start, "freq", swap)
    keep, give, peak = spectrum(audio, at[1:2])
    frames = keep.shape[1]
    extra = comp * comp // LANES
    taken = lax.ppermute(give, "core", swap)
    acts = lax.dynamic_slice_in_dim(h_start, freq_at * frames, frames, 1)
    message = ((SIDE, comp + extra, LANES), f32)
    lane_rows = ((comp, LANES), f32)

    def exchange(value, axes=("freq", "chips")):
        value = lax.all_to_all(value.astype(f16), axes, split_axis=0, concat_axis=0, tiled=True)
        return value.astype(f32)

    acts, mine = local(
        start_kernel,
        [(acts.shape, f32), lane_rows],
        "start",
        at,
        w_start,
        other,
        keep,
        give,
        acts,
        scratch=[pltpu.VMEM((LANES // 8 * (OUTER + 1), LANES), f32)],
        cost=pl.CostEstimate(flops=2**34, bytes_accessed=2**25, transcendentals=0),
    )
    sibling = lax.ppermute(acts, "core", swap)
    parts = local(sums_kernel, message, "sums", acts, sibling, keep, taken)
    for step in range(ITERS - 1):
        got = exchange(parts)
        mine, payload, exps = local(slice_kernel, [lane_rows] * 3, "slice", got, mine)
        got = exchange(jnp.broadcast_to(payload, (SIDE,) + payload.shape))
        half = local(partial_kernel, ((2 * comp + extra, LANES), f32), "partial", got, exps, keep, taken, peak)
        other_half = lax.ppermute(half, "core", swap)
        outs = [message, (acts.shape, f32)]
        parts, acts = local(
            again_kernel, outs, "again", half, other_half, acts, sibling, keep, taken
        )
    partner = lax.ppermute(acts, "freq", swap)
    got = exchange(parts)
    final, exps = local(last_kernel, [((2, OUTER // 4, LANES), f32), lane_rows], "last", got, mine)
    final = jnp.broadcast_to(final[:, None], (2, HALF // 2) + final.shape[1:])
    got = exchange(final.reshape((HALF,) + final.shape[2:]), ("freq", "chips", "core"))
    return local(
        natural_kernel,
        [(w_start.shape, f32), (h_start.shape, f32)],
        "natural",
        at,
        got,
        exps,
        acts,
        partner,
        scratch=[pltpu.VMEM((OUTER // 4 * (HALF + 1), LANES), f32)] * 2,
    )


def shards(n_freq, n_tm, audio, w_start, h_start):
    n_dev = n_freq * n_tm
    comp, w_cols = w_start.shape
    bins = w_cols * n_freq
    own = bins // n_dev
    width = OUTER // n_freq
    freq_at = lax.axis_index("freq")
    me = freq_at * n_tm + lax.axis_index("tm")
    grid = jnp.concatenate(spectrum(audio, jnp.zeros((1,), jnp.int32))[:2], axis=0)
    frames = grid.shape[1]
    comps = inner_order(gather_freq(w_start, n_freq, freq_at))
    acts = lax.dynamic_slice_in_dim(h_start, freq_at * frames, frames, 1)
    per_row = LANES // own
    mine = lax.dynamic_slice(
        comps, (me // per_row, 0, me % per_row * own), (1, comp, own)
    ).reshape(comp, own)
    for step in range(ITERS):
        parts, acts = advance(comps, grid, acts)
        sums = parts[:, :comp].reshape(HALF, comp, per_row, own).transpose(0, 2, 1, 3)
        gram = jnp.broadcast_to(parts[0, comp:].reshape(1, -1), (n_dev, comp * comp))
        parts = jnp.concatenate([sums.reshape(n_dev, -1), gram], axis=1).reshape(n_dev, -1, LANES)
        got = lax.all_to_all(parts, ALL, split_axis=0, concat_axis=0, tiled=True)
        value = jnp.sum(got, axis=0)
        rows = comp * own // LANES
        mine = update(mine, value[:rows].reshape(comp, own), unpack(value[rows:]))
        every = jnp.broadcast_to(mine.reshape(1, -1, LANES), (n_dev, rows, LANES))
        comps = lax.all_to_all(every, ALL, split_axis=0, concat_axis=0, tiled=True)
        comps = comps.reshape(HALF, per_row, comp, own).transpose(0, 2, 1, 3)
        comps = comps.reshape(HALF, comp, LANES)
    cut = lax.dynamic_slice_in_dim(comps.reshape(HALF, comp, 2, OUTER), freq_at * width, width, 3)
    components = natural_order(cut.reshape(HALF, comp, 2 * width))
    activations = gather_freq(acts, n_freq, freq_at)
    return (components, activations)


def solution(mesh):
    sizes = (mesh.shape["freq"], mesh.shape["tm"])
    if sizes == (2, SIDE):
        devices = mesh.devices.reshape(2, SIDE // 2, 2)
        mesh = jax.sharding.Mesh(devices, ("freq", "chips", "core"))
        body, tm = row_shards, ("chips", "core")
    else:
        body, tm = functools.partial(shards, *sizes), "tm"
    return jax.shard_map(
        body,
        mesh=mesh,
        in_specs=(P(tm, "freq"), P(None, "freq"), P(None, tm)),
        out_specs=(P(None, "freq"), P(None, tm)),
        check_vma=False,
    )
```

```python
import functools
import math

import jax
import jax.numpy as jnp
import numpy as np
from jax import lax
from jax.experimental import pallas as pl
from jax.experimental.pallas import tpu as pltpu
from jax.sharding import PartitionSpec as P

ITERS = 2
HIGHEST = lax.Precision.HIGHEST
ALL = ("freq", "tm")
LANES = 128
OUTER = 64
HALF = OUTER // 2
FRAME = OUTER * LANES
CHUNK = 16
PAIR = 2
GROUP = 4
NT = (((1,), (1,)), ((), ()))
LEAST = 2.0**-126


def tables():
    a = np.arange(OUTER)
    i = np.arange(LANES)
    r = np.arange(HALF)
    position = a[:, None] * LANES + i[None, :]
    window = 0.5 - 0.5 * np.cos(2 * np.pi * position / FRAME)
    window = window / math.sqrt(0.375 * FRAME)
    angle = 2 * np.pi * (r[:, None] * a[None, :] % OUTER) / OUTER
    first = np.stack([np.cos(angle), -np.sin(angle)], axis=1).reshape(2 * HALF, OUTER)
    first[1] = np.cos(np.pi * a)
    turn = 2 * np.pi * r[:, None] * i[None, :] / FRAME
    turn_cos = np.cos(turn)
    turn_sin = np.sin(turn)
    m = np.arange(OUTER)
    column = np.concatenate([m, LANES - 1 - m])
    angle = 2 * np.pi * (i[:, None] * column[None, :] % LANES) / LANES
    top = np.concatenate([np.cos(angle), -np.sin(angle)], axis=1)
    bottom = np.concatenate([np.sin(angle), np.cos(angle)], axis=1)
    second = np.concatenate([top, bottom], axis=0)
    zero = np.zeros((LANES, OUTER))
    angle_a = 2 * np.pi * i[:, None] * (m * OUTER)[None, :] / FRAME
    angle_b = 2 * np.pi * i[:, None] * (m * OUTER + HALF)[None, :] / FRAME
    top = np.concatenate([np.cos(angle_a), zero, -np.sin(angle_a), zero], axis=1)
    bottom = np.concatenate([zero, np.cos(angle_b), zero, -np.sin(angle_b)], axis=1)
    edge = np.concatenate([top, bottom], axis=0)

    first = np.concatenate([first, np.zeros((OUTER, LANES - OUTER))], axis=1)
    second, edge = (np.concatenate([t[:, :LANES], t[:, LANES:]], axis=0) for t in (second, edge))
    parts = [window, first, turn_cos, turn_sin, second, edge]
    return np.concatenate(parts, axis=0).astype(np.float32)


def halves(value):
    high = value.astype(jnp.bfloat16)
    return high, (value - high.astype(jnp.float32)).astype(jnp.bfloat16)


def spectrum_kernel(core, audio, source, keep, give, peak, heard, table, stack, held, audio_sems, table_sems):
    frames = keep.shape[1]
    chunks = frames // CHUNK
    turns = 2 * OUTER

    def audio_copy(chunk):
        span = pl.ds(pl.multiple_of(chunk * CHUNK * FRAME, CHUNK * FRAME), CHUNK * FRAME)
        return pltpu.make_async_copy(audio.at[:, span], heard.at[chunk], audio_sems.at[chunk])

    def table_copy(k):
        span = pl.ds(0, turns) if k == 0 else pl.ds(turns, table.shape[0] - turns)
        return pltpu.make_async_copy(source.at[span], table.at[span], table_sems.at[k])

    table_copy(0).start()
    for chunk in range(chunks):
        audio_copy(chunk).start()
    table_copy(1).start()
    table_copy(0).wait()
    high, low = halves(table[OUTER:turns, :OUTER])
    first_terms = jnp.concatenate([high, low, high], axis=1)

    @pl.loop(0, chunks)
    def _(chunk):
        audio_copy(chunk).wait()
        samples = heard[chunk].reshape(CHUNK * OUTER, LANES).astype(jnp.float32)
        shape = table[:OUTER]
        for start in range(0, CHUNK, PAIR):
            columns = []
            for frame in range(start, start + PAIR):
                high, low = halves(samples[frame * OUTER : (frame + 1) * OUTER] * shape)
                columns.append(jnp.concatenate([high, high, low], axis=0))
            sums = jnp.dot(
                first_terms, jnp.concatenate(columns, axis=1), preferred_element_type=jnp.float32
            )
            for frame in range(start, start + PAIR):
                place = pl.ds(chunk * CHUNK + frame, OUTER, stride=frames + 1)
                held[place, :] = sums[:, (frame - start) * LANES : (frame - start + 1) * LANES]

    table_copy(1).wait()
    for k in range(2):
        at = turns + 2 * HALF + k * 4 * LANES
        both = jnp.concatenate([table[at : at + 2 * LANES], table[at + 2 * LANES : at + 4 * LANES]], axis=1)
        high, low = halves(both)
        stack[k] = jnp.concatenate([high, low, high], axis=0)

    def turned(row):
        at = row * 2 * (frames + 1)
        real = held[pl.ds(at, frames), :]
        imag = held[pl.ds(at + frames + 1, frames), :]
        cos, sin = table[pl.ds(turns + row, 1), :], table[pl.ds(turns + HALF + row, 1), :]
        high_r, low_r = halves(real * cos + imag * sin)
        high_i, low_i = halves(imag * cos - real * sin)
        return jnp.concatenate([high_r, high_i, high_r, high_i, low_r, low_i], axis=1)

    def magnitude(terms, k):
        bins = jnp.dot(terms, stack[k], preferred_element_type=jnp.float32)
        real, imag = bins[:, :LANES], bins[:, LANES:]
        square = real * real + imag * imag
        found = (square * lax.rsqrt(jnp.maximum(square, LEAST))).astype(keep.dtype)
        peak[...] = jnp.maximum(peak[...], jnp.max(found.reshape(-1, 16, LANES), axis=0))
        return found

    peak[...] = jnp.zeros_like(peak)

    def rows_of(side, out):
        for group in range(HALF // 2 // GROUP):
            start = side * (HALF // 2) + group * GROUP
            found = magnitude(jnp.concatenate([turned(start + k) for k in range(GROUP)], axis=0), 0)
            for k in range(GROUP):
                out[group * GROUP + k] = found[k * frames : (k + 1) * frames]

    rows_of(1 - core[0], give)
    rows_of(core[0], keep)
    edge = magnitude(turned(0), 1)

    @pl.when(core[0] == 0)
    def _():
        keep[0] = edge

    @pl.when(core[0] != 0)
    def _():
        give[0] = edge


def spectrum(audio, core):
    frames = audio.shape[1] // FRAME
    table = jnp.asarray(tables())
    far = pl.BlockSpec(memory_space=pltpu.HBM)
    return pl.pallas_call(
        spectrum_kernel,
        out_shape=[jax.ShapeDtypeStruct((HALF // 2, frames, LANES), jnp.bfloat16)] * 2
        + [jax.ShapeDtypeStruct((16, LANES), jnp.bfloat16)],
        in_specs=[pl.BlockSpec(memory_space=pltpu.SMEM), far, far],
        out_specs=[pl.BlockSpec(memory_space=pltpu.VMEM)] * 3,
        scratch_shapes=[
            pltpu.VMEM((frames // CHUNK, 1, CHUNK * FRAME), jnp.bfloat16),
            pltpu.VMEM(table.shape, table.dtype),
            pltpu.VMEM((2, 6 * LANES, 2 * LANES), jnp.bfloat16),
            pltpu.VMEM((OUTER * (frames + 1), LANES), jnp.float32),
            pltpu.SemaphoreType.DMA((frames // CHUNK,)),
            pltpu.SemaphoreType.DMA((2,)),
        ],
        compiler_params=pltpu.CompilerParams(vmem_limit_bytes=105 * 2**19),
        cost_estimate=pl.CostEstimate(
            flops=6 * frames * FRAME * (OUTER + 2 * LANES), bytes_accessed=2**22, transcendentals=0
        ),
        name="spectrum",
    )(core, audio, table)


def update(state, numer, gram):
    return state * numer / jnp.dot(gram, state, precision=HIGHEST, preferred_element_type=jnp.float32)


def step_kernel(comps, grid, acts, parts, acts_out):
    rows, comp, lanes = comps.shape
    wide = jnp.concatenate([comps[r] for r in range(rows)], axis=1)
    tall = jnp.concatenate([grid[r] for r in range(rows)], axis=1)
    numer = lax.dot_general(wide.astype(jnp.bfloat16), tall, NT, preferred_element_type=jnp.float32)
    gram = lax.dot_general(wide, wide, NT, precision=HIGHEST, preferred_element_type=jnp.float32)
    acts_new = update(acts[...], numer, gram)
    acts_out[...] = acts_new
    gram = lax.dot_general(acts_new, acts_new, NT, precision=HIGHEST, preferred_element_type=jnp.float32)
    per = LANES // comp
    high = comp // per
    packed = jnp.concatenate([gram[j * high : (j + 1) * high] for j in range(per)], axis=1)
    sums = jnp.dot(acts_new.astype(jnp.bfloat16), tall, preferred_element_type=jnp.float32)
    for r in range(rows):
        parts[r, :comp, :] = sums[:, r * lanes : (r + 1) * lanes]
        parts[r, comp:, :] = packed


def advance(comps, grid, acts):
    rows, comp, lanes = comps.shape
    extra = comp * comp // LANES
    return pl.pallas_call(
        step_kernel,
        out_shape=(
            jax.ShapeDtypeStruct((rows, comp + extra, lanes), jnp.float32),
            jax.ShapeDtypeStruct(acts.shape, jnp.float32),
        ),
        compiler_params=pltpu.CompilerParams(vmem_limit_bytes=32 * 2**20),
        name="advance",
    )(comps, grid, acts)


def unpack(packed):
    high = packed.shape[0]
    comp = math.isqrt(packed.size)
    return packed.reshape(high, LANES // comp, comp).transpose(1, 0, 2).reshape(comp, comp)


def inner_order(natural):
    comp = natural.shape[0]
    cube = natural.reshape(comp, -1, OUTER).transpose(2, 0, 1)
    mirrored = jnp.concatenate([cube[HALF : HALF + 1], cube[: HALF : -1]], axis=0)
    return jnp.concatenate([cube[:HALF], mirrored], axis=2)


def natural_order(inner):
    comp, width = inner.shape[1], inner.shape[2] // 2
    low, mirrored = inner[:, :, :width], inner[:, :, width:]
    cube = jnp.concatenate([low, mirrored[:1], mirrored[:0:-1]], axis=0)
    return cube.transpose(1, 2, 0).reshape(comp, -1)


def gather_freq(block, n_freq, at):
    pieces = [block]
    for shift in range(1, n_freq):
        ring = [(i, (i + shift) % n_freq) for i in range(n_freq)]
        pieces.append(lax.ppermute(block, "freq", ring))
    placed = []
    for p in range(n_freq):
        value = pieces[0]
        for shift in range(1, n_freq):
            value = jnp.where((at - shift) % n_freq == p, pieces[shift], value)
        placed.append(value)
    return jnp.concatenate(placed, axis=1)


TOP = 13
SIDE = HALF // 2


def pack(gram):
    comp = gram.shape[0]
    per = LANES // comp
    high = comp // per
    return jnp.concatenate([gram[j * high : (j + 1) * high] for j in range(per)], axis=1)


def unpacked(packed):
    comp = math.isqrt(packed.size)
    return jnp.concatenate([packed[:, j * comp : (j + 1) * comp] for j in range(LANES // comp)], axis=0)


def exponent(value):
    peak = jnp.max(jnp.abs(value), axis=(0, 1), keepdims=True)
    return jnp.floor(jnp.log2(jnp.maximum(peak, 1e-30))) - TOP


def power(exps):
    count = jnp.abs(exps).astype(jnp.int32)
    value = jnp.ones_like(exps)
    for bit in range(7):
        step = jnp.where(exps < 0, 2.0 ** -(2**bit), 2.0 ** (2**bit))
        value = value * jnp.where((count >> bit) & 1 == 1, step, 1.0)
    return value


def places(shape):
    return [lax.broadcasted_iota(jnp.int32, shape, axis) for axis in range(2)]


def mirrored_at(r):
    return OUTER - r if r else HALF


def gram_of(value):
    rows = value.shape[0]
    both = jnp.concatenate(halves(value), axis=0)
    parts = lax.dot_general(both, both, NT, preferred_element_type=jnp.float32)
    cross = parts[:rows, rows:] + parts[rows:, :rows]
    return parts[:rows, :rows] + (cross + parts[rows:, rows:])


def start_kernel(at, own, other, keep, give, acts, acts_out, mine, held):
    comp = own.shape[0]
    row, side, first = at[0], at[1], at[2] == 0
    wide = jnp.concatenate(
        [jnp.where(first, own[...], other[...]), jnp.where(first, other[...], own[...])], axis=1
    )
    quads, eighth = LANES // comp, 8
    for q in range(eighth):
        columns = [wide[:, (c * eighth + q) * LANES : (c * eighth + q + 1) * LANES] for c in range(quads)]
        turned = jnp.concatenate(columns, axis=0).T
        for m in range(2):
            place = (2 * q + m) * (OUTER + 1)
            held[place : place + OUTER, :] = turned[m * OUTER : (m + 1) * OUTER]
    gram = gram_of(wide)
    span = OUTER // quads
    block = places((span, LANES))[1] // comp
    masks = [jnp.where(block == c, 1.0, 0.0).astype(jnp.bfloat16) for c in range(quads)]

    def pair(r):
        mirror = jnp.where(r == 0, HALF, OUTER - r)
        return [held[pl.ds(j, span, stride=OUTER + 1), :] for j in (r, mirror)]

    both = jnp.concatenate(pair(row), axis=0).T
    mine[...] = jnp.concatenate(
        [
            both[c * comp : (c + 1) * comp, h * span : (h + 1) * span]
            for h in range(2)
            for c in range(quads)
        ],
        axis=1,
    )
    total = jnp.zeros((acts.shape[1], LANES), jnp.float32)
    batch = SIDE
    for grid, start in ((keep, side * SIDE), (give, (1 - side) * SIDE)):
        for base in range(0, SIDE, batch):
            pieces = []
            for u in range(base, base + batch):
                for value in pair(start + u):
                    short = value.astype(jnp.bfloat16)
                    pieces += [short * mask for mask in masks]
            left = jnp.concatenate([grid[u] for u in range(base, base + batch)], axis=1)
            total += jnp.dot(left, jnp.concatenate(pieces, axis=0), preferred_element_type=jnp.float32)
    total = total.T
    numer = sum(total[c * comp : (c + 1) * comp] for c in range(quads))
    acts_out[...] = update(acts[...], numer, gram)


def sealed(sums, gram, squares, bound=None):
    comp = gram.shape[0]
    sums_exp, gram_exp = exponent(sums if bound is None else bound), exponent(squares)
    packed = pack(gram) * power(-gram_exp)
    rows, lanes = places(packed.shape)
    last, end = packed.shape[0] - 1, LANES - comp
    packed = jnp.where((rows == last) & (lanes == end), sums_exp, packed)
    packed = jnp.where((rows == last) & (lanes == end + 1), gram_exp, packed)
    return sums * power(-sums_exp), packed


def opened(got, comp):
    end = LANES - comp
    scales = power(got[:, got.shape[1] - 1, :])
    sources = range(got.shape[0])
    gram = sum(got[s, comp:, :] * scales[s : s + 1, end + 1 : end + 2] for s in sources)
    gram = unpacked(gram)
    at = places(gram.shape)
    for column in range(2):
        mirrored = gram[column : column + 1, comp - 1 : comp]
        gram = jnp.where((at[0] == comp - 1) & (at[1] == column), mirrored, gram)
    return [scales[s : s + 1, end : end + 1] for s in sources], gram


def tall(grid):
    return jnp.concatenate([grid[u] for u in range(SIDE)], axis=1)


def finish(acts, grids, parts, peak=None):
    comp = acts[0].shape[0]
    left = [value.astype(jnp.bfloat16) for value in acts]
    both = jnp.concatenate([tall(grid) for grid in grids], axis=0)
    sums = jnp.dot(jnp.concatenate(left, axis=1), both, preferred_element_type=jnp.float32)
    gram, weight, squares = 0.0, 0.0, 0.0
    for value, short in zip(acts, left):
        weight += jnp.sum(short.astype(jnp.float32), axis=1, keepdims=True)
        squares += jnp.sum(value * value, axis=1, keepdims=True)
        gram += lax.dot_general(value, value, NT, precision=HIGHEST, preferred_element_type=jnp.float32)
    sums, packed = sealed(sums, gram, squares, None if peak is None else weight * (1.01 * peak))
    for u in range(SIDE):
        parts[u, :comp, :] = sums[:, u * LANES : (u + 1) * LANES]
        parts[u, comp:, :] = packed


def sums_kernel(acts, sibling, keep, taken, parts):
    finish((acts[...], sibling[...]), (keep, taken), parts)


def partial_kernel(got, exps, keep, taken, peak, out):
    comp = got.shape[1]
    wide = jnp.concatenate([got[u] for u in range(SIDE)], axis=1) * power(exps[:, :1])
    left = wide.astype(jnp.bfloat16)
    both = jnp.concatenate([tall(keep), tall(taken)], axis=0)
    numer = lax.dot_general(left, both, NT, preferred_element_type=jnp.float32)
    for k in range(2):
        out[k * comp : (k + 1) * comp, :] = numer[:, k * LANES : (k + 1) * LANES]
    packed = pack(gram_of(wide))
    rows, lanes = places(packed.shape)
    highest = jnp.max(peak[...].astype(jnp.float32), axis=(0, 1), keepdims=True)
    place = (rows == packed.shape[0] - 1) & (lanes == LANES - comp)
    out[2 * comp :, :] = jnp.where(place, highest, packed)


def again_kernel(half, other_half, acts, sibling, keep, taken, parts, acts_out):
    comp = acts.shape[0]
    mine, theirs = half[2 * comp :, :], other_half[2 * comp :, :]
    last, end = mine.shape[0] - 1, LANES - comp
    peak = jnp.maximum(mine, theirs)[last : last + 1, end : end + 1]
    gram = unpacked(mine + theirs)
    at = places(gram.shape)
    gram = jnp.where((at[0] == comp - 1) & (at[1] == 0), gram[:1, comp - 1 : comp], gram)
    new = update(acts[...], half[:comp, :] + other_half[comp : 2 * comp, :], gram)
    sibling_new = update(sibling[...], half[comp : 2 * comp, :] + other_half[:comp, :], gram)
    acts_out[...] = new
    finish((new, sibling_new), (keep, taken), parts, peak)


def eleven_bits(value):
    split = value * 8193.0
    return split - (split - value)


def rounded(value):
    def short(x):
        return x.astype(jnp.bfloat16).astype(jnp.float32)

    near = eleven_bits(value)
    step = jnp.abs(near) * 2.0**-10.6
    moved = eleven_bits(near + jnp.where(value > near, step, -step))
    return jnp.where(short(near) == short(value), near, moved)


def slice_of(got, mine):
    comp = mine.shape[0]
    scales, gram = opened(got, comp)
    sums = sum(got[s, :comp, :] * scales[s] for s in range(got.shape[0]))
    at = places(gram.shape)
    diagonal = jnp.sum(jnp.where(at[0] == at[1], gram, 0.0), axis=1, keepdims=True)
    bound = sum(scales) * 2.0 ** (TOP + 1) / jnp.maximum(diagonal, 1e-30)
    exps = jnp.clip(jnp.floor(jnp.log2(jnp.maximum(bound, 1e-30))), -100, 100) - TOP
    return update(mine[...], sums, gram), exps


def slice_kernel(got, mine, out, payload, exps_out):
    new, exps = slice_of(got, mine)
    out[...] = new
    payload[...] = rounded(new * power(-exps))
    exps_out[...] = jnp.broadcast_to(exps, exps_out.shape)


def last_kernel(got, mine, out, exps_out):
    new, exps = slice_of(got, mine)
    exps_out[...] = jnp.broadcast_to(exps, exps_out.shape)
    turned = (new * power(-exps)).T
    span = OUTER // 4
    for freq in range(2):
        starts = [h * OUTER + freq * 2 * span + half * span for h in range(2) for half in range(2)]
        out[freq] = jnp.concatenate([turned[a : a + span] for a in starts], axis=1)


def natural_kernel(at, got, exps, acts, partner, out, acts_out, low, high):
    comp = out.shape[0]
    span = OUTER // 4
    for r in range(HALF):
        value = got[r % SIDE * 2 + r // SIDE]
        low[pl.ds(r, span, stride=HALF + 1), :] = value
        high[pl.ds(mirrored_at(r) % HALF, span, stride=HALF + 1), :] = pltpu.roll(value, LANES // 2, 1)
    factor = power(exps[...])
    for pair in range(span // 2):
        rows = []
        for place in (2 * pair, 2 * pair + 1):
            begin = place * (HALF + 1)
            rows += [ref[begin : begin + HALF, :] for ref in (low, high)]
        turned = jnp.concatenate(rows, axis=0).T
        for half in range(2):
            begin = (half * (span // 2) + pair) * LANES
            out[:, begin : begin + LANES] = turned[half * comp : (half + 1) * comp] * factor
    first, own, other = at[2] == 0, acts[...], partner[...]
    acts_out[...] = jnp.concatenate([jnp.where(first, own, other), jnp.where(first, other, own)], axis=1)


def local(kernel, outs, name, *arrays, scratch=(), cost=None):
    vmem = pl.BlockSpec(memory_space=pltpu.VMEM)
    smem = pl.BlockSpec(memory_space=pltpu.SMEM)
    many = isinstance(outs, list)
    shapes = [jax.ShapeDtypeStruct(shape, dtype) for shape, dtype in (outs if many else [outs])]
    return pl.pallas_call(
        kernel,
        out_shape=shapes if many else shapes[0],
        in_specs=[smem if a.dtype == jnp.int32 else vmem for a in arrays],
        out_specs=[vmem] * len(outs) if many else vmem,
        scratch_shapes=list(scratch),
        compiler_params=pltpu.CompilerParams(vmem_limit_bytes=32 * 2**20),
        cost_estimate=cost,
        name=name,
    )(*arrays)


def row_shards(audio, w_start, h_start):
    f16, f32 = jnp.float16, jnp.float32
    comp = w_start.shape[0]
    swap = [(0, 1), (1, 0)]
    freq_at, core_at = lax.axis_index("freq"), lax.axis_index("core")
    q = freq_at * lax.axis_size("chips") + lax.axis_index("chips")
    at = jnp.stack([core_at * SIDE + q, core_at, freq_at]).astype(jnp.int32)
    other = lax.ppermute(w_start, "freq", swap)
    keep, give, peak = spectrum(audio, at[1:2])
    frames = keep.shape[1]
    extra = comp * comp // LANES
    taken = lax.ppermute(give, "core", swap)
    acts = lax.dynamic_slice_in_dim(h_start, freq_at * frames, frames, 1)
    message = ((SIDE, comp + extra, LANES), f32)
    lane_rows = ((comp, LANES), f32)

    def exchange(value, axes=("freq", "chips")):
        value = lax.all_to_all(value.astype(f16), axes, split_axis=0, concat_axis=0, tiled=True)
        return value.astype(f32)

    acts, mine = local(
        start_kernel,
        [(acts.shape, f32), lane_rows],
        "start",
        at,
        w_start,
        other,
        keep,
        give,
        acts,
        scratch=[pltpu.VMEM((LANES // 8 * (OUTER + 1), LANES), f32)],
        cost=pl.CostEstimate(flops=2**34, bytes_accessed=2**25, transcendentals=0),
    )
    sibling = lax.ppermute(acts, "core", swap)
    parts = local(sums_kernel, message, "sums", acts, sibling, keep, taken)
    for step in range(ITERS - 1):
        got = exchange(parts)
        mine, payload, exps = local(slice_kernel, [lane_rows] * 3, "slice", got, mine)
        got = exchange(jnp.broadcast_to(payload, (SIDE,) + payload.shape))
        half = local(partial_kernel, ((2 * comp + extra, LANES), f32), "partial", got, exps, keep, taken, peak)
        other_half = lax.ppermute(half, "core", swap)
        outs = [message, (acts.shape, f32)]
        parts, acts = local(
            again_kernel, outs, "again", half, other_half, acts, sibling, keep, taken
        )
    got = exchange(parts)
    acts, got = lax.optimization_barrier((acts, got))
    partner = lax.ppermute(acts, "freq", swap)
    final, exps = local(last_kernel, [((2, OUTER // 4, LANES), f32), lane_rows], "last", got, mine)
    final = jnp.broadcast_to(final[:, None], (2, HALF // 2) + final.shape[1:])
    got = exchange(final.reshape((HALF,) + final.shape[2:]), ("freq", "chips", "core"))
    return local(
        natural_kernel,
        [(w_start.shape, f32), (h_start.shape, f32)],
        "natural",
        at,
        got,
        exps,
        acts,
        partner,
        scratch=[pltpu.VMEM((OUTER // 4 * (HALF + 1), LANES), f32)] * 2,
    )


def shards(n_freq, n_tm, audio, w_start, h_start):
    n_dev = n_freq * n_tm
    comp, w_cols = w_start.shape
    bins = w_cols * n_freq
    own = bins // n_dev
    width = OUTER // n_freq
    freq_at = lax.axis_index("freq")
    me = freq_at * n_tm + lax.axis_index("tm")
    grid = jnp.concatenate(spectrum(audio, jnp.zeros((1,), jnp.int32))[:2], axis=0)
    frames = grid.shape[1]
    comps = inner_order(gather_freq(w_start, n_freq, freq_at))
    acts = lax.dynamic_slice_in_dim(h_start, freq_at * frames, frames, 1)
    per_row = LANES // own
    mine = lax.dynamic_slice(
        comps, (me // per_row, 0, me % per_row * own), (1, comp, own)
    ).reshape(comp, own)
    for step in range(ITERS):
        parts, acts = advance(comps, grid, acts)
        sums = parts[:, :comp].reshape(HALF, comp, per_row, own).transpose(0, 2, 1, 3)
        gram = jnp.broadcast_to(parts[0, comp:].reshape(1, -1), (n_dev, comp * comp))
        parts = jnp.concatenate([sums.reshape(n_dev, -1), gram], axis=1).reshape(n_dev, -1, LANES)
        got = lax.all_to_all(parts, ALL, split_axis=0, concat_axis=0, tiled=True)
        value = jnp.sum(got, axis=0)
        rows = comp * own // LANES
        mine = update(mine, value[:rows].reshape(comp, own), unpack(value[rows:]))
        every = jnp.broadcast_to(mine.reshape(1, -1, LANES), (n_dev, rows, LANES))
        comps = lax.all_to_all(every, ALL, split_axis=0, concat_axis=0, tiled=True)
        comps = comps.reshape(HALF, per_row, comp, own).transpose(0, 2, 1, 3)
        comps = comps.reshape(HALF, comp, LANES)
    cut = lax.dynamic_slice_in_dim(comps.reshape(HALF, comp, 2, OUTER), freq_at * width, width, 3)
    components = natural_order(cut.reshape(HALF, comp, 2 * width))
    activations = gather_freq(acts, n_freq, freq_at)
    return (components, activations)


def solution(mesh):
    sizes = (mesh.shape["freq"], mesh.shape["tm"])
    if sizes == (2, SIDE):
        devices = mesh.devices.reshape(2, SIDE // 2, 2)
        mesh = jax.sharding.Mesh(devices, ("freq", "chips", "core"))
        body, tm = row_shards, ("chips", "core")
    else:
        body, tm = functools.partial(shards, *sizes), "tm"
    return jax.shard_map(
        body,
        mesh=mesh,
        in_specs=(P(tm, "freq"), P(None, "freq"), P(None, tm)),
        out_specs=(P(None, "freq"), P(None, tm)),
        check_vma=False,
    )
```
